32 devices in a mesh: dp: 4 (over x, core), tensor: 8 (over z, y).
Axes of the slice: x: 2, y: 2, z: 4, core: 2. Of those that a mesh axis runs over, the one named last changes fastest.
Arguments:
- tokens: bfloat16 [16384, 1024], P(('dp', 'tensor')), may hold values from -6 to 6
- lengths: int32 [8], P('dp'), may hold values from 1 to 2048, as said below
- ln1_gain: float32 [1024], replicated, may hold values from 0.5 to 1.5
- ln1_bias: float32 [1024], replicated, may hold values from -3 to 3
- w_query: bfloat16 [1024, 1024], P(None, 'tensor'), may hold values from -0.1875 to 0.1875
- w_key: bfloat16 [1024, 1024], P(None, 'tensor'), may hold values from -0.1875 to 0.1875
- w_value: bfloat16 [1024, 1024], P(None, 'tensor'), may hold values from -0.1875 to 0.1875
- w_out: bfloat16 [1024, 1024], P('tensor'), may hold values from -1.5 to 1.5
- ln2_gain: float32 [1024], replicated, may hold values from 0.5 to 1.5
- ln2_bias: float32 [1024], replicated, may hold values from -3 to 3
- w_gate: bfloat16 [1024, 4096], P(None, 'tensor'), may hold values from -0.1875 to 0.1875
- w_up: bfloat16 [1024, 4096], P(None, 'tensor'), may hold values from -0.1875 to 0.1875
- w_down: bfloat16 [4096, 1024], P('tensor'), may hold values from -0.09375 to 0.09375
- cotangent: bfloat16 [16384, 1024], P(('dp', 'tensor')), may hold values from -6 to 6
Outputs:
- output: bfloat16 [16384, 1024], P(('dp', 'tensor'))
- grad_tokens: bfloat16 [16384, 1024], P(('dp', 'tensor'))
- grad_ln1_gain: float32 [1024], replicated
- grad_ln1_bias: float32 [1024], replicated
- grad_w_query: float32 [1024, 1024], P(None, 'tensor')
- grad_w_key: float32 [1024, 1024], P(None, 'tensor')
- grad_w_value: float32 [1024, 1024], P(None, 'tensor')
- grad_w_out: float32 [1024, 1024], P('tensor')
- grad_ln2_gain: float32 [1024], replicated
- grad_ln2_bias: float32 [1024], replicated
- grad_w_gate: float32 [1024, 4096], P(None, 'tensor')
- grad_w_up: float32 [1024, 4096], P(None, 'tensor')
- grad_w_down: float32 [4096, 1024], P('tensor')
The draws below stay inside these ranges and needn't reach their ends.
Inputs may be any that keep to these rules, and one draw needn't show every extreme that they name: `lengths`: slot w holds the rows w * 2048 to w * 2048 + 2047; rows of a slot past its length are padding. Among the 2 slots of each index of dp, one holds exactly 2048 live rows.
All inputs are finite; a program needn't handle non-finite values.
Results may differ from the reference program's by a relative error of at most 0.024.
Values may be sent and summed in bfloat16 or wider, within the bound.
A program may use at most 320 MiB of HBM per device.

```python
import jax
import jax.numpy as jnp
from jax import lax

D = 1024
HEADS = 16
HD = 64
FF = 4096
WIN = 2048
SLOTS = 2
WINDOWS = 8
TOKENS = 16384
N_TENSOR = 8


def draw_lengths(key, part):
    key = jax.random.fold_in(key, 11)
    full_key, rest_key = jax.random.split(key)
    full_slot = jax.random.randint(full_key, (WINDOWS // SLOTS,), 0, SLOTS)
    slot_place = jnp.arange(WINDOWS, dtype=jnp.int32) % SLOTS
    full_each = jnp.repeat(full_slot, SLOTS)
    others = jax.random.randint(rest_key, (WINDOWS,), 1, WIN + 1)
    return jnp.where(slot_place == full_each, WIN, others).astype(jnp.int32)


def shard_levels(rng, extent, cuts, smallest, top_value):
    def one(axis_at, parts):
        heights = jax.random.uniform(jax.random.fold_in(jax.random.fold_in(rng, 6), axis_at), (parts,), jnp.float32, smallest / len(cuts), top_value / len(cuts))
        return jnp.repeat(jnp.exp(heights), extent[axis_at] // parts).reshape((-1,) + (1,) * (len(extent) - axis_at - 1))

    factor_of = one(*cuts[0])
    for cut in cuts[1:]:
        factor_of = factor_of * one(*cut)
    return factor_of


def centred(stream_key, dims, deviation, reach, pieces=(), held_as=jnp.bfloat16):
    values = jax.random.normal(stream_key, dims, jnp.float32) * deviation
    if len(pieces) > 0:
        values = shard_levels(stream_key, dims, pieces, -0.22, 0.18) * values
    return jnp.clip(values, min=-reach, max=reach).astype(held_as)


def setup_inputs(seed: int = 0) -> dict:
    key_of = jax.random.split(jax.random.key(seed), 15)
    return {
        "tokens": centred(key_of[0], (TOKENS, D), 1.0, 6.0, ((0, 32),)),
        "lengths": draw_lengths(jax.random.fold_in(key_of[14], 71), 0),
        "ln1_gain": jnp.clip(1.0 + 0.1 * jax.random.normal(key_of[2], (D,), jnp.float32), 0.5, 1.5),
        "ln1_bias": centred(key_of[3], (D,), 0.5, 3.0, (), jnp.float32),
        "w_query": centred(key_of[4], (D, D), D ** -0.5, 0.1875, ((1, 8),)),
        "w_key": centred(key_of[5], (D, D), D ** -0.5, 0.1875, ((1, 8),)),
        "w_value": centred(key_of[6], (D, D), D ** -0.5, 0.1875, ((1, 8),)),
        "w_out": centred(key_of[7], (D, D), (D * 32 // WIN) ** -0.5, 1.5, ((0, 8),)),
        "ln2_gain": jnp.clip(1.0 + 0.1 * jax.random.normal(key_of[8], (D,), jnp.float32), 0.5, 1.5),
        "ln2_bias": centred(key_of[9], (D,), 0.5, 3.0, (), jnp.float32),
        "w_gate": centred(key_of[10], (D, FF), D ** -0.5, 0.1875, ((1, 8),)),
        "w_up": centred(key_of[11], (D, FF), D ** -0.5, 0.1875, ((1, 8),)),
        "w_down": centred(key_of[12], (FF, D), FF ** -0.5, 0.09375, ((0, 8),)),
        "cotangent": centred(key_of[13], (TOKENS, D), 1.0, 6.0, ((0, 32),)),
    }


@jax.custom_vjp
def low(v):
    return lax.optimization_barrier(v.astype(jnp.bfloat16)).astype(jnp.float32)

@jax.custom_vjp
def low_back(v):
    return v

def low_keep(v):
    return (low(v), None)

def low_pass(kept, grad):
    return (grad,)

def back_keep(v):
    return (v, None)

def back_low(kept, grad):
    return (low(grad),)
low.defvjp(low_keep, low_pass)
low_back.defvjp(back_keep, back_low)
EPSILON = 1e-05

def rope_tables():
    half_width = HD // 2
    frequency = 10000.0 ** (-jnp.arange(half_width, dtype=jnp.float32) * 2.0 / HD)
    angles = jnp.arange(WIN, dtype=jnp.float32)[:, None] * frequency[None, :]
    angles = jnp.concatenate([angles, angles], axis=1)
    return (jnp.cos(angles), jnp.sin(angles))

def rotate_pairs(values_in, cosines, sines):
    half_width = values_in.shape[-1] // 2
    swapped = jnp.concatenate([-values_in[..., half_width:], values_in[..., :half_width]], axis=-1)
    return values_in * cosines + swapped * sines

def layer_norm(values_in, norm_gain, norm_bias):
    centre = values_in - lax.optimization_barrier(jnp.mean(values_in, axis=-1, keepdims=True))
    variance = lax.optimization_barrier(jnp.mean(centre * centre, axis=-1, keepdims=True))
    return centre * lax.rsqrt(variance + EPSILON) * norm_gain + norm_bias

def attend_head(query_head, key_head, value_head, live_keys):
    raw_scores = jnp.dot(query_head, key_head.T, precision=lax.Precision.HIGHEST)
    scores = low_back(raw_scores) * HD ** (-0.5)
    scores = jnp.where(live_keys[None, :], scores, -1e+30)
    row_max = lax.optimization_barrier(jnp.max(scores, axis=1, keepdims=True))
    shifted = jnp.exp(scores - row_max)
    attn_probs = shifted / lax.optimization_barrier(jnp.sum(shifted, axis=1, keepdims=True))
    return jnp.dot(low(attn_probs), value_head, precision=lax.Precision.HIGHEST)

def forward(block_rows, params, length):
    gain_one, bias_one, w_query, w_key, w_value, w_out, gain_two, bias_two, w_gate, w_up, w_down = params
    group_count = N_TENSOR
    group_width = D // group_count
    group_heads = HEADS // group_count
    group_hidden = FF // group_count
    cosines, sines = rope_tables()
    cos_four = cosines[None, :, None, :]
    sin_four = sines[None, :, None, :]
    live_keys = jnp.arange(WIN) < length
    normed_one = low(layer_norm(block_rows, gain_one, bias_one))
    copies_one = low_back(jnp.broadcast_to(normed_one, (group_count, WIN, D)))

    def project(weight):
        product = jnp.einsum('gtd,dgc->gtc', copies_one, weight.reshape(D, group_count, group_width), precision=lax.Precision.HIGHEST)
        return product.reshape(group_count, WIN, group_heads, HD)
    queries = low(rotate_pairs(low_back(project(w_query)), cos_four, sin_four))
    keys_all = low(rotate_pairs(low_back(project(w_key)), cos_four, sin_four))
    values_all = low(low_back(project(w_value)))

    def by_head(grouped):
        return jnp.transpose(grouped, (0, 2, 1, 3)).reshape(HEADS, WIN, HD)
    attend_saved = jax.checkpoint(attend_head)
    mixed = lax.map(lambda trio: attend_saved(trio[0], trio[1], trio[2], live_keys), (by_head(queries), by_head(keys_all), by_head(values_all)))
    mixed = low(low_back(mixed))
    mixed = jnp.transpose(mixed.reshape(group_count, group_heads, WIN, HD), (0, 2, 1, 3)).reshape(group_count, WIN, group_width)
    attn_parts = jnp.einsum('gtc,gcd->gtd', mixed, w_out.reshape(group_count, group_width, D), precision=lax.Precision.HIGHEST)
    attn_parts = low(low_back(attn_parts))
    middle = block_rows + lax.optimization_barrier(jnp.sum(attn_parts, axis=0))
    normed_two = low(layer_norm(middle, gain_two, bias_two))
    copies_two = low_back(jnp.broadcast_to(normed_two, (group_count, WIN, D)))
    gate_value = low_back(jnp.einsum('gtd,dgf->gtf', copies_two, w_gate.reshape(D, group_count, group_hidden), precision=lax.Precision.HIGHEST))
    up_value = low_back(jnp.einsum('gtd,dgf->gtf', copies_two, w_up.reshape(D, group_count, group_hidden), precision=lax.Precision.HIGHEST))
    hidden = low(jax.nn.silu(gate_value) * up_value)
    ffn_parts = jnp.einsum('gtf,gfd->gtd', hidden, w_down.reshape(group_count, group_hidden, D), precision=lax.Precision.HIGHEST)
    ffn_parts = low(low_back(ffn_parts))
    return middle + lax.optimization_barrier(jnp.sum(ffn_parts, axis=0))

def reference(tokens, lengths, ln1_gain, ln1_bias, w_query, w_key, w_value, w_out, ln2_gain, ln2_bias, w_gate, w_up, w_down, cotangent):
    params = tuple((item.astype(jnp.float32) for item in (ln1_gain, ln1_bias, w_query, w_key, w_value, w_out, ln2_gain, ln2_bias, w_gate, w_up, w_down)))
    blocks = tokens.astype(jnp.float32).reshape(WINDOWS, WIN, D)
    seeds = cotangent.astype(jnp.float32).reshape(WINDOWS, WIN, D)

    def one_window(running, window_item):
        block_rows, seed_rows, length = window_item
        result, pullback = jax.vjp(lambda rows_in, weights_in: forward(rows_in, weights_in, length), block_rows, params)
        grad_rows, grad_params = pullback(seed_rows)
        running = jax.tree.map(lambda left, right: left + right, running, grad_params)
        return (running, (result.astype(jnp.bfloat16), grad_rows.astype(jnp.bfloat16)))
    zeros_tree = jax.tree.map(jnp.zeros_like, params)
    totals, (outputs, grads) = lax.scan(one_window, zeros_tree, (blocks, seeds, lengths))
    return (outputs.reshape(TOKENS, D), grads.reshape(TOKENS, D), totals[0], totals[1], totals[2], totals[3], totals[4], totals[5], totals[6], totals[7], totals[8], totals[9], totals[10])
```

```python
import functools

import jax
import jax.numpy as jnp
import numpy as np
from jax import lax
from jax.experimental import pallas as pl
from jax.experimental.pallas import tpu as pltpu
from jax.sharding import PartitionSpec as P

HD = 64
WIN = 2048
EPSILON = 1e-05
SCALE = HD ** (-0.5)
LOG2E = 1.4426950408889634
C2 = SCALE * LOG2E
NT = (((1,), (1,)), ((), ()))
NN = (((1,), (0,)), ((), ()))
TN = (((0,), (0,)), ((), ()))
MESH = pl.DeviceIdType.MESH
F32 = jnp.float32
BF16 = jnp.bfloat16
MIB = 1024 * 1024
HBM = pl.BlockSpec(memory_space=pl.ANY)
VMEM = pl.BlockSpec(memory_space=pltpu.VMEM)


def dot(a, b, dims=NN):
    return lax.dot_general(a, b, dims, preferred_element_type=F32)


def shape(dims, kind=BF16):
    return jax.ShapeDtypeStruct(dims, kind)


class Sizes:
    def __init__(self, n_dp, n_t, rows, d, cw, cfull):
        self.n_dp, self.n_t, self.rows, self.d = n_dp, n_t, rows, d
        self.X, self.H = n_dp // 2, n_t // 2
        self.G = WIN // rows
        self.NG = n_t // self.G
        self.cw, self.hw = cw, self.NG * cw
        self.cf = cfull // 2


class Place:
    def __init__(self, z):
        self.z = z
        dp, t = lax.axis_index("dp"), lax.axis_index("tensor")
        self.dp, self.t = dp, t
        self.x, self.c = dp // 2, dp % 2
        self.hi, self.lo = t // 2, t % 2
        self.g, self.r = t // z.G, t % z.G

    def core(self):
        return (self.x * 2 + 1 - self.c, self.t)

    def y(self):
        return (self.dp, self.hi * 2 + 1 - self.lo)

    def xi(self, i):
        return (self.x + i) % self.z.X

    def xdev(self, i):
        return (self.xi(i) * 2 + self.c, self.t)

    def hii(self, i):
        return (self.hi + i) % self.z.H

    def hdev(self, i):
        return (self.dp, self.hii(i) * 2 + self.lo)

    def ri(self, i):
        return (self.r + i) % self.z.G

    def rdev(self, i):
        return (self.dp, self.g * self.z.G + self.ri(i))

    def gi(self, i):
        return (self.g + i) % self.z.NG

    def gdev(self, i):
        return (self.dp, self.gi(i) * self.z.G + self.r)


class Net:
    def __init__(self, send, recv, local=None):
        self.send, self.recv, self.local_sem = send, recv, local
        self.count, self.local_count = 0, 0
        self.all = []

    def remote(self, src, dst, device):
        k = self.count
        self.count += 1
        cp = pltpu.make_async_remote_copy(
            src_ref=src, dst_ref=dst, send_sem=self.send.at[k], recv_sem=self.recv.at[k],
            device_id=device, device_id_type=MESH,
        )
        self.all.append(cp)
        return cp

    def local(self, src, dst):
        k = self.local_count
        self.local_count += 1
        return pltpu.make_async_copy(src, dst, self.local_sem.at[k])

    def wait_sends(self):
        for cp in self.all:
            cp.wait_send()


def meet(devices):
    barrier = pltpu.get_barrier_semaphore()
    for device in devices:
        pl.semaphore_signal(barrier, inc=1, device_id=device, device_id_type=MESH)
    pl.semaphore_wait(barrier, len(devices))


def part(i, n):
    return pl.ds(pl.multiple_of(i * n, n), n)


def comm_call(body, z, name, cid, out_shape, in_specs, out_specs, scratch=(), n=64, vmem=None):
    return pl.pallas_call(
        functools.partial(body, z),
        out_shape=out_shape,
        in_specs=in_specs,
        out_specs=out_specs,
        scratch_shapes=[
            pltpu.SemaphoreType.DMA((n,)),
            pltpu.SemaphoreType.DMA((n,)),
            pltpu.SemaphoreType.DMA((16,)),
            *scratch,
        ],
        compiler_params=pltpu.CompilerParams(
            collective_id=cid, has_side_effects=True, vmem_limit_bytes=vmem
        ),
        name=name,
    )


def gather_rows_kernel(z, n1, w3, n1s, w3s, send, recv, lsem):
    p, net = Place(z), Net(send, recv, lsem)
    rq = z.d // z.n_dp
    meet(
        [p.rdev(i) for i in range(1, z.G)]
        + [p.gdev(i) for i in range(1, z.NG)]
        + [p.xdev(i) for i in range(1, z.X)]
        + [p.core()]
    )
    mine = n1s.at[part(p.r, z.rows)]
    rows_out = [net.remote(n1, mine, p.rdev(i)) for i in range(1, z.G)]
    quarter = part(p.dp, rq)
    w_own = w3s.at[p.g, :, quarter]
    w_out = [net.remote(w3.at[:, quarter], w_own, p.gdev(i)) for i in range(1, z.NG)]
    for cp in w_out + rows_out:
        cp.start()
    keep = [net.local(n1, mine), net.local(w3.at[:, quarter], w_own)]
    for cp in keep:
        cp.start()
    keep[1].wait()
    for cp in w_out:
        cp.wait_recv()
    block = w3s.at[:, :, quarter]
    along = [net.remote(block, block, p.xdev(i)) for i in range(1, z.X)]
    for cp in along:
        cp.start()
    for cp in along:
        cp.wait_recv()
    across = []
    for x in range(z.X):
        block = w3s.at[:, :, part(x * 2 + p.c, rq)]
        across.append(net.remote(block, block, p.core()))
        across[-1].start()
    for cp in across + rows_out:
        cp.wait_recv()
    keep[0].wait()
    net.wait_sends()


def gather_weights_kernel(z, wo, wg, wu, wd, wos, wgs, wus, wds, send, recv, lsem):
    p, net = Place(z), Net(send, recv, lsem)
    qc = z.d // z.n_dp
    rx, dx, cf = z.d // z.X, z.cf // z.X, z.cf
    meet(
        [p.hdev(i) for i in range(1, z.H)]
        + [p.xdev(i) for i in range(1, z.X)]
        + [p.y(), p.core()]
    )

    def wo_rows(t):
        return part((t % z.G) * z.NG + t // z.G, z.cw)

    cols = part(p.dp, qc)
    own = wos.at[wo_rows(p.t), cols]
    o_out = [net.remote(wo.at[:, cols], own, p.hdev(i)) for i in range(1, z.H)]
    o_keep = net.local(wo.at[:, cols], own)
    o_keep.start()
    for cp in o_out:
        cp.start()

    def pieces(hi, x):
        return (
            wgs.at[part(x, rx), part(hi, cf)],
            wus.at[part(x, rx), part(hi, cf)],
            wds.at[pl.ds(pl.multiple_of(hi * cf + x * dx, 16), dx)],
        )

    src = (
        wg.at[part(p.x, rx), part(p.c, cf)],
        wu.at[part(p.x, rx), part(p.c, cf)],
        wd.at[pl.ds(pl.multiple_of(p.c * cf + p.x * dx, 16), dx)],
    )
    f_out = []
    for i in range(1, z.H):
        f_out.append([net.remote(a, b, p.hdev(i)) for a, b in zip(src, pieces(p.hi, p.x))])
        for cp in f_out[-1]:
            cp.start()
    keep = [
        net.local(wg.at[:, part(p.c, cf)], wgs.at[:, part(p.hi, cf)]),
        net.local(wu.at[:, part(p.c, cf)], wus.at[:, part(p.hi, cf)]),
        net.local(wd.at[part(p.c, cf)], wds.at[part(p.hi, cf)]),
    ]
    for cp in keep:
        cp.start()
    o_keep.wait()
    hop = [net.remote(own, own, p.y())]
    hop[0].start()
    for i in range(1, z.H):
        o_out[i - 1].wait_recv()
        block = wos.at[wo_rows(((p.hi + z.H - i) % z.H) * 2 + p.lo), cols]
        hop.append(net.remote(block, block, p.y()))
        hop[-1].start()
    f_hop = []
    for i in range(1, z.H):
        for cp in f_out[i - 1]:
            cp.wait_recv()
        for ref in pieces((p.hi + z.H - i) % z.H, p.x):
            for k in range(1, z.X):
                f_hop.append(net.remote(ref, ref, p.xdev(k)))
                f_hop[-1].start()
    for cp in hop:
        cp.wait_recv()
    along = []
    for k in range(1, z.X):
        block = wos.at[:, cols]
        along.append(net.remote(block, block, p.xdev(k)))
        along[-1].start()
    for cp in along:
        cp.wait_recv()
    across = []
    for x in range(z.X):
        block = wos.at[:, part(x * 2 + p.c, qc)]
        across.append(net.remote(block, block, p.core()))
        across[-1].start()
    for cp in f_hop + across:
        cp.wait_recv()
    for cp in keep:
        cp.wait()
    net.wait_sends()


def gather_four_kernel(z, own, four, send, recv, lsem):
    p, net = Place(z), Net(send, recv, lsem)
    meet([p.y(), p.core()])
    mine = four.at[p.lo * 2 + p.c]
    a = net.remote(own, mine, p.y())
    b = net.remote(own, mine, p.core())
    a.start()
    b.start()
    keep = net.local(own, mine)
    keep.start()
    a.wait_recv()
    other = four.at[(1 - p.lo) * 2 + p.c]
    e = net.remote(other, other, p.core())
    e.start()
    b.wait_recv()
    e.wait_recv()
    keep.wait()
    net.wait_sends()


def scatter_four_kernel(z, one, two, out_one, out_two, send, recv, lsem, rc, ry, sums):
    p, net = Place(z), Net(send, recv, lsem)
    meet([p.y(), p.core()])
    arrays = (two, one)
    outs = (out_two, out_one)
    first = []
    for k, ref in enumerate(arrays):
        pair = []
        for far in range(2):
            lo = p.lo if far == 0 else 1 - p.lo
            pair.append(net.remote(ref.at[lo * 2 + 1 - p.c], rc.at[k, far], p.core()))
        first.append(pair)
    for pair in first:
        pair[1].start()
        pair[0].start()
    second = []
    for k, ref in enumerate(arrays):
        first[k][1].wait_recv()
        total = ref[(1 - p.lo) * 2 + p.c].astype(F32) + rc[k, 1].astype(F32)
        sums[k] = total.astype(BF16)
        second.append(net.remote(sums.at[k], ry.at[k], p.y()))
        second[-1].start()
    for k, ref in enumerate(arrays):
        first[k][0].wait_recv()
        outs[k][...] = ref[p.lo * 2 + p.c].astype(F32) + rc[k, 0].astype(F32)
    for k in range(2):
        second[k].wait_recv()
        outs[k][...] = outs[k][...] + ry[k].astype(F32)
    net.wait_sends()


def mixed_kernel(z, mixed, own, send, recv, lsem):
    p, net = Place(z), Net(send, recv, lsem)
    meet([p.rdev(i) for i in range(1, z.G)])
    mine = own.at[:, part(p.r, z.hw)]
    out = [net.remote(mixed.at[part(p.ri(i), z.rows)], mine, p.rdev(i)) for i in range(1, z.G)]
    for cp in out:
        cp.start()
    keep = net.local(mixed.at[part(p.r, z.rows)], mine)
    keep.start()
    for cp in out:
        cp.wait_recv()
    keep.wait()
    net.wait_sends()


def unmix_kernel(z, own, every, send, recv, lsem):
    p, net = Place(z), Net(send, recv, lsem)
    meet([p.rdev(i) for i in range(1, z.G)])
    mine = every.at[part(p.r, z.rows)]
    out = [net.remote(own.at[:, part(p.ri(i), z.hw)], mine, p.rdev(i)) for i in range(1, z.G)]
    for cp in out:
        cp.start()
    keep = net.local(own.at[:, part(p.r, z.hw)], mine)
    keep.start()
    for cp in out:
        cp.wait_recv()
    keep.wait()
    net.wait_sends()


def scatter_rows_kernel(z, partial, got, send, recv, lsem):
    p, net = Place(z), Net(send, recv, lsem)
    meet([p.rdev(i) for i in range(1, z.G)])
    out = [net.remote(partial.at[p.ri(i)], got.at[i - 1], p.rdev(i)) for i in range(1, z.G)]
    for cp in out:
        cp.start()
    keep = net.local(partial.at[p.r], got.at[z.G - 1])
    keep.start()
    for cp in out:
        cp.wait_recv()
    keep.wait()
    net.wait_sends()


def add_refs(*values):
    total = values[0].astype(F32)
    for v in values[1:]:
        total = total + v.astype(F32)
    return total


def reduce_ffn_kernel(
    z, dg, du, dd, og, ou, od, send, recv, lsem, rgx, rux, rdx, sg, su, sd, rgz, ruz, rdz
):
    p, net = Place(z), Net(send, recv, lsem)
    rx, dx, cf = z.d // z.X, z.cf // z.X, z.cf
    meet([p.hdev(i) for i in range(1, z.H)] + [p.xdev(i) for i in range(1, z.X)] + [p.core()])
    first = []
    for i in range(1, z.X):
        xi = p.xi(i)
        first.append(
            (
                net.remote(dd.at[:, part(xi, dx)], rdx.at[i - 1], p.xdev(i)),
                net.remote(dg.at[part(xi, rx)], rgx.at[i - 1], p.xdev(i)),
                net.remote(du.at[part(xi, rx)], rux.at[i - 1], p.xdev(i)),
            )
        )
    for k in range(3):
        for trio in first:
            trio[k].start()
    seconds = []
    for k in range(3):
        for trio in first:
            trio[k].wait_recv()
        if k == 0:
            for h in range(z.H):
                sd[h] = add_refs(
                    dd[h, part(p.x, dx)], *[rdx[i, h] for i in range(z.X - 1)]
                ).astype(BF16)
        else:
            own, got, out = ((dg, rgx, sg), (du, rux, su))[k - 1]
            out[...] = add_refs(own[part(p.x, rx)], *[got[i] for i in range(z.X - 1)]).astype(BF16)
        group = []
        for i in range(1, z.H):
            hi = p.hii(i)
            if k == 0:
                group.append(net.remote(sd.at[hi], rdz.at[i - 1], p.hdev(i)))
            else:
                out, got = ((sg, rgz), (su, ruz))[k - 1]
                group.append(net.remote(out.at[:, part(hi, cf)], got.at[i - 1], p.hdev(i)))
            group[-1].start()
        seconds.append(group)
    thirds = []
    for k in range(3):
        for cp in seconds[k]:
            cp.wait_recv()
        if k == 0:
            at = pl.ds(pl.multiple_of(p.c * cf + p.x * dx, 16), dx)
            od[at] = add_refs(sd[p.hi], *[rdz[i] for i in range(z.H - 1)]).astype(BF16)
            block = od.at[at]
        else:
            part_sum, got, out = ((sg, rgz, og), (su, ruz, ou))[k - 1]
            out[part(p.x, rx), part(p.c, cf)] = add_refs(
                part_sum[:, part(p.hi, cf)], *[got[i] for i in range(z.H - 1)]
            ).astype(BF16)
            block = out.at[part(p.x, rx), part(p.c, cf)]
        group = [net.remote(block, block, p.xdev(i)) for i in range(1, z.X)]
        for cp in group:
            cp.start()
        thirds.append(group)
    last = []
    for k in range(3):
        for cp in thirds[k]:
            cp.wait_recv()
        if k == 0:
            block = od.at[part(p.c, cf)]
        else:
            block = (og, ou)[k - 1].at[:, part(p.c, cf)]
        last.append(net.remote(block, block, p.core()))
        last[-1].start()
    for cp in last:
        cp.wait_recv()
    net.wait_sends()


def reduce_attn_kernel(
    z, dw, do, ow, oo, send, recv, lsem, wc, wx, ws, wg, oc, ox, os_, oy, oy_sum, oz
):
    p, net = Place(z), Net(send, recv, lsem)
    rq = z.d // z.n_dp
    qc = z.d // z.n_dp
    meet(
        [p.hdev(i) for i in range(1, z.H)]
        + [p.xdev(i) for i in range(1, z.X)]
        + [p.y(), p.core()]
    )
    c_out = []
    for k in range(z.X):
        x = p.xi(k)
        c_out.append(
            (
                net.remote(do.at[:, :, part(x * 2 + 1 - p.c, qc)], oc.at[k], p.core()),
                net.remote(dw.at[:, :, part(x * 2 + 1 - p.c, rq)], wc.at[k], p.core()),
            )
        )
    for k in list(range(1, z.X)) + [0]:
        for cp in c_out[k]:
            cp.start()
    x_out = []
    for k in list(range(1, z.X)) + [0]:
        for cp in c_out[k]:
            cp.wait_recv()
        x = p.xi(k)
        for r in range(z.G):
            os_[k, r] = add_refs(do[r, :, part(x * 2 + p.c, qc)], oc[k, r]).astype(BF16)
        for g in range(z.NG):
            ws[k, g] = add_refs(dw[g, :, part(x * 2 + p.c, rq)], wc[k, g]).astype(BF16)
        if k:
            pair = (
                net.remote(os_.at[k], ox.at[k - 1], p.xdev(k)),
                net.remote(ws.at[k], wx.at[k - 1], p.xdev(k)),
            )
            for cp in pair:
                cp.start()
            x_out.append(pair)
    for pair in x_out:
        for cp in pair:
            cp.wait_recv()
    for r in range(z.G):
        os_[0, r] = add_refs(os_[0, r], *[ox[i, r] for i in range(z.X - 1)]).astype(BF16)
    y_out = []
    for k in range(z.G // 2):
        y_out.append(net.remote(os_.at[0, k * 2 + 1 - p.lo], oy.at[k], p.y()))
        y_out[-1].start()
    for g in range(z.NG):
        ws[0, g] = add_refs(ws[0, g], *[wx[i, g] for i in range(z.X - 1)]).astype(BF16)
    g_out = []
    for i in range(1, z.NG):
        g_out.append(net.remote(ws.at[0, p.gi(i)], wg.at[i - 1], p.gdev(i)))
        g_out[-1].start()
    for cp in y_out:
        cp.wait_recv()
    for k in range(z.G // 2):
        oy_sum[k] = add_refs(os_[0, k * 2 + p.lo], oy[k]).astype(BF16)
    z_out = []
    half = z.G // 2
    for i in range(1, z.H):
        hi = p.hii(i)
        z_out.append(
            net.remote(oy_sum.at[hi % half, part(hi // half, z.cw)], oz.at[i - 1], p.hdev(i))
        )
        z_out[-1].start()
    for cp in g_out:
        cp.wait_recv()
    quarter = part(p.dp, rq)
    for m in range(3):
        ow[m, quarter] = add_refs(ws[0, p.g, m], *[wg[i, m] for i in range(z.NG - 1)]).astype(BF16)
    for cp in z_out:
        cp.wait_recv()
    cols = part(p.dp, qc)
    oo[:, cols] = add_refs(
        oy_sum[p.hi % half, part(p.hi // half, z.cw)], *[oz[i] for i in range(z.H - 1)]
    ).astype(BF16)
    along = []
    for i in range(1, z.X):
        for block in (ow.at[:, quarter], oo.at[:, cols]):
            along.append(net.remote(block, block, p.xdev(i)))
            along[-1].start()
    for cp in along:
        cp.wait_recv()
    across = []
    for x in range(z.X):
        for block in (ow.at[:, part(x * 2 + p.c, rq)], oo.at[:, part(x * 2 + p.c, qc)]):
            across.append(net.remote(block, block, p.core()))
            across[-1].start()
    for cp in across:
        cp.wait_recv()
    net.wait_sends()


def lane_of(rows):
    return lax.broadcasted_iota(jnp.int32, (rows, 128), 1)


def rope_tables():
    frequency = np.float32(10000.0) ** (-np.arange(HD // 2, dtype=np.float32) * 2.0 / HD)
    angles = np.arange(WIN, dtype=np.float32)[:, None] * frequency.astype(np.float32)[None, :]
    angles = np.concatenate([angles] * 4, axis=1)
    return np.cos(angles), np.sin(angles)


def turn(v, cosines, sines):
    swapped = jnp.where(
        lane_of(v.shape[0]) % HD < HD // 2, -pltpu.roll(v, 96, 1), pltpu.roll(v, 32, 1)
    )
    return v * cosines + swapped * sines


def spare_lanes(first, v, lane):
    high = v.astype(BF16)
    rest = v - high.astype(F32)
    middle = rest.astype(BF16)
    low = (rest - middle.astype(F32)).astype(BF16)
    s = lane % HD
    tail = jnp.where(s == 2, -middle.astype(F32), jnp.where(s == 3, -low.astype(F32), 0.0))
    return jnp.where(s == 0, first, jnp.where(s == 1, -high.astype(F32), tail))


def forward_kernel(n1, w3, cos, sin, bias, q, k, v, o, mixed, qa, *, bq):
    width = q.shape[1]
    chunk = 512

    def project(i, _):
        rows = part(i, chunk)
        a = n1[rows]
        for m, ref in enumerate((q, k, v)):
            y = dot(a, w3[m])
            for j in range(width // 128):
                t = y[:, j * 128 : j * 128 + 128]
                if m < 2:
                    t = turn(t, cos[rows], sin[rows])
                ref[rows, j * 128 : j * 128 + 128] = t.astype(BF16)
        return 0

    lax.fori_loop(0, WIN // chunk, project, 0)
    lane_k, lane_q = lane_of(WIN), lane_of(bq)

    def block(i, _):
        j, b = i // (WIN // bq), i % (WIN // bq)
        col, rows = part(j, 128), part(b, bq)
        k2, v2, kb, q2 = k[:, col], v[:, col], bias[...], q[rows, col]
        mixes = []
        for e in range(2):
            own_k = (lane_k < HD) if e == 0 else (lane_k >= HD)
            own_q = (lane_q < HD) if e == 0 else (lane_q >= HD)
            k_e = jnp.where(own_k, k2, kb)
            v_e = jnp.where(own_k, v2, jnp.ones_like(v2))
            q_e = jnp.where(own_q, q2, jnp.where(lane_q % HD == 0, 1.0, 0.0).astype(BF16))
            s = dot(q_e, k_e, NT)
            top = jnp.max(s, axis=1, keepdims=True)
            p = jnp.exp2((s - top) * C2).astype(BF16)
            sums = dot(p, v_e)
            mixes.append(sums / pltpu.roll(sums, HD, 1))
            norm = jnp.where(own_q, 0.0, top + jnp.log2(jnp.where(own_q, 1.0, sums)) * (1.0 / C2))
            full = jnp.where(own_q, q2.astype(F32), spare_lanes(1.0, norm, lane_q))
            qa[2 * j + e, rows] = full.astype(BF16)
        mix = jnp.where(lane_q < HD, mixes[0], mixes[1])
        o[rows, col] = mix
        mixed[rows, col] = mix.astype(BF16)
        return 0

    lax.fori_loop(0, (width // 128) * (WIN // bq), block, 0)


def attend_forward(n1, w3, cos, sin, bias):
    hw = w3.shape[2]
    return pl.pallas_call(
        functools.partial(forward_kernel, bq=256),
        out_shape=(
            shape((WIN, hw)),
            shape((WIN, hw)),
            shape((WIN, hw)),
            shape((WIN, hw), F32),
            shape((WIN, hw)),
            shape((hw // HD, WIN, 128)),
        ),
        in_specs=[VMEM] * 5,
        out_specs=[VMEM] * 6,
        compiler_params=pltpu.CompilerParams(vmem_limit_bytes=60 * MIB),
        name="attend_forward",
    )(n1, w3, cos, sin, bias)


def backward_kernel(qa, q, k, v, do, o, bias, cos, sin, dq, dk, dv, do_e, dk_sum, dv_sum, *, bq):
    width = q.shape[1]
    lane_q, lane_k = lane_of(bq), lane_of(WIN)
    blocks = WIN // bq

    def block(i, _):
        j, b = i // blocks, i % blocks
        col, rows = part(j, 128), part(b, bq)
        q2, do2, k2, v2 = q[rows, col], do[rows, col], k[:, col], v[:, col]
        prod = do2.astype(F32) * o[rows, col]
        s64 = lane_k % HD
        ones3 = jnp.where((s64 >= 1) & (s64 <= 3), 1.0, 0.0).astype(BF16)
        kb = bias[...] + ones3
        dks, dvs, dqs = [], [], []
        for e in range(2):
            own_q = (lane_q < HD) if e == 0 else (lane_q >= HD)
            own_k = (lane_k < HD) if e == 0 else (lane_k >= HD)
            delta = jnp.sum(jnp.where(own_q, prod, 0.0), axis=1, keepdims=True)
            spare = spare_lanes(0.0, jnp.broadcast_to(delta, prod.shape), lane_q)
            do_e[...] = jnp.where(own_q, do2.astype(F32), spare).astype(BF16)
            k_e = jnp.where(own_k, k2, kb)
            v_e = jnp.where(own_k, v2, ones3)
            p = jnp.exp2(dot(k_e, qa[2 * j + e, rows], NT) * C2)
            ds = (p * dot(v_e, do_e[...], NT)).astype(BF16)
            dvs.append(dot(p.astype(BF16), do2))
            dks.append(dot(ds, q2))
            dqs.append(dot(ds, k2, TN))
        dv_new = jnp.where(lane_k < HD, dvs[0], dvs[1])
        dk_new = jnp.where(lane_k < HD, dks[0], dks[1])

        @pl.when(b == 0)
        def _():
            dv_sum[...] = dv_new
            dk_sum[...] = dk_new

        @pl.when(b > 0)
        def _():
            dv_sum[...] += dv_new
            dk_sum[...] += dk_new

        dq_new = jnp.where(lane_q < HD, dqs[0], dqs[1]) * SCALE
        dq[rows, col] = turn(dq_new, cos[rows], -sin[rows]).astype(BF16)

        @pl.when(b == blocks - 1)
        def _():
            dv[:, col] = dv_sum[...].astype(BF16)
            dk[:, col] = turn(dk_sum[...] * SCALE, cos[...], -sin[...]).astype(BF16)

        return 0

    lax.fori_loop(0, (width // 128) * blocks, block, 0)


def attend_backward(qa, q, k, v, do, o, bias, cos, sin):
    hw = q.shape[1]
    bq = 512
    return pl.pallas_call(
        functools.partial(backward_kernel, bq=bq),
        out_shape=(shape((WIN, hw)),) * 3,
        in_specs=[VMEM] * 9,
        out_specs=[VMEM] * 3,
        scratch_shapes=[
            pltpu.VMEM((bq, 128), BF16),
            pltpu.VMEM((WIN, 128), F32),
            pltpu.VMEM((WIN, 128), F32),
        ],
        compiler_params=pltpu.CompilerParams(vmem_limit_bytes=60 * MIB),
        name="attend_backward",
    )(qa, q, k, v, do, o, bias, cos, sin)


def norm_stats(v):
    centre = v - jnp.mean(v, axis=-1, keepdims=True)
    inverse = lax.rsqrt(jnp.mean(centre * centre, axis=-1, keepdims=True) + EPSILON)
    return centre * inverse, inverse


def norm_backward(grad_in, scaled, inverse, gain):
    weighted = grad_in * gain
    first_mean = jnp.mean(weighted, axis=-1, keepdims=True)
    second_mean = jnp.mean(weighted * scaled, axis=-1, keepdims=True)
    return inverse * (weighted - first_mean - scaled * second_mean)


def per_device(
    n_dp, n_t, tokens, lengths, ln1_gain, ln1_bias, w_query, w_key, w_value, w_out,
    ln2_gain, ln2_bias, w_gate, w_up, w_down, cotangent,
):
    rows, d = tokens.shape
    cw, cfull = w_query.shape[1], w_gate.shape[1]
    z = Sizes(n_dp, n_t, rows, d, cw, cfull)
    G, NG, H, X, hw, cf = z.G, z.NG, z.H, z.X, z.hw, z.cf
    rq, rx, dx = d // n_dp, d // X, cf // X
    slot = lax.axis_index("tensor") // G
    length = lax.dynamic_index_in_dim(lengths, slot, keepdims=False)
    lane = lax.broadcasted_iota(jnp.int32, (WIN, 128), 1) % HD
    place = lax.broadcasted_iota(jnp.int32, (WIN, 128), 0)
    bias = jnp.where((lane == 0) & (place >= length), -1e30, 0.0).astype(BF16)
    cos, sin = (jnp.asarray(t, F32) for t in rope_tables())

    own_tokens = tokens.astype(F32)
    scaled_one, inverse_one = norm_stats(own_tokens)
    normed_one = (scaled_one * ln1_gain + ln1_bias).astype(BF16)
    w_three = jnp.stack([w_query, w_key, w_value])
    n1, w3 = comm_call(
        gather_rows_kernel, z, "gather_rows", 1,
        (shape((WIN, d)), shape((NG, 3, d, cw))), [HBM] * 2, [HBM] * 2,
    )(normed_one, w_three)
    wo, wg, wu, wd = comm_call(
        gather_weights_kernel, z, "gather_weights", 2,
        (shape((d, d)), shape((d, H * cf)), shape((d, H * cf)), shape((H * cf, d))),
        [HBM] * 4, [HBM] * 4, n=96,
    )(w_out, w_gate, w_up, w_down)
    w3 = jnp.transpose(w3, (1, 2, 0, 3)).reshape(3, d, hw)
    q, k, v, o, mixed, qa = attend_forward(n1, w3, cos, sin, bias)
    mixed_own = comm_call(
        mixed_kernel, z, "mixed_rows", 3, shape((rows, d)), [HBM], HBM
    )(mixed)
    middle = own_tokens + dot(mixed_own, wo)
    scaled_two, inverse_two = norm_stats(middle)
    normed_two = (scaled_two * ln2_gain + ln2_bias).astype(BF16)

    four = functools.partial(comm_call, gather_four_kernel, z)
    seed = four("gather_seed", 4, shape((4, rows, d)), [HBM], HBM)(cotangent)
    n2 = four("gather_normed", 5, shape((4, rows, d)), [HBM], HBM)(normed_two)
    seed, n2 = seed.reshape(4 * rows, d), n2.reshape(4 * rows, d)
    gate, up = dot(n2, wg), dot(n2, wu)
    sig = jax.nn.sigmoid(gate)
    silu = gate * sig
    hidden = (silu * up).astype(BF16)
    part_out = dot(hidden, wd).astype(BF16)
    grad_hidden = dot(seed, wd, NT)
    grad_gate = (grad_hidden * up * sig * (1.0 + gate * (1.0 - sig))).astype(BF16)
    grad_up = (grad_hidden * silu).astype(BF16)
    part_two = (dot(grad_gate, wg, NT) + dot(grad_up, wu, NT)).astype(BF16)
    p_down = dot(hidden, seed, TN).astype(BF16).reshape(H, cf, d)
    p_gate = dot(n2, grad_gate, TN).astype(BF16)
    p_up = dot(n2, grad_up, TN).astype(BF16)
    ffn, grad_two = comm_call(
        scatter_four_kernel, z, "scatter_four", 6,
        (shape((rows, d), F32), shape((rows, d), F32)), [VMEM] * 2, [VMEM] * 2,
        [
            pltpu.VMEM((2, 2, rows, d), BF16),
            pltpu.VMEM((2, rows, d), BF16),
            pltpu.VMEM((2, rows, d), BF16),
        ],
        vmem=60 * MIB,
    )(part_out.reshape(4, rows, d), part_two.reshape(4, rows, d))
    output = (middle + ffn).astype(BF16)
    gain_two = jnp.sum(grad_two * scaled_two, axis=0)
    bias_two = jnp.sum(grad_two, axis=0)
    grad_middle = cotangent.astype(F32) + norm_backward(grad_two, scaled_two, inverse_two, ln2_gain)
    grad_low = grad_middle.astype(BF16)
    p_wo = dot(mixed_own, grad_low, TN).astype(BF16).reshape(G, hw, d)
    grad_mixed = dot(grad_low, wo, NT).astype(BF16)
    do = comm_call(unmix_kernel, z, "unmix_rows", 7, shape((WIN, hw)), [HBM], HBM)(grad_mixed)
    g_gate, g_up, g_down = comm_call(
        reduce_ffn_kernel, z, "reduce_ffn", 8,
        (shape((d, 2 * cf)), shape((d, 2 * cf)), shape((2 * cf, d))), [VMEM] * 3, [VMEM] * 3,
        [
            pltpu.VMEM((X - 1, rx, H * cf), BF16),
            pltpu.VMEM((X - 1, rx, H * cf), BF16),
            pltpu.VMEM((X - 1, H, dx, d), BF16),
            pltpu.VMEM((rx, H * cf), BF16),
            pltpu.VMEM((rx, H * cf), BF16),
            pltpu.VMEM((H, dx, d), BF16),
            pltpu.VMEM((H - 1, rx, cf), BF16),
            pltpu.VMEM((H - 1, rx, cf), BF16),
            pltpu.VMEM((H - 1, dx, d), BF16),
        ],
        vmem=60 * MIB,
    )(p_gate, p_up, p_down)
    dq, dk, dv = attend_backward(qa, q, k, v, do, o, bias, cos, sin)
    part_one = (dot(dq, w3[0], NT) + dot(dk, w3[1], NT) + dot(dv, w3[2], NT)).astype(BF16)
    got = comm_call(
        scatter_rows_kernel, z, "scatter_rows", 9, shape((G, rows, d)), [HBM], HBM
    )(part_one.reshape(G, rows, d))
    p_w3 = jnp.stack([dot(n1, t, TN).astype(BF16) for t in (dq, dk, dv)])
    p_w3 = jnp.transpose(p_w3.reshape(3, d, NG, cw), (2, 0, 1, 3))
    g_w3, g_wo = comm_call(
        reduce_attn_kernel, z, "reduce_attn", 10,
        (shape((3, d, cw)), shape((cw, d))), [VMEM] * 2, [VMEM] * 2,
        [
            pltpu.VMEM((X, NG, 3, rq, cw), BF16),
            pltpu.VMEM((X - 1, NG, 3, rq, cw), BF16),
            pltpu.VMEM((X, NG, 3, rq, cw), BF16),
            pltpu.VMEM((NG - 1, 3, rq, cw), BF16),
            pltpu.VMEM((X, G, hw, rq), BF16),
            pltpu.VMEM((X - 1, G, hw, rq), BF16),
            pltpu.VMEM((X, G, hw, rq), BF16),
            pltpu.VMEM((G // 2, hw, rq), BF16),
            pltpu.VMEM((G // 2, hw, rq), BF16),
            pltpu.VMEM((H - 1, cw, rq), BF16),
        ],
        vmem=60 * MIB,
    )(p_w3, p_wo)
    grad_one = jnp.sum(got.astype(F32), axis=0)
    gain_one = jnp.sum(grad_one * scaled_one, axis=0)
    bias_one = jnp.sum(grad_one, axis=0)
    back_one = norm_backward(grad_one, scaled_one, inverse_one, ln1_gain)
    grad_tokens = (grad_middle + back_one).astype(BF16)
    norms = lax.psum(jnp.stack([gain_one, bias_one, gain_two, bias_two]), ("dp", "tensor"))
    return (
        output, grad_tokens, norms[0], norms[1],
        g_w3[0].astype(F32), g_w3[1].astype(F32), g_w3[2].astype(F32), g_wo.astype(F32),
        norms[2], norms[3], g_gate.astype(F32), g_up.astype(F32), g_down.astype(F32),
    )


def solution(mesh):
    rows, cols, each = P(("dp", "tensor"), None), P(None, "tensor"), P("tensor", None)
    return jax.shard_map(
        functools.partial(per_device, mesh.shape["dp"], mesh.shape["tensor"]),
        mesh=mesh,
        in_specs=(
            rows, P("dp"), P(), P(), cols, cols, cols, each, P(), P(), cols, cols, each, rows,
        ),
        out_specs=(
            rows, rows, P(), P(), cols, cols, cols, each, P(), P(), cols, cols, each,
        ),
        check_vma=False,
    )
```

```python
import functools

import jax
import jax.numpy as jnp
import numpy as np
from jax import lax
from jax.experimental import pallas as pl
from jax.experimental.pallas import tpu as pltpu
from jax.sharding import PartitionSpec as P

HD = 64
WIN = 2048
EPSILON = 1e-05
SCALE = HD ** (-0.5)
LOG2E = 1.4426950408889634
C2 = SCALE * LOG2E
NT = (((1,), (1,)), ((), ()))
NN = (((1,), (0,)), ((), ()))
TN = (((0,), (0,)), ((), ()))
MESH = pl.DeviceIdType.MESH
F32 = jnp.float32
BF16 = jnp.bfloat16
MIB = 1024 * 1024
HBM = pl.BlockSpec(memory_space=pl.ANY)
VMEM = pl.BlockSpec(memory_space=pltpu.VMEM)


def dot(a, b, dims=NN):
    return lax.dot_general(a, b, dims, preferred_element_type=F32)


def shape(dims, kind=BF16):
    return jax.ShapeDtypeStruct(dims, kind)


class Sizes:
    def __init__(self, n_dp, n_t, rows, d, cw, cfull):
        self.n_dp, self.n_t, self.rows, self.d = n_dp, n_t, rows, d
        self.X, self.H = n_dp // 2, n_t // 2
        self.G = WIN // rows
        self.NG = n_t // self.G
        self.cw, self.hw = cw, self.NG * cw
        self.cf = cfull // 2


class Place:
    def __init__(self, z):
        self.z = z
        dp, t = lax.axis_index("dp"), lax.axis_index("tensor")
        self.dp, self.t = dp, t
        self.x, self.c = dp // 2, dp % 2
        self.hi, self.lo = t // 2, t % 2
        self.g, self.r = t // z.G, t % z.G
        self.h2, self.hl = self.hi // 2, self.hi % 2

    def pair(self):
        return (self.dp, (self.h2 * 2 + 1 - self.hl) * 2 + self.lo)

    def h2dev(self, i):
        return (self.dp, (((self.h2 + i) % (self.z.H // 2)) * 2 + self.hl) * 2 + self.lo)

    def core(self):
        return (self.x * 2 + 1 - self.c, self.t)

    def y(self):
        return (self.dp, self.hi * 2 + 1 - self.lo)

    def xi(self, i):
        return (self.x + i) % self.z.X

    def xdev(self, i):
        return (self.xi(i) * 2 + self.c, self.t)

    def hii(self, i):
        return (self.hi + i) % self.z.H

    def hdev(self, i):
        return (self.dp, self.hii(i) * 2 + self.lo)

    def ri(self, i):
        return (self.r + i) % self.z.G

    def rdev(self, i):
        return (self.dp, self.g * self.z.G + self.ri(i))

    def gi(self, i):
        return (self.g + i) % self.z.NG

    def gdev(self, i):
        return (self.dp, self.gi(i) * self.z.G + self.r)


class Net:
    def __init__(self, send, recv, local=None):
        self.send, self.recv, self.local_sem = send, recv, local
        self.count, self.local_count = 0, 0
        self.all = []

    def remote(self, src, dst, device):
        k = self.count
        self.count += 1
        cp = pltpu.make_async_remote_copy(
            src_ref=src, dst_ref=dst, send_sem=self.send.at[k], recv_sem=self.recv.at[k],
            device_id=device, device_id_type=MESH,
        )
        self.all.append(cp)
        return cp

    def local(self, src, dst):
        k = self.local_count
        self.local_count += 1
        return pltpu.make_async_copy(src, dst, self.local_sem.at[k])

    def wait_sends(self):
        for cp in self.all:
            cp.wait_send()


def meet(devices):
    barrier = pltpu.get_barrier_semaphore()
    for device in devices:
        pl.semaphore_signal(barrier, inc=1, device_id=device, device_id_type=MESH)
    pl.semaphore_wait(barrier, len(devices))


def part(i, n):
    return pl.ds(pl.multiple_of(i * n, n), n)


def comm_call(body, z, name, cid, out_shape, in_specs, out_specs, scratch=(), n=64, vmem=None):
    return pl.pallas_call(
        functools.partial(body, z),
        out_shape=out_shape,
        in_specs=in_specs,
        out_specs=out_specs,
        scratch_shapes=[
            pltpu.SemaphoreType.DMA((n,)),
            pltpu.SemaphoreType.DMA((n,)),
            pltpu.SemaphoreType.DMA((64,)),
            *scratch,
        ],
        compiler_params=pltpu.CompilerParams(
            collective_id=cid, has_side_effects=True, vmem_limit_bytes=vmem
        ),
        name=name,
    )


def middle_kernel(
    z, own_h, tok_h, wo_h, wg_h, wu_h, wd_h, wg_o, wu_o, wd_o, seed_h, cot, gain, beta,
    out_part, out_pair, grad_mid, grad_mix, p_wo, p_gate, p_up, p_down, sums,
    send, recv, lsem,
    own, tok, wo, wg, wu, wd, seed, n2, middle, hidden, gg, gu, two, one, rc, ry, tot, out_f,
):
    p, net = Place(z), Net(send, recv, lsem)
    rows, d = z.rows, z.d
    cf = z.cf
    pairs = [(own_h, own), (wo_h, wo), (tok_h, tok)]
    for k in range(z.H):
        h2, lo = (p.h2 + k // 2) % (z.H // 2), (p.lo + k) % 2
        at = part(h2 * 2 + lo, cf)
        if k == 0:
            half = part(p.c, cf)
            pairs += [(wg_o.at[:, half], wg.at[:, at]), (wu_o.at[:, half], wu.at[:, at]),
                      (wd_o.at[half], wd.at[at])]
        else:
            pairs += [(wg_h.at[:, at], wg.at[:, at]), (wu_h.at[:, at], wu.at[:, at]),
                      (wd_h.at[at], wd.at[at])]
    for k, b in enumerate((p.hl * 2 + p.c, p.hl * 2 + 1 - p.c,
                           (1 - p.hl) * 2 + p.c, (1 - p.hl) * 2 + 1 - p.c)):
        at = part(b, rows)
        pairs.append((seed_h.at[at] if k else cot, seed.at[at]))
    loads = [net.local(a, b) for a, b in pairs]
    for cp in loads:
        cp.start()
    meet([p.pair(), p.core()])
    chunk = 128
    blocks = [p.hl * 2 + p.c, p.hl * 2 + 1 - p.c,
              (1 - p.hl) * 2 + 1 - p.c, (1 - p.hl) * 2 + p.c]

    def block_rows(b):
        return pl.ds(pl.multiple_of(b * rows, rows), rows)

    for cp in loads[:3]:
        cp.wait()

    def norm(i, _):
        at = part(i, chunk)
        m = tok[at].astype(F32) + dot(own[at], wo[...])
        middle[at] = m
        scaled, _ = norm_stats(m)
        here = pl.ds(pl.multiple_of(blocks[0] * rows + i * chunk, chunk), chunk)
        n2[here] = (scaled * gain[...] + beta[...]).astype(BF16)
        return 0

    lax.fori_loop(0, rows // chunk, norm, 0)
    mine, far = n2.at[block_rows(blocks[0])], n2.at[block_rows(blocks[3])]
    n_pair, n_core = net.remote(mine, mine, p.pair()), net.remote(mine, mine, p.core())
    n_hop = net.remote(far, far, p.core())
    n_pair.start()
    n_core.start()
    for cp in loads[3:]:
        cp.wait()
    sub = min(256, rows)

    def ffn(b):
        def body(i, _):
            at = pl.ds(pl.multiple_of(b * rows + i * sub, sub), sub)
            a, e = n2[at], seed[at]
            gate, up = dot(a, wg[...]), dot(a, wu[...])
            sig = jax.nn.sigmoid(gate)
            silu = gate * sig
            h = (silu * up).astype(BF16)
            hidden[at] = h
            one[at] = dot(h, wd[...]).astype(BF16)
            gh = dot(e, wd[...], NT)
            g1 = (gh * up * sig * (1.0 + gate * (1.0 - sig))).astype(BF16)
            g2 = (gh * silu).astype(BF16)
            gg[at] = g1
            gu[at] = g2
            two[at] = (dot(g1, wg[...], NT) + dot(g2, wu[...], NT)).astype(BF16)
            return 0

        lax.fori_loop(0, rows // sub, body, 0)

    def send_core(k, b, far):
        ref = (two, one)[k]
        cp = net.remote(ref.at[block_rows(b)], rc.at[k, far], p.core())
        cp.start()
        return cp

    ffn(blocks[0])
    n_core.wait_recv()
    ffn(blocks[1])
    near = [send_core(k, blocks[1], 0) for k in range(2)]
    n_pair.wait_recv()
    n_hop.start()
    n_hop.wait_recv()
    ffn(blocks[2])
    away = [send_core(k, blocks[2], 1) for k in range(2)]
    ffn(blocks[3])
    for k, ref in enumerate((two, one)):
        away[k].wait_recv()
        tot[k] = add_refs(ref[block_rows(blocks[3])], rc[k, 1]).astype(BF16)
        if k == 0:
            to_pair = net.remote(tot.at[0], ry, p.pair())
            to_pair.start()
    stores = []
    for a, b, into, out in ((hidden, seed, wd, p_down), (n2, gg, wg, p_gate), (n2, gu, wu, p_up)):
        for i in range(into.shape[0] // 256):
            at = pl.ds(i * 256, 256)
            into[at] = dot(a[:, at], b[...], TN).astype(BF16)
        stores.append(net.local(into, out))
        stores[-1].start()
    near[0].wait_recv()
    to_pair.wait_recv()

    def back(i, carry):
        at = part(i, chunk)
        here = pl.ds(pl.multiple_of(blocks[0] * rows + i * chunk, chunk), chunk)
        scaled, inverse = norm_stats(middle[at])
        e = add_refs(two[here], rc[0, 0, at], ry[at])
        m = seed[here].astype(F32) + norm_backward(e, scaled, inverse, gain[...])
        out_f[at] = add_refs(middle[at], one[here], rc[1, 0, at])
        middle[at] = m
        tok[at] = m.astype(BF16)
        return (
            carry[0] + jnp.sum(e * scaled, axis=0, keepdims=True),
            carry[1] + jnp.sum(e, axis=0, keepdims=True),
        )

    near[1].wait_recv()
    zero = jnp.zeros((1, d), F32)
    a, b = lax.fori_loop(0, rows // chunk, back, (zero, zero))
    sums[0:1] = a
    sums[1:2] = b
    net.wait_sends()
    for i in range(d // 256):
        at = pl.ds(i * 256, 256)
        n2[at] = dot(own[:, at], tok[...], TN).astype(BF16)
    stores.append(net.local(n2.at[pl.ds(0, d)], p_wo))
    stores.append(net.local(out_f, out_part))
    stores.append(net.local(tot.at[1], out_pair))
    stores.append(net.local(middle, grad_mid))
    for cp in stores[3:]:
        cp.start()
    mixed_at = pl.ds(0, rows)
    two[mixed_at] = dot(tok[...], wo[...], NT).astype(BF16)
    last = net.local(two.at[mixed_at], grad_mix)
    last.start()
    for cp in stores + [last]:
        cp.wait()


def add_refs(*values):
    total = values[0].astype(F32)
    for v in values[1:]:
        total = total + v.astype(F32)
    return total


def lane_of(rows):
    return lax.broadcasted_iota(jnp.int32, (rows, 128), 1)


def rope_tables():
    frequency = np.float32(10000.0) ** (-np.arange(HD // 2, dtype=np.float32) * 2.0 / HD)
    angles = np.arange(WIN, dtype=np.float32)[:, None] * frequency.astype(np.float32)[None, :]
    angles = np.concatenate([angles] * 4, axis=1)
    return np.cos(angles), np.sin(angles)


def turn(v, cosines, sines):
    swapped = jnp.where(
        lane_of(v.shape[0]) % HD < HD // 2, -pltpu.roll(v, 96, 1), pltpu.roll(v, 32, 1)
    )
    return v * cosines + swapped * sines


def spare_lanes(first, v, lane):
    high = v.astype(BF16)
    rest = v - high.astype(F32)
    middle = rest.astype(BF16)
    low = (rest - middle.astype(F32)).astype(BF16)
    s = lane % HD
    tail = jnp.where(s == 2, -middle.astype(F32), jnp.where(s == 3, -low.astype(F32), 0.0))
    return jnp.where(s == 0, first, jnp.where(s == 1, -high.astype(F32), tail))


def run_at(steps, i):
    for at, functions in sorted(steps.items()):

        @pl.when(i == at)
        def _(functions=functions):
            for f in functions:
                f()


def slot_order(p, z):
    half = z.G // 2
    rhi = p.r // 2
    order = [(rhi, p.lo), (rhi, 1 - p.lo)]
    for j in range(1, half):
        order += [((rhi + j) % half, p.lo), ((rhi + j) % half, 1 - p.lo)]
    return [a * 2 + b for a, b in order]


def front_kernel(
    z, n1, w3, cos, sin, bias, wo, wg, wu, wd, cot,
    n1s, w3c, q, k, v, o, qa, own, wos, wgs, wus, wds, seed,
    send, recv, lsem, w3s, mixed,
):
    p, net = Place(z), Net(send, recv, lsem)
    rq, qc = z.d // z.n_dp, z.d // z.n_dp
    rx, dx, cf = z.d // z.X, z.cf // z.X, z.cf
    half, wide = z.G // 2, z.cw % 128 == 0
    rhi = p.r // 2
    hr = z.rows // 2

    def slot_dev(a, b):
        return (p.dp, p.g * z.G + a * 2 + b)

    def slot_rows(a, b, top):
        return pl.ds(pl.multiple_of((a * 2 + b) * z.rows + top * hr, 16), hr)

    near = [((rhi + j) % half) for j in range(1, half)]
    back = [((rhi + half - j) % half) for j in range(1, half)]
    meet(
        [slot_dev(rhi, 1 - p.lo)]
        + [slot_dev(a, 1 - p.lo) for a in near]
        + [p.hdev(i) for i in range(1, z.H)]
        + [p.xdev(i) for i in range(1, z.X)]
        + [p.core()]
    )
    quarter = part(p.dp, rq)
    w_out = [
        net.remote(w3.at[:, quarter], w3s.at[p.g, :, quarter], p.gdev(i)) for i in range(1, z.NG)
    ]
    y_out, a_out = [], []
    for top in (1, 0):
        y_out.append(
            net.remote(n1.at[pl.ds(top * hr, hr)], n1s.at[slot_rows(rhi, p.lo, top)],
                       slot_dev(rhi, 1 - p.lo))
        )
    for top in (0, 1):
        a_out.append(
            [
                net.remote(n1.at[pl.ds(top * hr, hr)], n1s.at[slot_rows(rhi, p.lo, top)],
                           slot_dev(a, p.lo))
                for a in near
            ]
        )
    keep_w = net.local(w3, w3s.at[p.g])
    keep_n = net.local(n1, n1s.at[part(p.r, z.rows)])
    for cp in w_out:
        cp.start()
    y_out[0].start()
    for cp in a_out[0]:
        cp.start()
    keep_w.start()
    keep_n.start()
    y_out[1].start()
    for cp in a_out[1]:
        cp.start()
    for cp in w_out:
        cp.wait_recv()
    w_back = [(p.g + z.NG - i) % z.NG for i in range(1, z.NG)]
    along = []
    for g in w_back:
        block = w3s.at[g, :, quarter]
        along += [net.remote(block, block, p.xdev(i)) for i in range(1, z.X)]
    for cp in along:
        cp.start()
    for cp in along:
        cp.wait_recv()
    across = []
    for g in w_back:
        for x in range(z.X):
            block = w3s.at[g, :, part(x * 2 + p.c, rq)]
            across.append(net.remote(block, block, p.core()))
            across[-1].start()
    y_out[0].wait_recv()
    hop_a = []
    block = n1s.at[slot_rows(rhi, 1 - p.lo, 1)]
    hop_a = [net.remote(block, block, slot_dev(a, p.lo)) for a in near]
    for cp in hop_a:
        cp.start()
    hop_y = []
    for j, a in enumerate(back):
        a_out[0][j].wait_recv()
        block = n1s.at[slot_rows(a, p.lo, 0)]
        hop_y.append(net.remote(block, block, slot_dev(rhi, 1 - p.lo)))
        hop_y[-1].start()
    for cp in across:
        cp.wait_recv()
    keep_w.wait()
    keep_n.wait()
    for m in range(3):
        if wide:
            for g in range(z.NG):
                w3c[m, :, g * z.cw : (g + 1) * z.cw] = w3s[g, m]
        else:
            w3c[m] = add_refs(*[w3s[g, m] for g in range(z.NG)]).astype(BF16)

    def wo_rows(t):
        return part((t % z.G) * z.NG + t // z.G, z.cw)

    cols = part(p.dp, qc)
    own_o = wos.at[wo_rows(p.t), cols]
    o_out = [net.remote(wo.at[:, cols], own_o, p.hdev(i)) for i in range(1, z.H)]
    o_keep = net.local(wo.at[:, cols], own_o)
    o_hop = [net.remote(own_o, own_o, p.y())]
    for i in range(1, z.H):
        block = wos.at[wo_rows(((p.hi + z.H - i) % z.H) * 2 + p.lo), cols]
        o_hop.append(net.remote(block, block, p.y()))
    block = wos.at[:, cols]
    o_along = [net.remote(block, block, p.xdev(i)) for i in range(1, z.X)]
    o_across = []
    for x in range(z.X):
        block = wos.at[:, part(x * 2 + p.c, qc)]
        o_across.append(net.remote(block, block, p.core()))

    def pieces(h2, lo):
        k, x = h2 * 2 + lo, p.x
        return (
            wgs.at[part(x, rx), part(k, cf)],
            wus.at[part(x, rx), part(k, cf)],
            wds.at[pl.ds(pl.multiple_of(k * cf + x * dx, 16), dx)],
        )

    src = (
        wg.at[part(p.x, rx), part(p.c, cf)],
        wu.at[part(p.x, rx), part(p.c, cf)],
        wd.at[pl.ds(pl.multiple_of(p.c * cf + p.x * dx, 16), dx)],
    )
    h2n = z.H // 2
    h2_back = [(p.h2 + h2n - i) % h2n for i in range(1, h2n)]

    def to(refs, device):
        return [net.remote(ref, ref, device) for ref in refs]

    def all_x(refs):
        return [cp for m in range(1, z.X) for cp in to(refs, p.xdev(m))]

    own_piece = pieces(p.h2, p.lo)
    f_z = [[net.remote(a, b, p.h2dev(i)) for a, b in zip(src, own_piece)] for i in range(1, h2n)]
    f_y = [[net.remote(a, b, p.y()) for a, b in zip(src, own_piece)]]
    f_y += [to(pieces(h2, p.lo), p.y()) for h2 in h2_back]
    f_x = [all_x(pieces(p.h2, 1 - p.lo))]
    f_xz = [all_x(pieces(h2, p.lo)) for h2 in h2_back]
    f_x += [all_x(pieces(h2, 1 - p.lo)) for h2 in h2_back]
    mine = seed.at[p.hl * 2 + p.c]
    other = seed.at[(1 - p.hl) * 2 + p.c]
    s_y, s_core = net.remote(cot, mine, p.pair()), net.remote(cot, mine, p.core())
    s_hop = net.remote(other, other, p.core())

    def start(*copies):
        def f():
            for cp in copies:
                cp.start()
        return f

    def arrive(*copies):
        def f():
            for cp in copies:
                cp.wait_recv()
        return f

    width = q.shape[1]
    pairs, bq = width // 128, min(256, z.rows)
    per = z.rows // bq
    blocks = WIN // bq
    total = pairs * blocks
    steps = {}

    def at(i, *functions):
        steps.setdefault(min(i, total - 1), []).extend(functions)

    at(0, arrive(*f_y[0]), start(*f_x[0]))
    at(1, start(s_core, s_y))
    at(2, *[f for i in range(1, z.H) for f in (arrive(o_out[i - 1]), start(o_hop[i]))])
    for m in range(3):
        for i in range(h2n - 1):
            at(3 + m, arrive(f_z[i][m]), start(f_y[i + 1][m], *f_xz[i][m :: 3]))
    at(6, arrive(*o_hop), start(*o_along))
    at(8, arrive(*o_along), start(*o_across))
    for m in range(3):
        for i in range(1, h2n):
            at(9 + m, arrive(f_y[i][m]), start(*f_x[i][m :: 3]))
    at(13, arrive(s_y), start(s_hop))

    order = slot_order(p, z)

    def project(r):
        rows = part(r, z.rows)
        a = n1s[rows]
        for m, ref in enumerate((q, k, v)):
            y = dot(a, w3c[m])
            for j in range(width // 128):
                t = y[:, j * 128 : j * 128 + 128]
                if m < 2:
                    t = turn(t, cos[rows], sin[rows])
                ref[rows, j * 128 : j * 128 + 128] = t.astype(BF16)

    project(order[0])
    y_out[1].wait_recv()
    o_keep.start()
    for group in [o_out] + f_z + f_y[:1]:
        for cp in group:
            cp.start()
    project(order[1])
    o_keep.wait()
    o_hop[0].start()
    for j in range(half - 1):
        a_out[1][j].wait_recv()
        hop_a[j].wait_recv()
        hop_y[j].wait_recv()
    for r in order[2:]:
        project(r)
    lane_k, lane_q = lane_of(WIN), lane_of(bq)

    m_out = {}
    for j in range(pairs):
        for i in range(1, z.G):
            col = pl.ds(pl.multiple_of(p.r * z.hw + j * 128, 128), 128)
            cp = net.remote(
                mixed.at[part(p.ri(i), z.rows), j * 128 : j * 128 + 128],
                own.at[:, col], p.rdev(i),
            )
            m_out[j, i] = cp
            at(j * blocks + i * per - 1, start(cp))

    def block(i, _):
        j, b = i // blocks, i % blocks
        row = ((p.r + 1 + b // per) % z.G) * z.rows + (b % per) * bq
        col, rows = part(j, 128), pl.ds(pl.multiple_of(row, bq), bq)
        k2, v2, kb, q2 = k[:, col], v[:, col], bias[...], q[rows, col]
        mixes = []
        for e in range(2):
            own_k = (lane_k < HD) if e == 0 else (lane_k >= HD)
            own_q = (lane_q < HD) if e == 0 else (lane_q >= HD)
            k_e = jnp.where(own_k, k2, kb)
            v_e = jnp.where(own_k, v2, jnp.ones_like(v2))
            q_e = jnp.where(own_q, q2, jnp.where(lane_q % HD == 0, 1.0, 0.0).astype(BF16))
            s = dot(q_e, k_e, NT)
            top = jnp.max(s, axis=1, keepdims=True)
            prob = jnp.exp2((s - top) * C2).astype(BF16)
            sums = dot(prob, v_e)
            mixes.append(sums / pltpu.roll(sums, HD, 1))
            norm = jnp.where(own_q, 0.0, top + jnp.log2(jnp.where(own_q, 1.0, sums)) * (1.0 / C2))
            full = jnp.where(own_q, q2.astype(F32), spare_lanes(1.0, norm, lane_q))
            qa[2 * j + e, rows] = full.astype(BF16)
        mix = jnp.where(lane_q < HD, mixes[0], mixes[1])
        o[rows, col] = mix
        mixed[rows, col] = mix.astype(BF16)
        run_at(steps, i)
        return 0

    lax.fori_loop(0, total, block, 0)
    m_keep = net.local(mixed.at[part(p.r, z.rows)], own.at[:, part(p.r, z.hw)])
    m_keep.start()
    for cp in list(m_out.values()) + o_across + [s_core, s_hop]:
        cp.wait_recv()
    for group in f_x + f_xz:
        for cp in group:
            cp.wait_recv()
    m_keep.wait()
    net.wait_sends()


def back_kernel(
    z, gm, qa_h, q_h, k_h, v_h, o_h, w3_h, n1_h, dg, du, dd, do_w, out_pair, bias, cos, sin,
    got, out_got, og, ou, od, ow, oo,
    send, recv, lsem,
    qa, q, k, v, o, do, dq, dk, dv, do_e, dk_sum, dv_sum, w3, n1, part_one, p3,
    rgx, rux, rdx, sg, su, sd, rgy, ruy, rdy, rgz, ruz, rdz,
    oc, so, ox, oy, oz, wc, sw, wx, wgr,
):
    p, net = Place(z), Net(send, recv, lsem)
    d, rows = z.d, z.rows
    rq, rx, dx, cf, h2n = d // z.n_dp, d // z.X, z.cf // z.X, z.cf, z.H // 2
    width = q.shape[1]
    bq = min(512, rows)
    per, blocks, pairs = rows // bq, WIN // bq, width // 128
    total = pairs * blocks
    loads = [net.local(a, b) for a, b in (
        (qa_h, qa), (q_h, q), (k_h, k), (v_h, v), (o_h, o),
        (gm.at[:, part(p.r, z.hw)], do.at[part(p.r, rows)]),
    )]
    late = [net.local(a, b) for a, b in (
        (dd.at[:, part(p.x, dx)], sd), (dg.at[part(p.x, rx)], sg), (du.at[part(p.x, rx)], su),
        *[(do_w.at[:, :, part(x * 2 + p.c, rq)], so.at[x]) for x in range(z.X)],
        (w3_h, w3), (n1_h, n1),
    )]
    for cp in loads + late:
        cp.start()
    meet(
        [p.rdev(i) for i in range(1, z.G)]
        + [p.hdev(i) for i in range(1, z.H)]
        + [p.xdev(i) for i in range(1, z.X)]
        + [p.core()]
    )

    def start(*copies):
        def f():
            for cp in copies:
                cp.start()
        return f

    def arrive(*copies):
        def f():
            for cp in copies:
                cp.wait_recv()
        return f

    steps = {}

    def at(i, *functions):
        steps.setdefault(min(i, total - 1), []).extend(functions)

    dest = do.at[part(p.r, rows)]
    a_out = [net.remote(gm.at[:, part(p.ri(i), z.hw)], dest, p.rdev(i)) for i in range(1, z.G)]
    for cp in a_out:
        cp.start()
    def spot(h2, lo):
        return h2 * 2 + lo

    bufs = ((dd, rdx, sd, rdy, rdz, od), (dg, rgx, sg, rgy, rgz, og), (du, rux, su, ruy, ruz, ou))

    def rows_of(m, ref, x):
        return ref.at[:, part(x, dx)] if m == 0 else ref.at[part(x, rx)]

    def piece(m, ref, s):
        return ref.at[s] if m == 0 else ref.at[:, part(s, cf)]

    fx = [[net.remote(rows_of(m, bufs[m][0], p.xi(i)), bufs[m][1].at[i - 1], p.xdev(i))
           for i in range(1, z.X)] for m in range(3)]
    fy = [[net.remote(piece(m, bufs[m][2], spot(h2, 1 - p.lo)), bufs[m][3].at[h2], p.y())
           for h2 in range(h2n)] for m in range(3)]
    fz = [[net.remote(piece(m, bufs[m][2], spot((p.h2 + i) % h2n, p.lo)), bufs[m][4].at[i - 1],
                      p.h2dev(i)) for i in range(1, h2n)] for m in range(3)]
    done_at = [
        (pl.ds(pl.multiple_of(p.c * cf + p.x * dx, 16), dx),),
        (part(p.x, rx), part(p.c, cf)),
        (part(p.x, rx), part(p.c, cf)),
    ]
    fa, fc = [], []
    for m in range(3):
        block = bufs[m][5].at[done_at[m]]
        fa.append([net.remote(block, block, p.xdev(i)) for i in range(1, z.X)])
        block = od.at[part(p.c, cf)] if m == 0 else bufs[m][5].at[:, part(p.c, cf)]
        fc.append(net.remote(block, block, p.core()))

    def ffn_x(m):
        def f():
            arrive(*fx[m])()
            late[m].wait()
            got_x, own = bufs[m][1], bufs[m][2]
            for h in range(2 * h2n):
                if m == 0:
                    own[h] = add_refs(own[h], *[got_x[i, h] for i in range(z.X - 1)]).astype(BF16)
                else:
                    c = pl.ds(h * cf, cf)
                    own[:, c] = add_refs(
                        own[:, c], *[got_x[i, :, c] for i in range(z.X - 1)]
                    ).astype(BF16)
            start(*fy[m])()
        return f

    def ffn_y(m):
        def f():
            arrive(*fy[m])()
            own, got_y = bufs[m][2], bufs[m][3]
            for h2 in range(h2n):
                if m == 0:
                    own[spot(h2, p.lo)] = add_refs(own[spot(h2, p.lo)], got_y[h2]).astype(BF16)
                else:
                    c = part(spot(h2, p.lo), cf)
                    own[:, c] = add_refs(own[:, c], got_y[h2]).astype(BF16)
            start(*fz[m])()
        return f

    def ffn_z(m):
        def f():
            arrive(*fz[m])()
            own, got_z, out = bufs[m][2], bufs[m][4], bufs[m][5]
            s = spot(p.h2, p.lo)
            mine = own[s] if m == 0 else own[:, part(s, cf)]
            out[done_at[m]] = add_refs(mine, *[got_z[i] for i in range(h2n - 1)]).astype(BF16)
            start(*fa[m])()
        return f

    def ffn_c(m):
        def f():
            arrive(*fa[m])()
            fc[m].start()
        return f

    half = z.G // 2
    c_out = [net.remote(do_w.at[:, :, part(p.xi(i) * 2 + 1 - p.c, rq)], oc.at[i], p.core())
             for i in range(z.X)]
    c_x = [net.remote(so.at[p.xi(i)], ox.at[i - 1], p.xdev(i)) for i in range(1, z.X)]
    c_y = [net.remote(so.at[p.x, i * 2 + 1 - p.lo], oy.at[i], p.y()) for i in range(half)]
    c_z = [net.remote(so.at[p.x, (p.hii(i) % half) * 2 + p.lo, part(p.hii(i) // half, z.cw)],
                      oz.at[i - 1], p.hdev(i)) for i in range(1, z.H)]
    cols = part(p.dp, rq)
    block = oo.at[:, cols]
    c_a = [net.remote(block, block, p.xdev(i)) for i in range(1, z.X)]
    c_c = []
    for x in range(z.X):
        block = oo.at[:, part(x * 2 + p.c, rq)]
        c_c.append(net.remote(block, block, p.core()))

    def wo_c():
        for cp in late[3 : 3 + z.X]:
            cp.wait()
        for i in list(range(1, z.X)) + [0]:
            c_out[i].wait_recv()
            for r in range(z.G):
                so[p.xi(i), r] = add_refs(so[p.xi(i), r], oc[i, r]).astype(BF16)
        start(*c_x)()

    def wo_x():
        arrive(*c_x)()
        for r in range(z.G):
            so[p.x, r] = add_refs(so[p.x, r], *[ox[i, r] for i in range(z.X - 1)]).astype(BF16)
        start(*c_y)()

    def wo_y():
        arrive(*c_y)()
        for i in range(half):
            r = i * 2 + p.lo
            so[p.x, r] = add_refs(so[p.x, r], oy[i]).astype(BF16)
        start(*c_z)()

    def wo_z():
        arrive(*c_z)()
        mine = so[p.x, (p.hi % half) * 2 + p.lo, part(p.hi // half, z.cw)]
        oo[:, cols] = add_refs(mine, *[oz[i] for i in range(z.H - 1)]).astype(BF16)
        start(*c_a)()

    def wo_a():
        arrive(*c_a)()
        start(*c_c)()

    o_send = net.remote(out_pair, out_got, p.pair())
    start(*fx[0], *c_out)()
    at(0, wo_c, start(*fx[1]))
    at(1, start(o_send))
    at(2, ffn_x(0), wo_x)
    at(3, start(*fx[2]))
    at(4, ffn_y(0), wo_y)
    at(5, ffn_x(1), wo_z)
    at(6, ffn_z(0), wo_a)
    at(7, ffn_y(1), ffn_c(0))

    for cp in loads:
        cp.wait()
    lane_q, sub = lane_of(bq), 1024
    lane_k = lane_of(sub)
    s64 = lane_k % HD
    ones3 = jnp.where((s64 >= 1) & (s64 <= 3), 1.0, 0.0).astype(BF16)

    def block_step(i, _):
        j, b = i // blocks, i % blocks
        for n in range(1, z.G):

            @pl.when((j == 0) & (b == n * per))
            def _():
                a_out[z.G - 1 - n].wait_recv()

        row = ((p.r + b // per) % z.G) * rows + (b % per) * bq
        col, at_q = part(j, 128), pl.ds(pl.multiple_of(row, bq), bq)
        q2, do2 = q[at_q, col], do[at_q, col]
        prod = do2.astype(F32) * o[at_q, col]
        for e in range(2):
            own_q = (lane_q < HD) if e == 0 else (lane_q >= HD)
            delta = jnp.sum(jnp.where(own_q, prod, 0.0), axis=1, keepdims=True)
            spare = spare_lanes(0.0, jnp.broadcast_to(delta, prod.shape), lane_q)
            do_e[e] = jnp.where(own_q, do2.astype(F32), spare).astype(BF16)
        dqs = [jnp.zeros((bq, 128), F32)] * 2
        for s in range(WIN // sub):
            keys = pl.ds(s * sub, sub)
            k2, v2 = k[keys, col], v[keys, col]
            kb = bias[keys] + ones3
            dks, dvs = [], []
            for e in range(2):
                own_k = (lane_k < HD) if e == 0 else (lane_k >= HD)
                k_e = jnp.where(own_k, k2, kb)
                v_e = jnp.where(own_k, v2, ones3)
                prob = jnp.exp2(dot(k_e, qa[2 * j + e, at_q], NT) * C2)
                ds = (prob * dot(v_e, do_e[e], NT)).astype(BF16)
                dvs.append(dot(prob.astype(BF16), do2))
                dks.append(dot(ds, q2))
                dqs[e] = dqs[e] + dot(ds, k2, TN)
            dv_new = jnp.where(lane_k < HD, dvs[0], dvs[1])
            dk_new = jnp.where(lane_k < HD, dks[0], dks[1])

            @pl.when(b == 0)
            def _():
                dv_sum[keys] = dv_new
                dk_sum[keys] = dk_new

            @pl.when(b > 0)
            def _():
                dv_sum[keys] += dv_new
                dk_sum[keys] += dk_new

        dq_new = jnp.where(lane_q < HD, dqs[0], dqs[1]) * SCALE
        dq[at_q, col] = turn(dq_new, cos[at_q], -sin[at_q]).astype(BF16)

        @pl.when(b == blocks - 1)
        def _():
            dv[:, col] = dv_sum[...].astype(BF16)
            dk[:, col] = turn(dk_sum[...] * SCALE, cos[...], -sin[...]).astype(BF16)

        run_at(steps, i)
        return 0

    lax.fori_loop(0, total, block_step, 0)

    for cp in late[3 + z.X :]:
        cp.wait()
    r_out = []
    for i in list(range(1, z.G)) + [0]:
        here = part(p.ri(i), rows)
        part_one[here] = (
            dot(dq[here], w3[0], NT) + dot(dk[here], w3[1], NT) + dot(dv[here], w3[2], NT)
        ).astype(BF16)
        if i:
            r_out.append(net.remote(part_one.at[here], got.at[i - 1], p.rdev(i)))
            r_out[-1].start()
    r_keep = net.local(part_one.at[part(p.r, rows)], got.at[z.G - 1])
    r_keep.start()
    for m, t in enumerate((dq, dk, dv)):
        y = dot(n1[...], t[...], TN).astype(BF16)
        for g in range(z.NG):
            p3[g, m] = y[:, g * z.cw : (g + 1) * z.cw]
    w_c = [net.remote(p3.at[:, :, part(p.xi(i) * 2 + 1 - p.c, rq)], wc.at[i], p.core())
           for i in range(z.X)]
    start(*w_c)()
    ffn_x(2)()
    w_x = []
    for i in list(range(1, z.X)) + [0]:
        w_c[i].wait_recv()
        for g in range(z.NG):
            sw[i, g] = add_refs(p3[g, :, part(p.xi(i) * 2 + p.c, rq)], wc[i, g]).astype(BF16)
        if i:
            w_x.append(net.remote(sw.at[i], wx.at[i - 1], p.xdev(i)))
            w_x[-1].start()
    ffn_z(1)()
    arrive(*w_x)()
    for g in range(z.NG):
        sw[0, g] = add_refs(sw[0, g], *[wx[i, g] for i in range(z.X - 1)]).astype(BF16)
    w_g = [net.remote(sw.at[0, p.gi(i)], wgr.at[i - 1], p.gdev(i)) for i in range(1, z.NG)]
    start(*w_g)()
    ffn_y(2)()
    ffn_c(1)()
    arrive(*w_g)()
    quarter = part(p.dp, rq)
    for m in range(3):
        ow[m, quarter] = add_refs(
            sw[0, p.g, m], *[wgr[i, m] for i in range(z.NG - 1)]
        ).astype(BF16)
    block = ow.at[:, quarter]
    w_a = [net.remote(block, block, p.xdev(i)) for i in range(1, z.X)]
    start(*w_a)()
    ffn_z(2)()
    arrive(*w_a)()
    w_last = []
    for x in range(z.X):
        block = ow.at[:, part(x * 2 + p.c, rq)]
        w_last.append(net.remote(block, block, p.core()))
        w_last[-1].start()
    ffn_c(2)()
    arrive(*c_c, *fc, *w_last, o_send, *r_out)()
    r_keep.wait()
    net.wait_sends()


def sum_norms_kernel(z, own, out, send, recv, lsem, far, near):
    p, net = Place(z), Net(send, recv, lsem)
    t_dev = [(p.dp, (p.t + i) % z.n_t) for i in range(1, z.n_t)]
    d_dev = [((p.dp + i) % z.n_dp, p.t) for i in range(1, z.n_dp)]
    meet(t_dev + d_dev)
    first = [net.remote(own, far.at[p.t], dev) for dev in t_dev]
    for cp in first:
        cp.start()
    far[p.t] = own[...]
    for cp in first:
        cp.wait_recv()
    near[p.dp] = add_refs(*[far[i] for i in range(z.n_t)])
    second = [net.remote(near.at[p.dp], near.at[p.dp], dev) for dev in d_dev]
    for cp in second:
        cp.start()
    for cp in second:
        cp.wait_recv()
    out[...] = add_refs(*[near[i] for i in range(z.n_dp)])
    net.wait_sends()


def norm_stats(v):
    centre = v - jnp.mean(v, axis=-1, keepdims=True)
    inverse = lax.rsqrt(jnp.mean(centre * centre, axis=-1, keepdims=True) + EPSILON)
    return centre * inverse, inverse


def norm_backward(grad_in, scaled, inverse, gain):
    weighted = grad_in * gain
    first_mean = jnp.mean(weighted, axis=-1, keepdims=True)
    second_mean = jnp.mean(weighted * scaled, axis=-1, keepdims=True)
    return inverse * (weighted - first_mean - scaled * second_mean)


def per_device(
    n_dp, n_t, tokens, lengths, ln1_gain, ln1_bias, w_query, w_key, w_value, w_out,
    ln2_gain, ln2_bias, w_gate, w_up, w_down, cotangent,
):
    rows, d = tokens.shape
    cw, cfull = w_query.shape[1], w_gate.shape[1]
    z = Sizes(n_dp, n_t, rows, d, cw, cfull)
    G, NG, H, X, hw, cf = z.G, z.NG, z.H, z.X, z.hw, z.cf
    rq, rx, dx = d // n_dp, d // X, cf // X
    slot = lax.axis_index("tensor") // G
    length = lax.dynamic_index_in_dim(lengths, slot, keepdims=False)
    lane = lax.broadcasted_iota(jnp.int32, (WIN, 128), 1) % HD
    place = lax.broadcasted_iota(jnp.int32, (WIN, 128), 0)
    bias = jnp.where((lane == 0) & (place >= length), -1e30, 0.0).astype(BF16)
    cos, sin = (jnp.asarray(t, F32) for t in rope_tables())

    own_tokens = tokens.astype(F32)
    scaled_one, inverse_one = norm_stats(own_tokens)
    normed_one = (scaled_one * ln1_gain + ln1_bias).astype(BF16)
    w_three = jnp.stack([w_query, w_key, w_value])
    if cw % 128:
        wider = jnp.zeros((3, d, hw), BF16)
        w_three = lax.dynamic_update_slice(wider, w_three, (0, 0, slot * cw))
    n1, w3, q, k, v, o, qa, mixed_own, wo, wg, wu, wd, seed = comm_call(
        front_kernel, z, "front", 1,
        (
            shape((WIN, d)), shape((3, d, hw)), shape((WIN, hw)), shape((WIN, hw)),
            shape((WIN, hw)), shape((WIN, hw), F32), shape((hw // HD, WIN, 128)),
            shape((rows, d)), shape((d, d)), shape((d, H * cf)), shape((d, H * cf)),
            shape((H * cf, d)), shape((4, rows, d)),
        ),
        [HBM, HBM, VMEM, VMEM, VMEM] + [HBM] * 5,
        [VMEM] * 9 + [HBM] * 4,
        [pltpu.VMEM((NG,) + w_three.shape, BF16), pltpu.VMEM((WIN, hw), BF16)],
        n=160, vmem=60 * MIB,
    )(normed_one, w_three, cos, sin, bias, w_out, w_gate, w_up, w_down, cotangent)
    every = 4 * rows
    width = H * cf
    mid_out = (
        shape((rows, d), F32), shape((rows, d)), shape((rows, d), F32), shape((rows, d)),
        shape((d, d)), shape((d, width)), shape((d, width)), shape((width, d)), shape((2, d), F32),
    )
    out_part, out_pair, grad_middle, grad_mixed, p_wo, p_gate, p_up, p_down, sums_two = comm_call(
        middle_kernel, z, "middle", 4, mid_out,
        [HBM] * 11 + [VMEM] * 2, [HBM] * 8 + [VMEM],
        [
            pltpu.VMEM((rows, d), BF16), pltpu.VMEM((rows, d), BF16), pltpu.VMEM((d, d), BF16),
            pltpu.VMEM((d, width), BF16), pltpu.VMEM((d, width), BF16),
            pltpu.VMEM((width, d), BF16), pltpu.VMEM((every, d), BF16),
            pltpu.VMEM((every, d), BF16), pltpu.VMEM((rows, d), F32),
            pltpu.VMEM((every, width), BF16), pltpu.VMEM((every, width), BF16),
            pltpu.VMEM((every, width), BF16), pltpu.VMEM((every, d), BF16),
            pltpu.VMEM((every, d), BF16), pltpu.VMEM((2, 2, rows, d), BF16),
            pltpu.VMEM((rows, d), BF16), pltpu.VMEM((2, rows, d), BF16),
            pltpu.VMEM((rows, d), F32),
        ],
        vmem=60 * MIB,
    )(
        mixed_own, tokens, wo, wg, wu, wd, w_gate, w_up, w_down, seed.reshape(every, d), cotangent,
        ln2_gain.reshape(1, d), ln2_bias.reshape(1, d),
    )
    gain_two, bias_two = sums_two[0], sums_two[1]
    p_wo = p_wo.reshape(G, hw, d)
    p_down = p_down.reshape(H, cf, d)
    V = pltpu.VMEM
    pieces = ((rx, cf), (rx, cf), (dx, d))
    got, out_got, g_gate, g_up, g_down, g_w3, g_wo = comm_call(
        back_kernel, z, "back", 8,
        (
            shape((G, rows, d)), shape((rows, d)), shape((d, 2 * cf)), shape((d, 2 * cf)),
            shape((2 * cf, d)), shape((3, d, cw)), shape((cw, d)),
        ),
        [HBM] * 13 + [VMEM] * 3, [HBM] * 2 + [VMEM] * 5,
        [
            V((hw // HD, WIN, 128), BF16), V((WIN, hw), BF16), V((WIN, hw), BF16),
            V((WIN, hw), BF16), V((WIN, hw), F32), V((WIN, hw), BF16), V((WIN, hw), BF16),
            V((WIN, hw), BF16), V((WIN, hw), BF16), V((2, min(512, rows), 128), BF16),
            V((WIN, 128), F32), V((WIN, 128), F32), V((3, d, hw), BF16), V((WIN, d), BF16),
            V((WIN, d), BF16), V((NG, 3, d, cw), BF16),
            V((X - 1, rx, width), BF16), V((X - 1, rx, width), BF16), V((X - 1, H, dx, d), BF16),
            V((rx, width), BF16), V((rx, width), BF16), V((H, dx, d), BF16),
            *[V((H // 2,) + dims, BF16) for dims in pieces],
            *[V((H // 2 - 1,) + dims, BF16) for dims in pieces],
            V((X, G, hw, rq), BF16), V((X, G, hw, rq), BF16), V((X - 1, G, hw, rq), BF16),
            V((G // 2, hw, rq), BF16), V((H - 1, cw, rq), BF16),
            V((X, NG, 3, rq, cw), BF16), V((X, NG, 3, rq, cw), BF16),
            V((X - 1, NG, 3, rq, cw), BF16), V((NG - 1, 3, rq, cw), BF16),
        ],
        n=160, vmem=62 * MIB,
    )(
        grad_mixed, qa, q, k, v, o, w3, n1, p_gate, p_up, p_down, p_wo, out_pair, bias, cos, sin,
    )
    output = (out_part + out_got.astype(F32)).astype(BF16)
    grad_one = jnp.sum(got.astype(F32), axis=0)
    gain_one = jnp.sum(grad_one * scaled_one, axis=0)
    bias_one = jnp.sum(grad_one, axis=0)
    back_one = norm_backward(grad_one, scaled_one, inverse_one, ln1_gain)
    grad_tokens = (grad_middle + back_one).astype(BF16)
    norms = comm_call(
        sum_norms_kernel, z, "sum_norms", 9, shape((4, d), F32), [VMEM], VMEM,
        [V((n_t, 4, d), F32), V((n_dp, 4, d), F32)],
    )(jnp.stack([gain_one, bias_one, gain_two, bias_two]))
    return (
        output, grad_tokens, norms[0], norms[1],
        g_w3[0].astype(F32), g_w3[1].astype(F32), g_w3[2].astype(F32), g_wo.astype(F32),
        norms[2], norms[3], g_gate.astype(F32), g_up.astype(F32), g_down.astype(F32),
    )


def solution(mesh):
    rows, cols, each = P(("dp", "tensor"), None), P(None, "tensor"), P("tensor", None)
    return jax.shard_map(
        functools.partial(per_device, mesh.shape["dp"], mesh.shape["tensor"]),
        mesh=mesh,
        in_specs=(
            rows, P("dp"), P(), P(), cols, cols, cols, each, P(), P(), cols, cols, each, rows,
        ),
        out_specs=(
            rows, rows, P(), P(), cols, cols, cols, each, P(), P(), cols, cols, each,
        ),
        check_vma=False,
    )
```

```python
import functools

import jax
import jax.numpy as jnp
import numpy as np
from jax import lax
from jax.experimental import pallas as pl
from jax.experimental.pallas import tpu as pltpu
from jax.sharding import PartitionSpec as P

HD = 64
WIN = 2048
EPSILON = 1e-05
SCALE = HD ** (-0.5)
LOG2E = 1.4426950408889634
C2 = SCALE * LOG2E
NT = (((1,), (1,)), ((), ()))
NN = (((1,), (0,)), ((), ()))
TN = (((0,), (0,)), ((), ()))
MESH = pl.DeviceIdType.MESH
F32 = jnp.float32
BF16 = jnp.bfloat16
MIB = 1024 * 1024
HBM = pl.BlockSpec(memory_space=pl.ANY)
VMEM = pl.BlockSpec(memory_space=pltpu.VMEM)


def dot(a, b, dims=NN):
    return lax.dot_general(a, b, dims, preferred_element_type=F32)


def shape(dims, kind=BF16):
    return jax.ShapeDtypeStruct(dims, kind)


class Sizes:
    def __init__(self, n_dp, n_t, rows, d, cw, cfull):
        self.n_dp, self.n_t, self.rows, self.d = n_dp, n_t, rows, d
        self.X, self.H = n_dp // 2, n_t // 2
        self.G = WIN // rows
        self.NG = n_t // self.G
        self.cw, self.hw = cw, self.NG * cw
        self.cf = cfull // 2


class Place:
    def __init__(self, z):
        self.z = z
        dp, t = lax.axis_index("dp"), lax.axis_index("tensor")
        self.dp, self.t = dp, t
        self.x, self.c = dp // 2, dp % 2
        self.hi, self.lo = t // 2, t % 2
        self.g, self.r = t // z.G, t % z.G
        self.h2, self.hl = self.hi // 2, self.hi % 2

    def pair(self):
        return (self.dp, (self.h2 * 2 + 1 - self.hl) * 2 + self.lo)

    def h2dev(self, i):
        return (self.dp, (((self.h2 + i) % (self.z.H // 2)) * 2 + self.hl) * 2 + self.lo)

    def core(self):
        return (self.x * 2 + 1 - self.c, self.t)

    def y(self):
        return (self.dp, self.hi * 2 + 1 - self.lo)

    def xi(self, i):
        return (self.x + i) % self.z.X

    def xdev(self, i):
        return (self.xi(i) * 2 + self.c, self.t)

    def hii(self, i):
        return (self.hi + i) % self.z.H

    def hdev(self, i):
        return (self.dp, self.hii(i) * 2 + self.lo)

    def ri(self, i):
        return (self.r + i) % self.z.G

    def rdev(self, i):
        return (self.dp, self.g * self.z.G + self.ri(i))

    def gi(self, i):
        return (self.g + i) % self.z.NG

    def gdev(self, i):
        return (self.dp, self.gi(i) * self.z.G + self.r)


class Net:
    def __init__(self, send, recv, local=None):
        self.send, self.recv, self.local_sem = send, recv, local
        self.count, self.local_count = 0, 0
        self.all = []

    def remote(self, src, dst, device):
        k = self.count
        self.count += 1
        cp = pltpu.make_async_remote_copy(
            src_ref=src, dst_ref=dst, send_sem=self.send.at[k], recv_sem=self.recv.at[k],
            device_id=device, device_id_type=MESH,
        )
        self.all.append(cp)
        return cp

    def local(self, src, dst):
        k = self.local_count
        self.local_count += 1
        return pltpu.make_async_copy(src, dst, self.local_sem.at[k])

    def wait_sends(self):
        for cp in self.all:
            cp.wait_send()


def meet(devices):
    barrier = pltpu.get_barrier_semaphore()
    for device in devices:
        pl.semaphore_signal(barrier, inc=1, device_id=device, device_id_type=MESH)
    pl.semaphore_wait(barrier, len(devices))


def part(i, n):
    return pl.ds(pl.multiple_of(i * n, n), n)


def comm_call(body, z, name, cid, out_shape, in_specs, out_specs, scratch=(), n=64, vmem=None):
    return pl.pallas_call(
        functools.partial(body, z),
        out_shape=out_shape,
        in_specs=in_specs,
        out_specs=out_specs,
        scratch_shapes=[
            pltpu.SemaphoreType.DMA((n,)),
            pltpu.SemaphoreType.DMA((n,)),
            pltpu.SemaphoreType.DMA((64,)),
            *scratch,
        ],
        compiler_params=pltpu.CompilerParams(
            collective_id=cid, has_side_effects=True, vmem_limit_bytes=vmem
        ),
        name=name,
    )


def middle_kernel(
    z, own_h, tok_h, wo_h, wg_h, wu_h, wd_h, wg_o, wu_o, wd_o, seed_h, cot, gain, beta,
    out_part, out_pair, grad_mid, grad_mix, p_wo, p_gate, p_up, p_down, sums,
    send, recv, lsem,
    own, tok, wo, wg, wu, wd, seed, n2, middle, hidden, gg, gu, two, one, rc, ry, tot, out_f, rdx,
):
    p, net = Place(z), Net(send, recv, lsem)
    rows, d = z.rows, z.d
    cf, f_x = z.cf, []
    pairs = [(own_h, own), (wo_h, wo), (tok_h, tok)]
    for k in range(z.H):
        at = pl.ds(k * cf, cf)
        if k == 0:
            half = part(p.c, cf)
            pairs += [(wg_o.at[:, half], wg.at[:, at]), (wu_o.at[:, half], wu.at[:, at]),
                      (wd_o.at[half], wd.at[at])]
        elif k <= z.H // 2:
            pairs += [(wg_h.at[:, at], wg.at[:, at]), (wu_h.at[:, at], wu.at[:, at]),
                      (wd_h.at[at], wd.at[at])]
        else:
            up = part(p.x, d // z.X)
            down = pl.ds(pl.multiple_of(k * cf + p.x * (cf // z.X), 16), cf // z.X)
            some = [(wg_h.at[up, at], wg.at[up, at]), (wu_h.at[up, at], wu.at[up, at]),
                    (wd_h.at[down], wd.at[down])]
            pairs += some
            f_x += [net.remote(a, b, p.xdev(i)) for i in range(1, z.X) for a, b in some]
    for k, b in enumerate((p.hl * 2 + p.c, p.hl * 2 + 1 - p.c,
                           (1 - p.hl) * 2 + p.c, (1 - p.hl) * 2 + 1 - p.c)):
        at = part(b, rows)
        pairs.append((seed_h.at[at] if k else cot, seed.at[at]))
    loads = [net.local(a, b) for a, b in pairs]
    for cp in loads:
        cp.start()
    meet([p.pair(), p.core()] + [p.xdev(i) for i in range(1, z.X)])
    for cp in f_x:
        cp.start()
    chunk = 128
    blocks = [p.hl * 2 + p.c, p.hl * 2 + 1 - p.c,
              (1 - p.hl) * 2 + 1 - p.c, (1 - p.hl) * 2 + p.c]

    def block_rows(b):
        return pl.ds(pl.multiple_of(b * rows, rows), rows)

    for cp in loads[:3]:
        cp.wait()

    def norm(i, _):
        at = part(i, chunk)
        m = tok[at].astype(F32) + dot(own[at], wo[...])
        middle[at] = m
        scaled, _ = norm_stats(m)
        here = pl.ds(pl.multiple_of(blocks[0] * rows + i * chunk, chunk), chunk)
        n2[here] = (scaled * gain[...] + beta[...]).astype(BF16)
        return 0

    sub = rows // 2
    n_pair, n_core, n_hop = [], [], []
    for h in range(2):
        lax.fori_loop(h * (sub // chunk), (h + 1) * (sub // chunk), norm, 0)
        mine, far = [
            n2.at[pl.ds(pl.multiple_of(blocks[i] * rows + h * sub, sub), sub)] for i in (0, 3)
        ]
        n_pair.append(net.remote(mine, mine, p.pair()))
        n_core.append(net.remote(mine, mine, p.core()))
        n_hop.append(net.remote(far, far, p.core()))
        n_pair[h].start()
        n_core[h].start()
    for cp in loads[3:]:
        cp.wait()
    early, every = (z.H // 2 + 1) * cf, z.H * cf

    def sub_rows(b, i):
        return pl.ds(pl.multiple_of(b * rows + i * sub, sub), sub)

    def grads(b, low, high):
        cols = pl.ds(low, high - low)

        def body(i, _):
            at = sub_rows(b, i)
            a, e = n2[at], seed[at]
            gate, up = dot(a, wg[:, cols]), dot(a, wu[:, cols])
            sig = jax.nn.sigmoid(gate)
            silu = gate * sig
            hidden[at, cols] = (silu * up).astype(BF16)
            gh = dot(e, wd[cols], NT)
            gg[at, cols] = (gh * up * sig * (1.0 + gate * (1.0 - sig))).astype(BF16)
            gu[at, cols] = (gh * silu).astype(BF16)
            return 0

        lax.fori_loop(0, rows // sub, body, 0)

    def back_rows(b, i):
        at = sub_rows(b, i)
        two[at] = (dot(gg[at], wg[...], NT) + dot(gu[at], wu[...], NT)).astype(BF16)

    def out_rows(b, i):
        at = sub_rows(b, i)
        one[at] = dot(hidden[at], wd[...]).astype(BF16)

    def send_core(k, b, far):
        ref = (two, one)[k]
        cp = net.remote(ref.at[block_rows(b)], rc.at[k, far], p.core())
        cp.start()
        return cp

    grads(blocks[0], 0, early)
    for cp in n_core:
        cp.wait_recv()
    grads(blocks[1], 0, early)
    for cp in f_x:
        cp.wait_recv()
    for b in blocks[:2]:
        grads(b, early, every)

        def both(i, _):
            back_rows(b, i)
            out_rows(b, i)
            return 0

        lax.fori_loop(0, 2, both, 0)
    near = [send_core(k, blocks[1], 0) for k in range(2)]
    for h in range(2):
        n_pair[h].wait_recv()
        n_hop[h].start()
    for cp in n_hop:
        cp.wait_recv()
    grads(blocks[2], 0, every)
    back_rows(blocks[2], 0)
    back_rows(blocks[2], 1)
    away = [send_core(0, blocks[2], 1)]
    grads(blocks[3], 0, every)
    away[0].wait_recv()
    to_pair = []
    for i in range(2):
        back_rows(blocks[3], i)
        at = pl.ds(i * sub, sub)
        tot[0, at] = add_refs(two[sub_rows(blocks[3], i)], rc[0, 1, at]).astype(BF16)
        to_pair.append(net.remote(tot.at[0, at], ry.at[at], p.pair()))
        to_pair[i].start()
    out_rows(blocks[2], 0)
    out_rows(blocks[2], 1)
    away.append(send_core(1, blocks[2], 1))
    out_rows(blocks[3], 0)
    out_rows(blocks[3], 1)
    away[1].wait_recv()
    tot[1] = add_refs(one[block_rows(blocks[3])], rc[1, 1]).astype(BF16)
    d_x, dx = [], cf // z.X
    stores = []
    for a, b, into, out in ((hidden, seed, wd, p_down), (n2, gg, wg, p_gate), (n2, gu, wu, p_up)):
        for i in range(into.shape[0] // 256):
            at = pl.ds(i * 256, 256)
            into[at] = dot(a[:, at], b[...], TN).astype(BF16)
        if into is wd:
            for i in range(1, z.X):
                for h in range(z.H):
                    far = pl.ds(pl.multiple_of(h * cf + p.xi(i) * dx, 16), dx)
                    d_x.append(net.remote(wd.at[far], rdx.at[i - 1, h], p.xdev(i)))
                    d_x[-1].start()
            continue
        stores.append(net.local(into, out))
        stores[-1].start()
    near[0].wait_recv()
    for cp in to_pair:
        cp.wait_recv()

    def back(i, carry):
        at = part(i, chunk)
        here = pl.ds(pl.multiple_of(blocks[0] * rows + i * chunk, chunk), chunk)
        scaled, inverse = norm_stats(middle[at])
        e = add_refs(two[here], rc[0, 0, at], ry[at])
        m = seed[here].astype(F32) + norm_backward(e, scaled, inverse, gain[...])
        out_f[at] = add_refs(middle[at], one[here], rc[1, 0, at])
        middle[at] = m
        tok[at] = m.astype(BF16)
        return (
            carry[0] + jnp.sum(e * scaled, axis=0, keepdims=True),
            carry[1] + jnp.sum(e, axis=0, keepdims=True),
        )

    near[1].wait_recv()
    zero = jnp.zeros((1, d), F32)
    a, b = lax.fori_loop(0, rows // chunk, back, (zero, zero))
    sums[0:1] = a
    sums[1:2] = b
    net.wait_sends()
    for i in range(d // 256):
        at = pl.ds(i * 256, 256)
        n2[at] = dot(own[:, at], tok[...], TN).astype(BF16)
    for h in range(z.H):
        mine = pl.ds(pl.multiple_of(h * cf + p.x * dx, 16), dx)
        for i in range(1, z.X):
            d_x[(i - 1) * z.H + h].wait_recv()
        wd[mine] = add_refs(wd[mine], *[rdx[i, h] for i in range(z.X - 1)]).astype(BF16)
        stores.append(net.local(wd.at[mine], p_down.at[h]))
        stores[-1].start()
    before = len(stores)
    stores.append(net.local(n2.at[pl.ds(0, d)], p_wo))
    stores.append(net.local(out_f, out_part))
    stores.append(net.local(tot.at[1], out_pair))
    stores.append(net.local(middle, grad_mid))
    for cp in stores[before:]:
        cp.start()
    mixed_at = pl.ds(0, rows)
    two[mixed_at] = dot(tok[...], wo[...], NT).astype(BF16)
    last = net.local(two.at[mixed_at], grad_mix)
    last.start()
    for cp in stores + [last]:
        cp.wait()


def add_refs(*values):
    total = values[0].astype(F32)
    for v in values[1:]:
        total = total + v.astype(F32)
    return total


def lane_of(rows):
    return lax.broadcasted_iota(jnp.int32, (rows, 128), 1)


def rope_tables():
    frequency = np.float32(10000.0) ** (-np.arange(HD // 2, dtype=np.float32) * 2.0 / HD)
    angles = np.arange(WIN, dtype=np.float32)[:, None] * frequency.astype(np.float32)[None, :]
    angles = np.concatenate([angles] * 4, axis=1)
    return np.cos(angles), np.sin(angles)


def turn(v, cosines, sines):
    swapped = jnp.where(
        lane_of(v.shape[0]) % HD < HD // 2, -pltpu.roll(v, 96, 1), pltpu.roll(v, 32, 1)
    )
    return v * cosines + swapped * sines


def spare_lanes(first, v, lane):
    high = v.astype(BF16)
    rest = v - high.astype(F32)
    middle = rest.astype(BF16)
    low = (rest - middle.astype(F32)).astype(BF16)
    s = lane % HD
    tail = jnp.where(s == 2, -middle.astype(F32), jnp.where(s == 3, -low.astype(F32), 0.0))
    return jnp.where(s == 0, first, jnp.where(s == 1, -high.astype(F32), tail))


def run_at(steps, i):
    for at, functions in sorted(steps.items()):

        @pl.when(i == at)
        def _(functions=functions):
            for f in functions:
                f()


def slot_order(p, z):
    half = z.G // 2
    rhi = p.r // 2
    order = [(rhi, p.lo), (rhi, 1 - p.lo)]
    for j in range(1, half):
        order += [((rhi + j) % half, p.lo), ((rhi + j) % half, 1 - p.lo)]
    return [a * 2 + b for a, b in order]


def front_kernel(
    z, tok, gain, beta, w3, cos, sin, bias, wo, wg, wu, wd, cot,
    n1_o, w3_o, q_o, k_o, v_o, o, qa, own, wos, wgs, wus, wds, seed,
    send, recv, lsem, w3s, mixed, n1s, w3c, q, k, v, n1,
):
    p, net = Place(z), Net(send, recv, lsem)
    rq, qc = z.d // z.n_dp, z.d // z.n_dp
    rx, dx, cf = z.d // z.X, z.cf // z.X, z.cf
    half, wide = z.G // 2, z.cw % 128 == 0
    rhi = p.r // 2
    hr = z.rows // 2

    def slot_dev(a, b):
        return (p.dp, p.g * z.G + a * 2 + b)

    def slot_rows(a, b, top):
        return pl.ds(pl.multiple_of((a * 2 + b) * z.rows + top * hr, 16), hr)

    def norm(i, _):
        at = part(i, 128)
        scaled, _ = norm_stats(tok[at].astype(F32))
        n1[at] = (scaled * gain[...] + beta[...]).astype(BF16)
        return 0

    lax.fori_loop(0, z.rows // 128, norm, 0)
    near = [((rhi + j) % half) for j in range(1, half)]
    back = [((rhi + half - j) % half) for j in range(1, half)]
    meet(
        [slot_dev(rhi, 1 - p.lo)]
        + [slot_dev(a, 1 - p.lo) for a in near]
        + [p.hdev(i) for i in range(1, z.H)]
        + [p.xdev(i) for i in range(1, z.X)]
        + [p.core()]
    )
    quarter = part(p.dp, rq)
    w_out = [
        net.remote(w3.at[:, quarter], w3s.at[p.g, :, quarter], p.gdev(i)) for i in range(1, z.NG)
    ]
    y_out, a_out = [], []
    for top in (1, 0):
        y_out.append(
            net.remote(n1.at[pl.ds(top * hr, hr)], n1s.at[slot_rows(rhi, p.lo, top)],
                       slot_dev(rhi, 1 - p.lo))
        )
    for top in (0, 1):
        a_out.append(
            [
                net.remote(n1.at[pl.ds(top * hr, hr)], n1s.at[slot_rows(rhi, p.lo, top)],
                           slot_dev(a, p.lo))
                for a in near
            ]
        )
    def wo_rows(t):
        return part((t % z.G) * z.NG + t // z.G, z.cw)

    cols = part(p.dp, qc)
    own_o = wos.at[wo_rows(p.t), cols]
    o_out = [net.remote(wo.at[:, cols], own_o, p.hdev(i)) for i in range(1, z.H)]
    o_keep = net.local(wo.at[:, cols], own_o)
    o_hop = [net.remote(own_o, own_o, p.y())]
    for i in range(1, z.H):
        block = wos.at[wo_rows(((p.hi + z.H - i) % z.H) * 2 + p.lo), cols]
        o_hop.append(net.remote(block, block, p.y()))
    block = wos.at[:, cols]
    o_along = [net.remote(block, block, p.xdev(i)) for i in range(1, z.X)]
    o_across = []
    for x in range(z.X):
        block = wos.at[:, part(x * 2 + p.c, qc)]
        o_across.append(net.remote(block, block, p.core()))

    def pieces(h2, lo):
        k, x = lo * (z.H // 2) + h2, p.x
        return (
            wgs.at[part(x, rx), part(k, cf)],
            wus.at[part(x, rx), part(k, cf)],
            wds.at[pl.ds(pl.multiple_of(k * cf + x * dx, 16), dx)],
        )

    src = (
        wg.at[part(p.x, rx), part(p.c, cf)],
        wu.at[part(p.x, rx), part(p.c, cf)],
        wd.at[pl.ds(pl.multiple_of(p.c * cf + p.x * dx, 16), dx)],
    )
    h2n = z.H // 2

    def to(refs, into, device):
        return [net.remote(a, b, device) for a, b in zip(refs, into)]

    def all_x(refs):
        return [cp for m in range(1, z.X) for cp in to(refs, refs, p.xdev(m))]

    f_z = [to(src, pieces(h2n - i, 0), p.h2dev(i)) for i in range(1, h2n)]
    f_y = [to(src, pieces(0, 1), p.y())]
    f_y += [to(pieces(h2n - i, 0), pieces(h2n - i, 1), p.y()) for i in range(1, h2n)]
    f_x = [all_x(pieces(0, 1))]
    f_xz = [all_x(pieces(h2n - i, 0)) for i in range(1, h2n)]
    mine = seed.at[p.hl * 2 + p.c]
    other = seed.at[(1 - p.hl) * 2 + p.c]
    s_y, s_core = net.remote(cot, mine, p.pair()), net.remote(cot, mine, p.core())
    s_hop = net.remote(other, other, p.core())

    keep_w = net.local(w3, w3s.at[p.g])
    keep_n = net.local(n1, n1s.at[part(p.r, z.rows)])
    o_keep.start()
    for cp in w_out + o_out:
        cp.start()
    y_out[0].start()
    for cp in a_out[0]:
        cp.start()
    keep_w.start()
    keep_n.start()
    y_out[1].start()
    for cp in a_out[1]:
        cp.start()
    for cp in w_out:
        cp.wait_recv()
    w_back = [(p.g + z.NG - i) % z.NG for i in range(1, z.NG)]
    along = []
    for g in w_back:
        block = w3s.at[g, :, quarter]
        along += [net.remote(block, block, p.xdev(i)) for i in range(1, z.X)]
    for cp in along:
        cp.start()
    o_keep.wait()
    o_hop[0].start()
    for i in range(1, z.H):
        o_out[i - 1].wait_recv()
        o_hop[i].start()
    for cp in along:
        cp.wait_recv()
    across = []
    for g in w_back:
        for x in range(z.X):
            block = w3s.at[g, :, part(x * 2 + p.c, rq)]
            across.append(net.remote(block, block, p.core()))
            across[-1].start()
    y_out[0].wait_recv()
    hop_a = []
    block = n1s.at[slot_rows(rhi, 1 - p.lo, 1)]
    hop_a = [net.remote(block, block, slot_dev(a, p.lo)) for a in near]
    for cp in hop_a:
        cp.start()
    hop_y = []
    for j, a in enumerate(back):
        a_out[0][j].wait_recv()
        block = n1s.at[slot_rows(a, p.lo, 0)]
        hop_y.append(net.remote(block, block, slot_dev(rhi, 1 - p.lo)))
        hop_y[-1].start()
    for cp in across:
        cp.wait_recv()
    for cp in o_hop:
        cp.wait_recv()
    for cp in o_along:
        cp.start()
    keep_w.wait()
    keep_n.wait()
    for m in range(3):
        if wide:
            for g in range(z.NG):
                w3c[m, :, g * z.cw : (g + 1) * z.cw] = w3s[g, m]
        else:
            w3c[m] = add_refs(*[w3s[g, m] for g in range(z.NG)]).astype(BF16)

    def start(*copies):
        def f():
            for cp in copies:
                cp.start()
        return f

    def arrive(*copies):
        def f():
            for cp in copies:
                cp.wait_recv()
        return f

    width = q.shape[1]
    pairs, bq = width // 128, min(256, z.rows)
    per = z.rows // bq
    blocks = WIN // bq
    total = pairs * blocks
    steps = {}

    def at(i, *functions):
        steps.setdefault(min(i, total - 1), []).extend(functions)

    at(0, arrive(*o_along), start(*o_across))
    for m in range(3):
        at(3 + m, arrive(f_y[0][m]), start(*f_x[0][m::3]))
        for i in range(h2n - 1):
            at(7 + m, arrive(f_z[i][m]), start(f_y[i + 1][m], *f_xz[i][m::3]))
    at(0, start(s_core, s_y))
    at(total - 1, arrive(s_y), start(s_hop))

    order = slot_order(p, z)

    def project(r):
        rows = part(r, z.rows)
        a = n1s[rows]
        for m, ref in enumerate((q, k, v)):
            y = dot(a, w3c[m])
            for j in range(width // 128):
                t = y[:, j * 128 : j * 128 + 128]
                if m < 2:
                    t = turn(t, cos[rows], sin[rows])
                ref[rows, j * 128 : j * 128 + 128] = t.astype(BF16)

    project(order[0])
    y_out[1].wait_recv()
    for group in f_y[:1] + f_z:
        for cp in group:
            cp.start()
    project(order[1])
    for j in range(half - 1):
        a_out[1][j].wait_recv()
        hop_a[j].wait_recv()
        hop_y[j].wait_recv()
    for r in order[2:]:
        project(r)
    stores = [net.local(a, b) for a, b in (
        (n1s, n1_o), (w3c, w3_o), (q, q_o), (k, k_o), (v, v_o)
    )]
    for cp in stores:
        cp.start()
    lane_k, lane_q = lane_of(WIN), lane_of(bq)

    m_out = {}
    for j in range(pairs):
        for i in range(1, z.G):
            col = pl.ds(pl.multiple_of(p.r * z.hw + j * 128, 128), 128)
            cp = net.remote(
                mixed.at[part(p.ri(i), z.rows), j * 128 : j * 128 + 128],
                own.at[:, col], p.rdev(i),
            )
            m_out[j, i] = cp
            at(j * blocks + i * per - 1, start(cp))

    def block(i, _):
        j, b = i // blocks, i % blocks
        row = ((p.r + 1 + b // per) % z.G) * z.rows + (b % per) * bq
        col, rows = part(j, 128), pl.ds(pl.multiple_of(row, bq), bq)
        k2, v2, kb, q2 = k[:, col], v[:, col], bias[...], q[rows, col]
        mixes = []
        for e in range(2):
            own_k = (lane_k < HD) if e == 0 else (lane_k >= HD)
            own_q = (lane_q < HD) if e == 0 else (lane_q >= HD)
            k_e = jnp.where(own_k, k2, kb)
            v_e = jnp.where(own_k, v2, jnp.ones_like(v2))
            q_e = jnp.where(own_q, q2, jnp.where(lane_q % HD == 0, 1.0, 0.0).astype(BF16))
            s = dot(q_e, k_e, NT)
            top = jnp.max(s, axis=1, keepdims=True)
            prob = jnp.exp2((s - top) * C2).astype(BF16)
            sums = dot(prob, v_e)
            mixes.append(sums / pltpu.roll(sums, HD, 1))
            norm = jnp.where(own_q, 0.0, top + jnp.log2(jnp.where(own_q, 1.0, sums)) * (1.0 / C2))
            full = jnp.where(own_q, q2.astype(F32), spare_lanes(1.0, norm, lane_q))
            qa[2 * j + e, rows] = full.astype(BF16)
        mix = jnp.where(lane_q < HD, mixes[0], mixes[1])
        o[rows, col] = mix
        mixed[rows, col] = mix.astype(BF16)
        run_at(steps, i)
        return 0

    lax.fori_loop(0, total, block, 0)
    m_keep = net.local(mixed.at[part(p.r, z.rows)], own.at[:, part(p.r, z.hw)])
    m_keep.start()
    for cp in list(m_out.values()) + o_across + [s_core]:
        cp.wait_recv()
    for group in f_x + f_xz + f_y[1:]:
        for cp in group:
            cp.wait_recv()
    s_hop.wait_recv()
    for cp in stores + [m_keep]:
        cp.wait()
    net.wait_sends()


def back_kernel(
    z, gm, qa_h, q_h, k_h, v_h, o_h, w3_h, n1_h, dg, du, dd, do_w, out_pair, bias, cos, sin,
    got, out_got, og, ou, od, ow, oo,
    send, recv, lsem,
    qa, q, k, v, o, do, dq, dk, dv, do_e, dk_sum, dv_sum, w3, n1, part_one, p3,
    rgx, rux, sg, su, sd, rgy, ruy, rdy, rgz, ruz, rdz,
    oc, so, ox, oy, oz, wc, sw, wx, wgr, join_y, join_z,
):
    p, net = Place(z), Net(send, recv, lsem)
    d, rows = z.d, z.rows
    rq, rx, dx, cf, h2n = d // z.n_dp, d // z.X, z.cf // z.X, z.cf, z.H // 2
    width = q.shape[1]
    bq = min(512, rows)
    per, blocks, pairs = rows // bq, WIN // bq, width // 128
    total = pairs * blocks
    loads = [net.local(a, b) for a, b in (
        (qa_h, qa), (q_h, q), (k_h, k), (v_h, v), (o_h, o),
        (gm.at[:, part(p.r, z.hw)], do.at[part(p.r, rows)]),
    )]
    late = [net.local(a, b) for a, b in (
        (dd, sd), (dg.at[part(p.x, rx)], sg),
        *[(do_w.at[:, :, part(x * 2 + p.c, rq)], so.at[x]) for x in range(z.X)],
        (w3_h, w3), (n1_h, n1),
    )]
    for cp in loads + late:
        cp.start()
    meet(
        [p.rdev(i) for i in range(1, z.G)]
        + [p.hdev(i) for i in range(1, z.H)]
        + [p.xdev(i) for i in range(1, z.X)]
        + [p.core()]
    )

    def start(*copies):
        def f():
            for cp in copies:
                cp.start()
        return f

    def arrive(*copies):
        def f():
            for cp in copies:
                cp.wait_recv()
        return f

    steps = {}

    def at(i, *functions):
        steps.setdefault(min(i, total - 1), []).extend(functions)

    dest = do.at[part(p.r, rows)]
    a_out = [net.remote(gm.at[:, part(p.ri(i), z.hw)], dest, p.rdev(i)) for i in range(1, z.G)]
    for cp in a_out:
        cp.start()
    def spot(h2, lo):
        return ((lo + p.lo) % 2) * h2n + (h2 + h2n - p.h2) % h2n

    bufs = ((dd, None, sd, rdy, rdz, od), (dg, rgx, sg, rgy, rgz, og), (du, rux, su, ruy, ruz, ou))

    def piece(m, ref, s):
        return ref.at[s] if m == 0 else ref.at[:, part(s, cf)]

    fx = [[net.remote(bufs[m][0].at[part(p.xi(i), rx)], bufs[m][1].at[i - 1], p.xdev(i))
           for i in range(1, z.X) if m == 1] for m in range(2)]
    fy = [[net.remote(piece(m, bufs[m][2], spot(h2, 1 - p.lo)), bufs[m][3].at[h2], p.y())
           for h2 in range(h2n)] for m in range(2)]
    fz = [[net.remote(piece(m, bufs[m][2], spot((p.h2 + i) % h2n, p.lo)), bufs[m][4].at[i - 1],
                      p.h2dev(i)) for i in range(1, h2n)] for m in range(2)]
    up_y = [net.remote(du.at[:, part(spot(h2, 1 - p.lo), cf)], ruy.at[h2], p.y())
            for h2 in range(h2n)]
    up_own = [net.local(du.at[:, part(spot(h2, p.lo), cf)], su.at[h2]) for h2 in range(h2n)]
    up_x = [net.remote(su.at[:, part(p.xi(i), rx)], rux.at[i - 1], p.xdev(i))
            for i in range(1, z.X)]
    up_z = [net.remote(su.at[(p.h2 + i) % h2n, part(p.x, rx)], ruz.at[i - 1], p.h2dev(i))
            for i in range(1, h2n)]

    def up_y_in():
        for h2 in range(h2n):
            up_own[h2].wait()
            up_y[h2].wait_recv()
            su[h2] = add_refs(su[h2], ruy[h2]).astype(BF16)
        start(*up_x)()

    def up_x_in():
        arrive(*up_x)()
        for h2 in range(h2n):
            su[h2, part(p.x, rx)] = add_refs(
                su[h2, part(p.x, rx)], *[rux[i, h2] for i in range(z.X - 1)]
            ).astype(BF16)
        start(*up_z)()

    def up_z_in():
        arrive(*up_z)()
        ou[done_at[2]] = add_refs(
            su[p.h2, part(p.x, rx)], *[ruz[i] for i in range(h2n - 1)]
        ).astype(BF16)
        start(*fa[2])()
    done_at = [
        (pl.ds(pl.multiple_of(p.c * cf + p.x * dx, 16), dx),),
        (part(p.x, rx), part(p.c, cf)),
        (part(p.x, rx), part(p.c, cf)),
    ]
    fa, fc = [], []
    for m in range(3):
        block = bufs[m][5].at[done_at[m]]
        fa.append([net.remote(block, block, p.xdev(i)) for i in range(1, z.X)])
        block = od.at[part(p.c, cf)] if m == 0 else bufs[m][5].at[:, part(p.c, cf)]
        fc.append(net.remote(block, block, p.core()))

    def ffn_x(m):
        def f():
            arrive(*fx[m])()
            late[m].wait()
            got_x, own = bufs[m][1], bufs[m][2]
            for h in range(2 * h2n):
                c = pl.ds(h * cf, cf)
                own[:, c] = add_refs(
                    own[:, c], *[got_x[i, :, c] for i in range(z.X - 1)]
                ).astype(BF16)
            start(*fy[m])()
        return f

    def ffn_y(m):
        def f():
            arrive(*fy[m])()
            own, got_y = bufs[m][2], bufs[m][3]
            for h2 in range(h2n):
                if m == 0:
                    own[spot(h2, p.lo)] = add_refs(own[spot(h2, p.lo)], got_y[h2]).astype(BF16)
                else:
                    c = part(spot(h2, p.lo), cf)
                    own[:, c] = add_refs(own[:, c], got_y[h2]).astype(BF16)
            start(*fz[m])()
        return f

    def ffn_z(m):
        def f():
            arrive(*fz[m])()
            own, got_z, out = bufs[m][2], bufs[m][4], bufs[m][5]
            s = spot(p.h2, p.lo)
            mine = own[s] if m == 0 else own[:, part(s, cf)]
            out[done_at[m]] = add_refs(mine, *[got_z[i] for i in range(h2n - 1)]).astype(BF16)
            start(*fa[m])()
        return f

    def ffn_c(m):
        def f():
            arrive(*fa[m])()
            fc[m].start()
        return f

    half = z.G // 2
    c_out = [net.remote(do_w.at[:, :, part(p.xi(i) * 2 + 1 - p.c, rq)], oc.at[i], p.core())
             for i in range(z.X)]
    c_x = [net.remote(so.at[p.xi(i)], ox.at[i - 1], p.xdev(i)) for i in range(1, z.X)]
    c_y = [net.remote(so.at[p.x, i * 2 + 1 - p.lo], oy.at[i], p.y()) for i in range(half)]
    c_z = [net.remote(so.at[p.x, (p.hii(i) % half) * 2 + p.lo, part(p.hii(i) // half, z.cw)],
                      oz.at[i - 1], p.hdev(i)) for i in range(1, z.H)]
    cols = part(p.dp, rq)
    block = oo.at[:, cols]
    c_a = [net.remote(block, block, p.xdev(i)) for i in range(1, z.X)]
    c_c = []
    for x in range(z.X):
        block = oo.at[:, part(x * 2 + p.c, rq)]
        c_c.append(net.remote(block, block, p.core()))

    def wo_c():
        for cp in late[2 : 2 + z.X]:
            cp.wait()
        for i in list(range(1, z.X)) + [0]:
            c_out[i].wait_recv()
            for r in range(z.G):
                so[p.xi(i), r] = add_refs(so[p.xi(i), r], oc[i, r]).astype(BF16)
        start(*c_x)()

    def wo_x():
        arrive(*c_x)()
        for r in range(z.G):
            so[p.x, r] = add_refs(so[p.x, r], *[ox[i, r] for i in range(z.X - 1)]).astype(BF16)
        start(*c_y)()

    def wo_y():
        arrive(*c_y)()
        for i in range(half):
            r = i * 2 + p.lo
            so[p.x, r] = add_refs(so[p.x, r], oy[i]).astype(BF16)
        start(*c_z)()

    def wo_z():
        arrive(*c_z)()
        mine = so[p.x, (p.hi % half) * 2 + p.lo, part(p.hi // half, z.cw)]
        oo[:, cols] = add_refs(mine, *[oz[i] for i in range(z.H - 1)]).astype(BF16)
        start(*c_a)()

    def wo_a():
        arrive(*c_a)()
        start(*c_c)()

    o_send = net.remote(out_pair, out_got, p.pair())
    start(*fx[1], *c_out)()
    late[0].wait()
    start(*fy[0], *up_y, *up_own)()
    at(0, start(o_send))
    at(1, ffn_y(0))
    at(2, wo_c)
    at(3, ffn_x(1))
    at(4, ffn_z(0), up_y_in)
    at(5, ffn_y(1), wo_x)
    at(6, up_x_in, ffn_c(0))
    at(7, ffn_z(1))

    for cp in loads:
        cp.wait()
    lane_q, sub = lane_of(bq), 1024
    lane_k = lane_of(sub)
    s64 = lane_k % HD
    ones3 = jnp.where((s64 >= 1) & (s64 <= 3), 1.0, 0.0).astype(BF16)

    def block_step(i, _):
        j, b = i // blocks, i % blocks
        for n in range(1, z.G):

            @pl.when((j == 0) & (b == n * per))
            def _():
                a_out[z.G - 1 - n].wait_recv()

        row = ((p.r + b // per) % z.G) * rows + (b % per) * bq
        col, at_q = part(j, 128), pl.ds(pl.multiple_of(row, bq), bq)
        q2, do2 = q[at_q, col], do[at_q, col]
        prod = do2.astype(F32) * o[at_q, col]
        for e in range(2):
            own_q = (lane_q < HD) if e == 0 else (lane_q >= HD)
            delta = jnp.sum(jnp.where(own_q, prod, 0.0), axis=1, keepdims=True)
            spare = spare_lanes(0.0, jnp.broadcast_to(delta, prod.shape), lane_q)
            do_e[e] = jnp.where(own_q, do2.astype(F32), spare).astype(BF16)
        dqs = [jnp.zeros((bq, 128), F32)] * 2
        for s in range(WIN // sub):
            keys = pl.ds(s * sub, sub)
            k2, v2 = k[keys, col], v[keys, col]
            kb = bias[keys] + ones3
            dks, dvs = [], []
            for e in range(2):
                own_k = (lane_k < HD) if e == 0 else (lane_k >= HD)
                k_e = jnp.where(own_k, k2, kb)
                v_e = jnp.where(own_k, v2, ones3)
                prob = jnp.exp2(dot(k_e, qa[2 * j + e, at_q], NT) * C2)
                ds = (prob * dot(v_e, do_e[e], NT)).astype(BF16)
                dvs.append(dot(prob.astype(BF16), do2))
                dks.append(dot(ds, q2))
                dqs[e] = dqs[e] + dot(ds, k2, TN)
            dv_new = jnp.where(lane_k < HD, dvs[0], dvs[1])
            dk_new = jnp.where(lane_k < HD, dks[0], dks[1])

            @pl.when(b == 0)
            def _():
                dv_sum[keys] = dv_new
                dk_sum[keys] = dk_new

            @pl.when(b > 0)
            def _():
                dv_sum[keys] += dv_new
                dk_sum[keys] += dk_new

        dq_new = jnp.where(lane_q < HD, dqs[0], dqs[1]) * SCALE
        dq[at_q, col] = turn(dq_new, cos[at_q], -sin[at_q]).astype(BF16)

        @pl.when(b == blocks - 1)
        def _():
            dv[:, col] = dv_sum[...].astype(BF16)
            dk[:, col] = turn(dk_sum[...] * SCALE, cos[...], -sin[...]).astype(BF16)

        run_at(steps, i)
        return 0

    lax.fori_loop(0, total, block_step, 0)

    for cp in late[2 + z.X :]:
        cp.wait()
    half, hr, rhi = z.G // 2, rows // 2, p.r // 2
    near = [(rhi + j) % half for j in range(1, half)]

    def slot_dev(a, b):
        return (p.dp, p.g * z.G + a * 2 + b)

    def top(a, b, h):
        return pl.ds(pl.multiple_of((a * 2 + b) * rows + h * hr, 16), hr)

    def rows_one(a, b):
        here = part(a * 2 + b, rows)
        part_one[here] = (
            dot(dq[here], w3[0], NT) + dot(dk[here], w3[1], NT) + dot(dv[here], w3[2], NT)
        ).astype(BF16)

    y_dev = slot_dev(rhi, 1 - p.lo)
    r_y, r_z = [], []
    for j, a in enumerate(near):
        rows_one(a, 1 - p.lo)
        r_y.append(net.remote(part_one.at[top(a, 1 - p.lo, 0)], join_y.at[j], y_dev))
        r_z.append(net.remote(part_one.at[top(a, 1 - p.lo, 1)], join_z.at[j], slot_dev(a, p.lo)))
        start(r_y[j], r_z[j])()
    rows_one(rhi, 1 - p.lo)
    g_y = [net.remote(part_one.at[top(rhi, 1 - p.lo, h)], got.at[0, pl.ds(h * hr, hr)], y_dev)
           for h in range(2)]
    g_y[0].start()
    g_z = []
    for j, a in enumerate(near):
        rows_one(a, p.lo)
        g_z.append([net.remote(part_one.at[top(a, p.lo, h)], got.at[1 + j, pl.ds(h * hr, hr)],
                               slot_dev(a, p.lo)) for h in range(2)])
        g_z[j][1].start()
    rows_one(rhi, p.lo)
    r_keep = net.local(part_one.at[part(p.r, rows)], got.at[half])
    r_keep.start()

    def join():
        arrive(*r_z)()
        here = top(rhi, 1 - p.lo, 1)
        part_one[here] = add_refs(
            part_one[here], *[join_z[j] for j in range(half - 1)]
        ).astype(BF16)
        g_y[1].start()
        for j, a in enumerate(near):
            r_y[j].wait_recv()
            here = top(a, p.lo, 0)
            part_one[here] = add_refs(part_one[here], join_y[j]).astype(BF16)
            g_z[j][0].start()

    for m, t in enumerate((dq, dk, dv)):
        y = dot(n1[...], t[...], TN).astype(BF16)
        for g in range(z.NG):
            p3[g, m] = y[:, g * z.cw : (g + 1) * z.cw]
    w_c = [net.remote(p3.at[:, :, part(p.xi(i) * 2 + 1 - p.c, rq)], wc.at[i], p.core())
           for i in range(z.X)]
    start(*w_c)()
    wo_y()
    w_x = []
    for i in list(range(1, z.X)) + [0]:
        w_c[i].wait_recv()
        for g in range(z.NG):
            sw[i, g] = add_refs(p3[g, :, part(p.xi(i) * 2 + p.c, rq)], wc[i, g]).astype(BF16)
        if i:
            w_x.append(net.remote(sw.at[i], wx.at[i - 1], p.xdev(i)))
            w_x[-1].start()
    join()
    ffn_c(1)()
    wo_z()
    up_z_in()
    arrive(*w_x)()
    for g in range(z.NG):
        sw[0, g] = add_refs(sw[0, g], *[wx[i, g] for i in range(z.X - 1)]).astype(BF16)
    w_g = [net.remote(sw.at[0, p.gi(i)], wgr.at[i - 1], p.gdev(i)) for i in range(1, z.NG)]
    start(*w_g)()
    wo_a()
    ffn_c(2)()
    arrive(*w_g)()
    quarter = part(p.dp, rq)
    for m in range(3):
        ow[m, quarter] = add_refs(
            sw[0, p.g, m], *[wgr[i, m] for i in range(z.NG - 1)]
        ).astype(BF16)
    block = ow.at[:, quarter]
    w_a = [net.remote(block, block, p.xdev(i)) for i in range(1, z.X)]
    start(*w_a)()
    arrive(*w_a)()
    w_last = []
    for x in range(z.X):
        block = ow.at[:, part(x * 2 + p.c, rq)]
        w_last.append(net.remote(block, block, p.core()))
        w_last[-1].start()
    arrive(*c_c, *fc, *w_last, o_send, *g_y, *[cp for pair in g_z for cp in pair])()
    r_keep.wait()
    net.wait_sends()


def sum_norms_kernel(z, own, out, send, recv, lsem, far, near):
    p, net = Place(z), Net(send, recv, lsem)
    t_dev = [(p.dp, (p.t + i) % z.n_t) for i in range(1, z.n_t)]
    d_dev = [((p.dp + i) % z.n_dp, p.t) for i in range(1, z.n_dp)]
    meet(t_dev + d_dev)
    first = [net.remote(own, far.at[p.t], dev) for dev in t_dev]
    for cp in first:
        cp.start()
    far[p.t] = own[...]
    for cp in first:
        cp.wait_recv()
    near[p.dp] = add_refs(*[far[i] for i in range(z.n_t)])
    second = [net.remote(near.at[p.dp], near.at[p.dp], dev) for dev in d_dev]
    for cp in second:
        cp.start()
    for cp in second:
        cp.wait_recv()
    out[...] = add_refs(*[near[i] for i in range(z.n_dp)])
    net.wait_sends()


def norm_stats(v):
    centre = v - jnp.mean(v, axis=-1, keepdims=True)
    inverse = lax.rsqrt(jnp.mean(centre * centre, axis=-1, keepdims=True) + EPSILON)
    return centre * inverse, inverse


def norm_backward(grad_in, scaled, inverse, gain):
    weighted = grad_in * gain
    first_mean = jnp.mean(weighted, axis=-1, keepdims=True)
    second_mean = jnp.mean(weighted * scaled, axis=-1, keepdims=True)
    return inverse * (weighted - first_mean - scaled * second_mean)


def per_device(
    n_dp, n_t, tokens, lengths, ln1_gain, ln1_bias, w_query, w_key, w_value, w_out,
    ln2_gain, ln2_bias, w_gate, w_up, w_down, cotangent,
):
    rows, d = tokens.shape
    cw, cfull = w_query.shape[1], w_gate.shape[1]
    z = Sizes(n_dp, n_t, rows, d, cw, cfull)
    G, NG, H, X, hw, cf = z.G, z.NG, z.H, z.X, z.hw, z.cf
    rq, rx, dx = d // n_dp, d // X, cf // X
    slot = lax.axis_index("tensor") // G
    length = lax.dynamic_index_in_dim(lengths, slot, keepdims=False)
    lane = lax.broadcasted_iota(jnp.int32, (WIN, 128), 1) % HD
    place = lax.broadcasted_iota(jnp.int32, (WIN, 128), 0)
    bias = jnp.where((lane == 0) & (place >= length), -1e30, 0.0).astype(BF16)
    cos, sin = (jnp.asarray(t, F32) for t in rope_tables())

    w_three = jnp.stack([w_query, w_key, w_value])
    if cw % 128:
        wider = jnp.zeros((3, d, hw), BF16)
        w_three = lax.dynamic_update_slice(wider, w_three, (0, 0, slot * cw))
    n1, w3, q, k, v, o, qa, mixed_own, wo, wg, wu, wd, seed = comm_call(
        front_kernel, z, "front", 1,
        (
            shape((WIN, d)), shape((3, d, hw)), shape((WIN, hw)), shape((WIN, hw)),
            shape((WIN, hw)), shape((WIN, hw), F32), shape((hw // HD, WIN, 128)),
            shape((rows, d)), shape((d, d)), shape((d, H * cf)), shape((d, H * cf)),
            shape((H * cf, d)), shape((4, rows, d)),
        ),
        [VMEM] * 3 + [HBM, VMEM, VMEM, VMEM] + [HBM] * 5,
        [HBM] * 5 + [VMEM] * 4 + [HBM] * 4,
        [
            pltpu.VMEM((NG,) + w_three.shape, BF16), pltpu.VMEM((WIN, hw), BF16),
            pltpu.VMEM((WIN, d), BF16), pltpu.VMEM((3, d, hw), BF16),
            *[pltpu.VMEM((WIN, hw), BF16)] * 3, pltpu.VMEM((rows, d), BF16),
        ],
        n=160, vmem=60 * MIB,
    )(
        tokens, ln1_gain.reshape(1, d), ln1_bias.reshape(1, d), w_three, cos, sin, bias,
        w_out, w_gate, w_up, w_down, cotangent,
    )
    every = 4 * rows
    width = H * cf
    mid_out = (
        shape((rows, d), F32), shape((rows, d)), shape((rows, d), F32), shape((rows, d)),
        shape((d, d)), shape((d, width)), shape((d, width)), shape((H, dx, d)), shape((2, d), F32),
    )
    out_part, out_pair, grad_middle, grad_mixed, p_wo, p_gate, p_up, p_down, sums_two = comm_call(
        middle_kernel, z, "middle", 4, mid_out,
        [HBM] * 11 + [VMEM] * 2, [HBM] * 8 + [VMEM],
        [
            pltpu.VMEM((rows, d), BF16), pltpu.VMEM((rows, d), BF16), pltpu.VMEM((d, d), BF16),
            pltpu.VMEM((d, width), BF16), pltpu.VMEM((d, width), BF16),
            pltpu.VMEM((width, d), BF16), pltpu.VMEM((every, d), BF16),
            pltpu.VMEM((every, d), BF16), pltpu.VMEM((rows, d), F32),
            pltpu.VMEM((every, width), BF16), pltpu.VMEM((every, width), BF16),
            pltpu.VMEM((every, width), BF16), pltpu.VMEM((every, d), BF16),
            pltpu.VMEM((every, d), BF16), pltpu.VMEM((2, 2, rows, d), BF16),
            pltpu.VMEM((rows, d), BF16), pltpu.VMEM((2, rows, d), BF16),
            pltpu.VMEM((rows, d), F32), pltpu.VMEM((X - 1, H, dx, d), BF16),
        ],
        vmem=62 * MIB,
    )(
        mixed_own, tokens, wo, wg, wu, wd, w_gate, w_up, w_down, seed.reshape(every, d), cotangent,
        ln2_gain.reshape(1, d), ln2_bias.reshape(1, d),
    )
    gain_two, bias_two = sums_two[0], sums_two[1]
    p_wo = p_wo.reshape(G, hw, d)
    V = pltpu.VMEM
    pieces = ((rx, cf), (rx, cf), (dx, d))
    got, out_got, g_gate, g_up, g_down, g_w3, g_wo = comm_call(
        back_kernel, z, "back", 8,
        (
            shape((G // 2 + 1, rows, d)), shape((rows, d)), shape((d, 2 * cf)), shape((d, 2 * cf)),
            shape((2 * cf, d)), shape((3, d, cw)), shape((cw, d)),
        ),
        [HBM] * 13 + [VMEM] * 3, [HBM] * 2 + [VMEM] * 5,
        [
            V((hw // HD, WIN, 128), BF16), V((WIN, hw), BF16), V((WIN, hw), BF16),
            V((WIN, hw), BF16), V((WIN, hw), F32), V((WIN, hw), BF16), V((WIN, hw), BF16),
            V((WIN, hw), BF16), V((WIN, hw), BF16), V((2, min(512, rows), 128), BF16),
            V((WIN, 128), F32), V((WIN, 128), F32), V((3, d, hw), BF16), V((WIN, d), BF16),
            V((WIN, d), BF16), V((NG, 3, d, cw), BF16),
            V((X - 1, rx, width), BF16), V((X - 1, H // 2, rx, cf), BF16),
            V((rx, width), BF16), V((H // 2, d, cf), BF16), V((H, dx, d), BF16),
            *[V((H // 2,) + dims, BF16) for dims in ((rx, cf), (d, cf), (dx, d))],
            *[V((H // 2 - 1,) + dims, BF16) for dims in pieces],
            V((X, G, hw, rq), BF16), V((X, G, hw, rq), BF16), V((X - 1, G, hw, rq), BF16),
            V((G // 2, hw, rq), BF16), V((H - 1, cw, rq), BF16),
            V((X, NG, 3, rq, cw), BF16), V((X, NG, 3, rq, cw), BF16),
            V((X - 1, NG, 3, rq, cw), BF16), V((NG - 1, 3, rq, cw), BF16),
            *[V((G // 2 - 1, rows // 2, d), BF16)] * 2,
        ],
        n=160, vmem=62 * MIB,
    )(
        grad_mixed, qa, q, k, v, o, w3, n1, p_gate, p_up, p_down, p_wo, out_pair, bias, cos, sin,
    )
    output = (out_part + out_got.astype(F32)).astype(BF16)
    scaled_one, inverse_one = norm_stats(tokens.astype(F32))
    grad_one = jnp.sum(got.astype(F32), axis=0)
    gain_one = jnp.sum(grad_one * scaled_one, axis=0)
    bias_one = jnp.sum(grad_one, axis=0)
    back_one = norm_backward(grad_one, scaled_one, inverse_one, ln1_gain)
    grad_tokens = (grad_middle + back_one).astype(BF16)
    norms = comm_call(
        sum_norms_kernel, z, "sum_norms", 9, shape((4, d), F32), [VMEM], VMEM,
        [V((n_t, 4, d), F32), V((n_dp, 4, d), F32)],
    )(jnp.stack([gain_one, bias_one, gain_two, bias_two]))
    return (
        output, grad_tokens, norms[0], norms[1],
        g_w3[0].astype(F32), g_w3[1].astype(F32), g_w3[2].astype(F32), g_wo.astype(F32),
        norms[2], norms[3], g_gate.astype(F32), g_up.astype(F32), g_down.astype(F32),
    )


def solution(mesh):
    rows, cols, each = P(("dp", "tensor"), None), P(None, "tensor"), P("tensor", None)
    return jax.shard_map(
        functools.partial(per_device, mesh.shape["dp"], mesh.shape["tensor"]),
        mesh=mesh,
        in_specs=(
            rows, P("dp"), P(), P(), cols, cols, cols, each, P(), P(), cols, cols, each, rows,
        ),
        out_specs=(
            rows, rows, P(), P(), cols, cols, cols, each, P(), P(), cols, cols, each,
        ),
        check_vma=False,
    )
```

```python
import functools

import jax
import jax.numpy as jnp
import numpy as np
from jax import lax
from jax.experimental import pallas as pl
from jax.experimental.pallas import tpu as pltpu
from jax.sharding import PartitionSpec as P

HD = 64
WIN = 2048
EPSILON = 1e-05
SCALE = HD ** (-0.5)
LOG2E = 1.4426950408889634
C2 = SCALE * LOG2E
NT = (((1,), (1,)), ((), ()))
NN = (((1,), (0,)), ((), ()))
TN = (((0,), (0,)), ((), ()))
MESH = pl.DeviceIdType.MESH
F32 = jnp.float32
BF16 = jnp.bfloat16
MIB = 1024 * 1024
HBM = pl.BlockSpec(memory_space=pl.ANY)
VMEM = pl.BlockSpec(memory_space=pltpu.VMEM)


def dot(a, b, dims=NN):
    return lax.dot_general(a, b, dims, preferred_element_type=F32)


def shape(dims, kind=BF16):
    return jax.ShapeDtypeStruct(dims, kind)


class Sizes:
    def __init__(self, n_dp, n_t, rows, d, cw, cfull):
        self.n_dp, self.n_t, self.rows, self.d = n_dp, n_t, rows, d
        self.X, self.H = n_dp // 2, n_t // 2
        self.G = WIN // rows
        self.NG = n_t // self.G
        self.cw, self.hw = cw, self.NG * cw
        self.cf = cfull // 2


class Place:
    def __init__(self, z):
        self.z = z
        dp, t = lax.axis_index("dp"), lax.axis_index("tensor")
        self.dp, self.t = dp, t
        self.x, self.c = dp // 2, dp % 2
        self.hi, self.lo = t // 2, t % 2
        self.g, self.r = t // z.G, t % z.G
        self.h2, self.hl = self.hi // 2, self.hi % 2

    def pair(self):
        return (self.dp, (self.h2 * 2 + 1 - self.hl) * 2 + self.lo)

    def h2dev(self, i):
        return (self.dp, (((self.h2 + i) % (self.z.H // 2)) * 2 + self.hl) * 2 + self.lo)

    def core(self):
        return (self.x * 2 + 1 - self.c, self.t)

    def y(self):
        return (self.dp, self.hi * 2 + 1 - self.lo)

    def xi(self, i):
        return (self.x + i) % self.z.X

    def xdev(self, i):
        return (self.xi(i) * 2 + self.c, self.t)

    def hii(self, i):
        return (self.hi + i) % self.z.H

    def hdev(self, i):
        return (self.dp, self.hii(i) * 2 + self.lo)

    def ri(self, i):
        return (self.r + i) % self.z.G

    def rdev(self, i):
        return (self.dp, self.g * self.z.G + self.ri(i))

    def gi(self, i):
        return (self.g + i) % self.z.NG

    def gdev(self, i):
        return (self.dp, self.gi(i) * self.z.G + self.r)


class Net:
    def __init__(self, send, recv, local=None):
        self.send, self.recv, self.local_sem = send, recv, local
        self.count, self.local_count = 0, 0
        self.all = []

    def remote(self, src, dst, device):
        k = self.count
        self.count += 1
        cp = pltpu.make_async_remote_copy(
            src_ref=src, dst_ref=dst, send_sem=self.send.at[k], recv_sem=self.recv.at[k],
            device_id=device, device_id_type=MESH,
        )
        self.all.append(cp)
        return cp

    def local(self, src, dst):
        k = self.local_count
        self.local_count += 1
        return pltpu.make_async_copy(src, dst, self.local_sem.at[k])

    def wait_sends(self):
        for cp in self.all:
            cp.wait_send()


def meet(devices):
    barrier = pltpu.get_barrier_semaphore()
    for device in devices:
        pl.semaphore_signal(barrier, inc=1, device_id=device, device_id_type=MESH)
    pl.semaphore_wait(barrier, len(devices))


def part(i, n):
    return pl.ds(pl.multiple_of(i * n, n), n)


def comm_call(body, z, name, cid, out_shape, in_specs, out_specs, scratch=(), n=64, vmem=None):
    return pl.pallas_call(
        functools.partial(body, z),
        out_shape=out_shape,
        in_specs=in_specs,
        out_specs=out_specs,
        scratch_shapes=[
            pltpu.SemaphoreType.DMA((n,)),
            pltpu.SemaphoreType.DMA((n,)),
            pltpu.SemaphoreType.DMA((64,)),
            *scratch,
        ],
        compiler_params=pltpu.CompilerParams(
            collective_id=cid, has_side_effects=True, vmem_limit_bytes=vmem
        ),
        name=name,
    )


def middle_kernel(
    z, own_h, tok_h, wo_h, wg_h, wu_h, wd_h, wg_o, wu_o, wd_o, seed_h, cot, gain, beta,
    out_part, out_pair, grad_mid, grad_mix, p_wo, p_gate, p_up, p_down, sums,
    send, recv, lsem,
    own, tok, wo, wg, wu, wd, seed, n2, middle, hidden, gg, gu, two, one, rc, ry, tot, out_f, rdx,
):
    p, net = Place(z), Net(send, recv, lsem)
    rows, d = z.rows, z.d
    cf, f_x = z.cf, []
    pairs = [(own_h, own), (wo_h, wo), (tok_h, tok)]
    for k in range(z.H):
        at = pl.ds(k * cf, cf)
        if k == 0:
            half = part(p.c, cf)
            pairs += [(wg_o.at[:, half], wg.at[:, at]), (wu_o.at[:, half], wu.at[:, at]),
                      (wd_o.at[half], wd.at[at])]
        elif k <= z.H // 2:
            pairs += [(wg_h.at[:, at], wg.at[:, at]), (wu_h.at[:, at], wu.at[:, at]),
                      (wd_h.at[at], wd.at[at])]
        else:
            up = part(p.x, d // z.X)
            down = pl.ds(pl.multiple_of(k * cf + p.x * (cf // z.X), 16), cf // z.X)
            some = [(wg_h.at[up, at], wg.at[up, at]), (wu_h.at[up, at], wu.at[up, at]),
                    (wd_h.at[down], wd.at[down])]
            pairs += some
            f_x += [net.remote(a, b, p.xdev(i)) for i in range(1, z.X) for a, b in some]
    for k, b in enumerate((p.hl * 2 + p.c, p.hl * 2 + 1 - p.c,
                           (1 - p.hl) * 2 + p.c, (1 - p.hl) * 2 + 1 - p.c)):
        at = part(b, rows)
        pairs.append((seed_h.at[at] if k else cot, seed.at[at]))
    loads = [net.local(a, b) for a, b in pairs]
    for cp in loads:
        cp.start()
    meet([p.pair(), p.core()] + [p.xdev(i) for i in range(1, z.X)])
    for cp in f_x:
        cp.start()
    chunk = 128
    blocks = [p.hl * 2 + p.c, p.hl * 2 + 1 - p.c,
              (1 - p.hl) * 2 + 1 - p.c, (1 - p.hl) * 2 + p.c]

    def block_rows(b):
        return pl.ds(pl.multiple_of(b * rows, rows), rows)

    for cp in loads[:3]:
        cp.wait()

    def norm(i, _):
        at = part(i, chunk)
        m = tok[at].astype(F32) + dot(own[at], wo[...])
        middle[at] = m
        scaled, _ = norm_stats(m)
        here = pl.ds(pl.multiple_of(blocks[0] * rows + i * chunk, chunk), chunk)
        n2[here] = (scaled * gain[...] + beta[...]).astype(BF16)
        return 0

    sub = rows // 2
    n_pair, n_core, n_hop = [], [], []
    for h in range(2):
        lax.fori_loop(h * (sub // chunk), (h + 1) * (sub // chunk), norm, 0)
        mine, far = [
            n2.at[pl.ds(pl.multiple_of(blocks[i] * rows + h * sub, sub), sub)] for i in (0, 3)
        ]
        n_pair.append(net.remote(mine, mine, p.pair()))
        n_core.append(net.remote(mine, mine, p.core()))
        n_hop.append(net.remote(far, far, p.core()))
        n_pair[h].start()
        n_core[h].start()
    for cp in loads[3:]:
        cp.wait()
    early, every = (z.H // 2 + 1) * cf, z.H * cf

    def sub_rows(b, i):
        return pl.ds(pl.multiple_of(b * rows + i * sub, sub), sub)

    def grads(b, low, high, first=0, last=2):
        cols = pl.ds(low, high - low)

        def body(i, _):
            at = sub_rows(b, i)
            a, e = n2[at], seed[at]
            gate, up = dot(a, wg[:, cols]), dot(a, wu[:, cols])
            sig = jax.nn.sigmoid(gate)
            silu = gate * sig
            hidden[at, cols] = (silu * up).astype(BF16)
            gh = dot(e, wd[cols], NT)
            gg[at, cols] = (gh * up * sig * (1.0 + gate * (1.0 - sig))).astype(BF16)
            gu[at, cols] = (gh * silu).astype(BF16)
            return 0

        lax.fori_loop(first, last, body, 0)

    def back_rows(b, i):
        at = sub_rows(b, i)
        two[at] = (dot(gg[at], wg[...], NT) + dot(gu[at], wu[...], NT)).astype(BF16)

    def out_rows(b, i):
        at = sub_rows(b, i)
        one[at] = dot(hidden[at], wd[...]).astype(BF16)

    def send_core(k, b, far):
        ref = (two, one)[k]
        cp = net.remote(ref.at[block_rows(b)], rc.at[k, far], p.core())
        cp.start()
        return cp

    grads(blocks[0], 0, early)
    for cp in n_core:
        cp.wait_recv()
    grads(blocks[1], 0, early)
    for cp in f_x:
        cp.wait_recv()
    for b in blocks[:2]:
        grads(b, early, every)
    to_pair = []
    for h in range(2):
        at = pl.ds(h * sub, sub)
        n_pair[h].wait_recv()
        n_hop[h].start()
        grads(blocks[3], 0, every, h, h + 1)
        n_hop[h].wait_recv()
        grads(blocks[2], 0, every, h, h + 1)
        back_rows(blocks[2], h)
        cp = net.remote(two.at[sub_rows(blocks[2], h)], rc.at[0, 1, at], p.core())
        cp.start()
        back_rows(blocks[3], h)
        cp.wait_recv()
        tot[0, at] = add_refs(two[sub_rows(blocks[3], h)], rc[0, 1, at]).astype(BF16)
        to_pair.append(net.remote(tot.at[0, at], ry.at[at], p.pair()))
        to_pair[h].start()

    def rows_of(f, b):
        def body(i, _):
            f(b, i)
            return 0

        lax.fori_loop(0, 2, body, 0)

    rows_of(back_rows, blocks[1])
    near = [send_core(0, blocks[1], 0)]
    rows_of(back_rows, blocks[0])
    rows_of(out_rows, blocks[2])
    away = send_core(1, blocks[2], 1)
    rows_of(out_rows, blocks[1])
    near.append(send_core(1, blocks[1], 0))
    rows_of(out_rows, blocks[3])
    rows_of(out_rows, blocks[0])
    away.wait_recv()
    tot[1] = add_refs(one[block_rows(blocks[3])], rc[1, 1]).astype(BF16)
    d_x, dx = [], cf // z.X
    stores = []
    for a, b, into, out in ((hidden, seed, wd, p_down), (n2, gg, wg, p_gate), (n2, gu, wu, p_up)):
        for i in range(into.shape[0] // 256):
            at = pl.ds(i * 256, 256)
            into[at] = dot(a[:, at], b[...], TN).astype(BF16)
        if into is wd:
            for i in range(1, z.X):
                for h in range(z.H):
                    far = pl.ds(pl.multiple_of(h * cf + p.xi(i) * dx, 16), dx)
                    d_x.append(net.remote(wd.at[far], rdx.at[i - 1, h], p.xdev(i)))
                    d_x[-1].start()
            continue
        stores.append(net.local(into, out))
        stores[-1].start()
    near[0].wait_recv()
    for cp in to_pair:
        cp.wait_recv()

    def back(i, carry):
        at = part(i, chunk)
        here = pl.ds(pl.multiple_of(blocks[0] * rows + i * chunk, chunk), chunk)
        scaled, inverse = norm_stats(middle[at])
        e = add_refs(two[here], rc[0, 0, at], ry[at])
        m = seed[here].astype(F32) + norm_backward(e, scaled, inverse, gain[...])
        out_f[at] = add_refs(middle[at], one[here], rc[1, 0, at])
        middle[at] = m
        tok[at] = m.astype(BF16)
        return (
            carry[0] + jnp.sum(e * scaled, axis=0, keepdims=True),
            carry[1] + jnp.sum(e, axis=0, keepdims=True),
        )

    near[1].wait_recv()
    zero = jnp.zeros((1, d), F32)
    a, b = lax.fori_loop(0, rows // chunk, back, (zero, zero))
    sums[0:1] = a
    sums[1:2] = b
    net.wait_sends()
    for i in range(d // 256):
        at = pl.ds(i * 256, 256)
        n2[at] = dot(own[:, at], tok[...], TN).astype(BF16)
    for h in range(z.H):
        mine = pl.ds(pl.multiple_of(h * cf + p.x * dx, 16), dx)
        for i in range(1, z.X):
            d_x[(i - 1) * z.H + h].wait_recv()
        wd[mine] = add_refs(wd[mine], *[rdx[i, h] for i in range(z.X - 1)]).astype(BF16)
        stores.append(net.local(wd.at[mine], p_down.at[h]))
        stores[-1].start()
    before = len(stores)
    stores.append(net.local(n2.at[pl.ds(0, d)], p_wo))
    stores.append(net.local(out_f, out_part))
    stores.append(net.local(tot.at[1], out_pair))
    stores.append(net.local(middle, grad_mid))
    for cp in stores[before:]:
        cp.start()
    mixed_at = pl.ds(0, rows)
    two[mixed_at] = dot(tok[...], wo[...], NT).astype(BF16)
    last = net.local(two.at[mixed_at], grad_mix)
    last.start()
    for cp in stores + [last]:
        cp.wait()


def add_refs(*values):
    total = values[0].astype(F32)
    for v in values[1:]:
        total = total + v.astype(F32)
    return total


def lane_of(rows):
    return lax.broadcasted_iota(jnp.int32, (rows, 128), 1)


def rope_tables():
    frequency = np.float32(10000.0) ** (-np.arange(HD // 2, dtype=np.float32) * 2.0 / HD)
    angles = np.arange(WIN, dtype=np.float32)[:, None] * frequency.astype(np.float32)[None, :]
    angles = np.concatenate([angles] * 4, axis=1)
    return np.cos(angles), np.sin(angles)


def turn(v, cosines, sines):
    swapped = jnp.where(
        lane_of(v.shape[0]) % HD < HD // 2, -pltpu.roll(v, 96, 1), pltpu.roll(v, 32, 1)
    )
    return v * cosines + swapped * sines


def spare_lanes(first, v, lane):
    high = v.astype(BF16)
    rest = v - high.astype(F32)
    middle = rest.astype(BF16)
    low = (rest - middle.astype(F32)).astype(BF16)
    s = lane % HD
    tail = jnp.where(s == 2, -middle.astype(F32), jnp.where(s == 3, -low.astype(F32), 0.0))
    return jnp.where(s == 0, first, jnp.where(s == 1, -high.astype(F32), tail))


def run_at(steps, i):
    for at, functions in sorted(steps.items()):

        @pl.when(i == at)
        def _(functions=functions):
            for f in functions:
                f()


def slot_order(p, z):
    half = z.G // 2
    rhi = p.r // 2
    order = [(rhi, p.lo), (rhi, 1 - p.lo)]
    for j in range(1, half):
        order += [((rhi + j) % half, p.lo), ((rhi + j) % half, 1 - p.lo)]
    return [a * 2 + b for a, b in order]


def front_kernel(
    z, tok, gain, beta, w_q, w_k, w_v, cos, sin, bias, wo, wg, wu, wd, cot,
    n1_o, w3_o, q_o, k_o, v_o, o, qa, own, wos, wgs, wus, wds, seed,
    send, recv, lsem, w3s, mixed, n1s, w3c, q, k, v, n1,
):
    p, net = Place(z), Net(send, recv, lsem)
    rq, qc = z.d // z.n_dp, z.d // z.n_dp
    rx, dx, cf = z.d // z.X, z.cf // z.X, z.cf
    half, wide = z.G // 2, z.cw % 128 == 0
    rhi = p.r // 2
    hr = z.rows // 2

    def slot_dev(a, b):
        return (p.dp, p.g * z.G + a * 2 + b)

    def slot_rows(a, b, top):
        return pl.ds(pl.multiple_of((a * 2 + b) * z.rows + top * hr, 16), hr)

    def norm(i, _):
        at = part(i, 128)
        scaled, _ = norm_stats(tok[at].astype(F32))
        n1[at] = (scaled * gain[...] + beta[...]).astype(BF16)
        return 0

    lax.fori_loop(0, z.rows // 128, norm, 0)
    near = [((rhi + j) % half) for j in range(1, half)]
    back = [((rhi + half - j) % half) for j in range(1, half)]
    meet(
        [slot_dev(rhi, 1 - p.lo)]
        + [slot_dev(a, 1 - p.lo) for a in near]
        + [p.hdev(i) for i in range(1, z.H)]
        + [p.xdev(i) for i in range(1, z.X)]
        + [p.core()]
    )
    quarter = part(p.dp, rq)
    w_out = [
        net.remote(ref.at[quarter], w3s.at[p.g, m, quarter], p.gdev(i))
        for i in range(1, z.NG) for m, ref in enumerate((w_q, w_k, w_v))
    ]
    y_out, a_out = [], []
    for top in (1, 0):
        y_out.append(
            net.remote(n1.at[pl.ds(top * hr, hr)], n1s.at[slot_rows(rhi, p.lo, top)],
                       slot_dev(rhi, 1 - p.lo))
        )
    for top in (0, 1):
        a_out.append(
            [
                net.remote(n1.at[pl.ds(top * hr, hr)], n1s.at[slot_rows(rhi, p.lo, top)],
                           slot_dev(a, p.lo))
                for a in near
            ]
        )
    def wo_rows(t):
        return part((t % z.G) * z.NG + t // z.G, z.cw)

    cols = part(p.dp, qc)
    own_o = wos.at[wo_rows(p.t), cols]
    o_out = [net.remote(wo.at[:, cols], own_o, p.hdev(i)) for i in range(1, z.H)]
    o_keep = net.local(wo.at[:, cols], own_o)
    o_hop = [net.remote(own_o, own_o, p.y())]
    for i in range(1, z.H):
        block = wos.at[wo_rows(((p.hi + z.H - i) % z.H) * 2 + p.lo), cols]
        o_hop.append(net.remote(block, block, p.y()))
    block = wos.at[:, cols]
    o_along = [net.remote(block, block, p.xdev(i)) for i in range(1, z.X)]
    o_across = []
    for x in range(z.X):
        block = wos.at[:, part(x * 2 + p.c, qc)]
        o_across.append(net.remote(block, block, p.core()))

    def pieces(h2, lo):
        k, x = lo * (z.H // 2) + h2, p.x
        return (
            wgs.at[part(x, rx), part(k, cf)],
            wus.at[part(x, rx), part(k, cf)],
            wds.at[pl.ds(pl.multiple_of(k * cf + x * dx, 16), dx)],
        )

    src = (
        wg.at[part(p.x, rx), part(p.c, cf)],
        wu.at[part(p.x, rx), part(p.c, cf)],
        wd.at[pl.ds(pl.multiple_of(p.c * cf + p.x * dx, 16), dx)],
    )
    h2n = z.H // 2

    def to(refs, into, device):
        return [net.remote(a, b, device) for a, b in zip(refs, into)]

    def all_x(refs):
        return [cp for m in range(1, z.X) for cp in to(refs, refs, p.xdev(m))]

    f_z = [to(src, pieces(h2n - i, 0), p.h2dev(i)) for i in range(1, h2n)]
    f_y = [to(src, pieces(0, 1), p.y())]
    f_y += [to(pieces(h2n - i, 0), pieces(h2n - i, 1), p.y()) for i in range(1, h2n)]
    f_x = [all_x(pieces(0, 1))]
    f_xz = [all_x(pieces(h2n - i, 0)) for i in range(1, h2n)]
    mine = seed.at[p.hl * 2 + p.c]
    other = seed.at[(1 - p.hl) * 2 + p.c]
    s_y, s_core = net.remote(cot, mine, p.pair()), net.remote(cot, mine, p.core())
    s_hop = net.remote(other, other, p.core())

    keep_w = [net.local(ref, w3s.at[p.g, m]) for m, ref in enumerate((w_q, w_k, w_v))]
    keep_n = net.local(n1, n1s.at[part(p.r, z.rows)])
    o_keep.start()
    for cp in w_out + o_out:
        cp.start()
    y_out[0].start()
    for cp in a_out[0]:
        cp.start()
    for cp in keep_w:
        cp.start()
    keep_n.start()
    y_out[1].start()
    for cp in a_out[1]:
        cp.start()
    for cp in w_out:
        cp.wait_recv()
    w_back = [(p.g + z.NG - i) % z.NG for i in range(1, z.NG)]
    along = []
    for g in w_back:
        block = w3s.at[g, :, quarter]
        along += [net.remote(block, block, p.xdev(i)) for i in range(1, z.X)]
    for cp in along:
        cp.start()
    o_keep.wait()
    o_hop[0].start()
    for i in range(1, z.H):
        o_out[i - 1].wait_recv()
        o_hop[i].start()
    for cp in along:
        cp.wait_recv()
    across = []
    for g in w_back:
        for x in range(z.X):
            block = w3s.at[g, :, part(x * 2 + p.c, rq)]
            across.append(net.remote(block, block, p.core()))
            across[-1].start()
    y_out[0].wait_recv()
    hop_a = []
    block = n1s.at[slot_rows(rhi, 1 - p.lo, 1)]
    hop_a = [net.remote(block, block, slot_dev(a, p.lo)) for a in near]
    for cp in hop_a:
        cp.start()
    hop_y = []
    for j, a in enumerate(back):
        a_out[0][j].wait_recv()
        block = n1s.at[slot_rows(a, p.lo, 0)]
        hop_y.append(net.remote(block, block, slot_dev(rhi, 1 - p.lo)))
        hop_y[-1].start()
    for cp in across:
        cp.wait_recv()
    for cp in o_hop:
        cp.wait_recv()
    for cp in o_along:
        cp.start()
    for cp in keep_w:
        cp.wait()
    keep_n.wait()
    for m in range(3):
        if wide:
            for g in range(z.NG):
                w3c[m, :, g * z.cw : (g + 1) * z.cw] = w3s[g, m]
        else:
            w3c[m] = add_refs(*[w3s[g, m] for g in range(z.NG)]).astype(BF16)

    def start(*copies):
        def f():
            for cp in copies:
                cp.start()
        return f

    def arrive(*copies):
        def f():
            for cp in copies:
                cp.wait_recv()
        return f

    width = q.shape[1]
    pairs, bq = width // 128, min(256, z.rows)
    per = z.rows // bq
    blocks = WIN // bq
    total = pairs * blocks
    steps = {}

    def at(i, *functions):
        steps.setdefault(min(i, total - 1), []).extend(functions)

    at(0, arrive(*o_along), start(*o_across))
    for m in range(3):
        at(3 + m, arrive(f_y[0][m]), start(*f_x[0][m::3]))
        for i in range(h2n - 1):
            at(7 + m, arrive(f_z[i][m]), start(f_y[i + 1][m], *f_xz[i][m::3]))
    at(0, start(s_core, s_y))
    at(total - 1, arrive(s_y), start(s_hop))

    order = slot_order(p, z)

    def project(r):
        rows = part(r, z.rows)
        a = n1s[rows]
        for m, ref in enumerate((q, k, v)):
            y = dot(a, w3c[m])
            for j in range(width // 128):
                t = y[:, j * 128 : j * 128 + 128]
                if m < 2:
                    t = turn(t, cos[rows], sin[rows])
                ref[rows, j * 128 : j * 128 + 128] = t.astype(BF16)

    project(order[0])
    y_out[1].wait_recv()
    for group in f_y[:1] + f_z:
        for cp in group:
            cp.start()
    project(order[1])
    for j in range(half - 1):
        a_out[1][j].wait_recv()
        hop_a[j].wait_recv()
        hop_y[j].wait_recv()
    for r in order[2:]:
        project(r)
    stores = [net.local(a, b) for a, b in (
        (n1s, n1_o), (w3c, w3_o), (q, q_o), (k, k_o), (v, v_o)
    )]
    for cp in stores:
        cp.start()
    lane_k, lane_q = lane_of(WIN), lane_of(bq)

    m_out = {}
    for j in range(pairs):
        for i in range(1, z.G):
            col = pl.ds(pl.multiple_of(p.r * z.hw + j * 128, 128), 128)
            cp = net.remote(
                mixed.at[part(p.ri(i), z.rows), j * 128 : j * 128 + 128],
                own.at[:, col], p.rdev(i),
            )
            m_out[j, i] = cp
            at(j * blocks + i * per - 1, start(cp))

    def block(i, _):
        j, b = i // blocks, i % blocks
        row = ((p.r + 1 + b // per) % z.G) * z.rows + (b % per) * bq
        col, rows = part(j, 128), pl.ds(pl.multiple_of(row, bq), bq)
        k2, v2, kb, q2 = k[:, col], v[:, col], bias[...], q[rows, col]
        mixes = []
        for e in range(2):
            own_k = (lane_k < HD) if e == 0 else (lane_k >= HD)
            own_q = (lane_q < HD) if e == 0 else (lane_q >= HD)
            k_e = jnp.where(own_k, k2, kb)
            v_e = jnp.where(own_k, v2, jnp.ones_like(v2))
            q_e = jnp.where(own_q, q2, jnp.where(lane_q % HD == 0, 1.0, 0.0).astype(BF16))
            s = dot(q_e, k_e, NT)
            top = jnp.max(s, axis=1, keepdims=True)
            prob = jnp.exp2((s - top) * C2).astype(BF16)
            sums = dot(prob, v_e)
            mixes.append(sums / pltpu.roll(sums, HD, 1))
            norm = jnp.where(own_q, 0.0, top + jnp.log2(jnp.where(own_q, 1.0, sums)) * (1.0 / C2))
            full = jnp.where(own_q, q2.astype(F32), spare_lanes(1.0, norm, lane_q))
            qa[2 * j + e, rows] = full.astype(BF16)
        mix = jnp.where(lane_q < HD, mixes[0], mixes[1])
        o[rows, col] = mix
        mixed[rows, col] = mix.astype(BF16)
        run_at(steps, i)
        return 0

    lax.fori_loop(0, total, block, 0)
    m_keep = net.local(mixed.at[part(p.r, z.rows)], own.at[:, part(p.r, z.hw)])
    m_keep.start()
    for cp in list(m_out.values()) + o_across + [s_core]:
        cp.wait_recv()
    for group in f_x + f_xz + f_y[1:]:
        for cp in group:
            cp.wait_recv()
    s_hop.wait_recv()
    for cp in stores + [m_keep]:
        cp.wait()
    net.wait_sends()


def back_kernel(
    z, gm, qa_h, q_h, k_h, v_h, o_h, w3_h, n1_h, dg, du, dd, do_w, out_pair, bias, cos, sin,
    got, out_got, og, ou, od, ow, oo,
    send, recv, lsem,
    qa, q, k, v, o, do, dq, dk, dv, do_e, dk_sum, dv_sum, w3, n1, part_one, p3,
    rgx, rux, sg, su, sd, rgy, ruy, rdy, rgz, ruz, rdz,
    oc, so, ox, oy, oz, wc, sw, wx, wgr, join_y, join_z,
):
    p, net = Place(z), Net(send, recv, lsem)
    d, rows = z.d, z.rows
    rq, rx, dx, cf, h2n = d // z.n_dp, d // z.X, z.cf // z.X, z.cf, z.H // 2
    width = q.shape[1]
    bq = min(512, rows)
    per, blocks, pairs = rows // bq, WIN // bq, width // 128
    total = pairs * blocks
    loads = [net.local(a, b) for a, b in (
        (qa_h, qa), (q_h, q), (k_h, k), (v_h, v), (o_h, o),
        (gm.at[:, part(p.r, z.hw)], do.at[part(p.r, rows)]),
    )]
    late = [net.local(a, b) for a, b in (
        (dd, sd), (dg.at[part(p.x, rx)], sg),
        *[(do_w.at[:, :, part(x * 2 + p.c, rq)], so.at[x]) for x in range(z.X)],
        (w3_h, w3), (n1_h, n1),
    )]
    for cp in loads + late:
        cp.start()
    meet(
        [p.rdev(i) for i in range(1, z.G)]
        + [p.hdev(i) for i in range(1, z.H)]
        + [p.xdev(i) for i in range(1, z.X)]
        + [p.core()]
    )

    def start(*copies):
        def f():
            for cp in copies:
                cp.start()
        return f

    def arrive(*copies):
        def f():
            for cp in copies:
                cp.wait_recv()
        return f

    steps = {}

    def at(i, *functions):
        steps.setdefault(min(i, total - 1), []).extend(functions)

    dest = do.at[part(p.r, rows)]
    a_out = [net.remote(gm.at[:, part(p.ri(i), z.hw)], dest, p.rdev(i)) for i in range(1, z.G)]
    for cp in a_out:
        cp.start()
    def spot(h2, lo):
        return ((lo + p.lo) % 2) * h2n + (h2 + h2n - p.h2) % h2n

    bufs = ((dd, None, sd, rdy, rdz, od), (dg, rgx, sg, rgy, rgz, og), (du, rux, su, ruy, ruz, ou))

    def piece(m, ref, s):
        return ref.at[s] if m == 0 else ref.at[:, part(s, cf)]

    fx = [[net.remote(bufs[m][0].at[part(p.xi(i), rx)], bufs[m][1].at[i - 1], p.xdev(i))
           for i in range(1, z.X) if m == 1] for m in range(2)]
    fy = [[net.remote(piece(m, bufs[m][2], spot(h2, 1 - p.lo)), bufs[m][3].at[h2], p.y())
           for h2 in range(h2n)] for m in range(2)]
    fz = [[net.remote(piece(m, bufs[m][2], spot((p.h2 + i) % h2n, p.lo)), bufs[m][4].at[i - 1],
                      p.h2dev(i)) for i in range(1, h2n)] for m in range(2)]
    up_y = [net.remote(du.at[:, part(spot(h2, 1 - p.lo), cf)], ruy.at[h2], p.y())
            for h2 in range(h2n)]
    up_own = [net.local(du.at[:, part(spot(h2, p.lo), cf)], su.at[h2]) for h2 in range(h2n)]
    up_x = [net.remote(su.at[:, part(p.xi(i), rx)], rux.at[i - 1], p.xdev(i))
            for i in range(1, z.X)]
    up_z = [net.remote(su.at[(p.h2 + i) % h2n, part(p.x, rx)], ruz.at[i - 1], p.h2dev(i))
            for i in range(1, h2n)]

    def up_y_in():
        for h2 in range(h2n):
            up_own[h2].wait()
            up_y[h2].wait_recv()
            su[h2] = add_refs(su[h2], ruy[h2]).astype(BF16)
        start(*up_x)()

    def up_x_in():
        arrive(*up_x)()
        for h2 in range(h2n):
            su[h2, part(p.x, rx)] = add_refs(
                su[h2, part(p.x, rx)], *[rux[i, h2] for i in range(z.X - 1)]
            ).astype(BF16)
        start(*up_z)()

    def up_z_in():
        arrive(*up_z)()
        ou[done_at[2]] = add_refs(
            su[p.h2, part(p.x, rx)], *[ruz[i] for i in range(h2n - 1)]
        ).astype(BF16)
        start(*fa[2])()
    done_at = [
        (pl.ds(pl.multiple_of(p.c * cf + p.x * dx, 16), dx),),
        (part(p.x, rx), part(p.c, cf)),
        (part(p.x, rx), part(p.c, cf)),
    ]
    fa, fc = [], []
    for m in range(3):
        block = bufs[m][5].at[done_at[m]]
        fa.append([net.remote(block, block, p.xdev(i)) for i in range(1, z.X)])
        block = od.at[part(p.c, cf)] if m == 0 else bufs[m][5].at[:, part(p.c, cf)]
        fc.append(net.remote(block, block, p.core()))

    def ffn_x(m):
        def f():
            arrive(*fx[m])()
            late[m].wait()
            got_x, own = bufs[m][1], bufs[m][2]
            for h in range(2 * h2n):
                c = pl.ds(h * cf, cf)
                own[:, c] = add_refs(
                    own[:, c], *[got_x[i, :, c] for i in range(z.X - 1)]
                ).astype(BF16)
            start(*fy[m])()
        return f

    def ffn_y(m):
        def f():
            arrive(*fy[m])()
            own, got_y = bufs[m][2], bufs[m][3]
            for h2 in range(h2n):
                if m == 0:
                    own[spot(h2, p.lo)] = add_refs(own[spot(h2, p.lo)], got_y[h2]).astype(BF16)
                else:
                    c = part(spot(h2, p.lo), cf)
                    own[:, c] = add_refs(own[:, c], got_y[h2]).astype(BF16)
            start(*fz[m])()
        return f

    def ffn_z(m):
        def f():
            arrive(*fz[m])()
            own, got_z, out = bufs[m][2], bufs[m][4], bufs[m][5]
            s = spot(p.h2, p.lo)
            mine = own[s] if m == 0 else own[:, part(s, cf)]
            out[done_at[m]] = add_refs(mine, *[got_z[i] for i in range(h2n - 1)]).astype(BF16)
            start(*fa[m])()
        return f

    def ffn_c(m):
        def f():
            arrive(*fa[m])()
            fc[m].start()
        return f

    half = z.G // 2
    c_out = [net.remote(do_w.at[:, :, part(p.xi(i) * 2 + 1 - p.c, rq)], oc.at[i], p.core())
             for i in range(z.X)]
    c_x = [net.remote(so.at[p.xi(i)], ox.at[i - 1], p.xdev(i)) for i in range(1, z.X)]
    c_y = [net.remote(so.at[p.x, i * 2 + 1 - p.lo], oy.at[i], p.y()) for i in range(half)]
    c_z = [net.remote(so.at[p.x, (p.hii(i) % half) * 2 + p.lo, part(p.hii(i) // half, z.cw)],
                      oz.at[i - 1], p.hdev(i)) for i in range(1, z.H)]
    cols = part(p.dp, rq)
    block = oo.at[:, cols]
    c_a = [net.remote(block, block, p.xdev(i)) for i in range(1, z.X)]
    c_c = []
    for x in range(z.X):
        block = oo.at[:, part(x * 2 + p.c, rq)]
        c_c.append(net.remote(block, block, p.core()))

    def wo_c():
        for cp in late[2 : 2 + z.X]:
            cp.wait()
        for i in list(range(1, z.X)) + [0]:
            c_out[i].wait_recv()
            for r in range(z.G):
                so[p.xi(i), r] = add_refs(so[p.xi(i), r], oc[i, r]).astype(BF16)
        start(*c_x)()

    def wo_x():
        arrive(*c_x)()
        for r in range(z.G):
            so[p.x, r] = add_refs(so[p.x, r], *[ox[i, r] for i in range(z.X - 1)]).astype(BF16)
        start(*c_y)()

    def wo_y():
        arrive(*c_y)()
        for i in range(half):
            r = i * 2 + p.lo
            so[p.x, r] = add_refs(so[p.x, r], oy[i]).astype(BF16)
        start(*c_z)()

    def wo_z():
        arrive(*c_z)()
        mine = so[p.x, (p.hi % half) * 2 + p.lo, part(p.hi // half, z.cw)]
        oo[:, cols] = add_refs(mine, *[oz[i] for i in range(z.H - 1)]).astype(BF16)
        start(*c_a)()

    def wo_a():
        arrive(*c_a)()
        start(*c_c)()

    o_send = net.remote(out_pair, out_got, p.pair())
    start(*fx[1], *c_out)()
    late[0].wait()
    start(*fy[0], *up_y, *up_own)()
    at(0, start(o_send))
    at(1, ffn_y(0))
    at(2, wo_c)
    at(3, ffn_x(1))
    at(4, ffn_z(0), up_y_in)
    at(5, ffn_y(1), wo_x)
    at(6, up_x_in, ffn_c(0))
    at(7, ffn_z(1))

    for cp in loads:
        cp.wait()
    lane_q, sub = lane_of(bq), 1024
    lane_k = lane_of(sub)
    s64 = lane_k % HD
    ones3 = jnp.where((s64 >= 1) & (s64 <= 3), 1.0, 0.0).astype(BF16)

    def block_step(i, _):
        j, b = i // blocks, i % blocks
        for n in range(1, z.G):

            @pl.when((j == 0) & (b == n * per))
            def _():
                a_out[z.G - 1 - n].wait_recv()

        row = ((p.r + b // per) % z.G) * rows + (b % per) * bq
        col, at_q = part(j, 128), pl.ds(pl.multiple_of(row, bq), bq)
        q2, do2 = q[at_q, col], do[at_q, col]
        prod = do2.astype(F32) * o[at_q, col]
        for e in range(2):
            own_q = (lane_q < HD) if e == 0 else (lane_q >= HD)
            delta = jnp.sum(jnp.where(own_q, prod, 0.0), axis=1, keepdims=True)
            spare = spare_lanes(0.0, jnp.broadcast_to(delta, prod.shape), lane_q)
            do_e[e] = jnp.where(own_q, do2.astype(F32), spare).astype(BF16)
        dqs = [jnp.zeros((bq, 128), F32)] * 2
        for s in range(WIN // sub):
            keys = pl.ds(s * sub, sub)
            k2, v2 = k[keys, col], v[keys, col]
            kb = bias[keys] + ones3
            dks, dvs = [], []
            for e in range(2):
                own_k = (lane_k < HD) if e == 0 else (lane_k >= HD)
                k_e = jnp.where(own_k, k2, kb)
                v_e = jnp.where(own_k, v2, ones3)
                prob = jnp.exp2(dot(k_e, qa[2 * j + e, at_q], NT) * C2)
                ds = (prob * dot(v_e, do_e[e], NT)).astype(BF16)
                dvs.append(dot(prob.astype(BF16), do2))
                dks.append(dot(ds, q2))
                dqs[e] = dqs[e] + dot(ds, k2, TN)
            dv_new = jnp.where(lane_k < HD, dvs[0], dvs[1])
            dk_new = jnp.where(lane_k < HD, dks[0], dks[1])

            @pl.when(b == 0)
            def _():
                dv_sum[keys] = dv_new
                dk_sum[keys] = dk_new

            @pl.when(b > 0)
            def _():
                dv_sum[keys] += dv_new
                dk_sum[keys] += dk_new

        dq_new = jnp.where(lane_q < HD, dqs[0], dqs[1]) * SCALE
        dq[at_q, col] = turn(dq_new, cos[at_q], -sin[at_q]).astype(BF16)

        @pl.when(b == blocks - 1)
        def _():
            dv[:, col] = dv_sum[...].astype(BF16)
            dk[:, col] = turn(dk_sum[...] * SCALE, cos[...], -sin[...]).astype(BF16)

        run_at(steps, i)
        return 0

    lax.fori_loop(0, total, block_step, 0)

    for cp in late[2 + z.X :]:
        cp.wait()
    half, hr, rhi = z.G // 2, rows // 2, p.r // 2
    near = [(rhi + j) % half for j in range(1, half)]

    def slot_dev(a, b):
        return (p.dp, p.g * z.G + a * 2 + b)

    def top(a, b, h):
        return pl.ds(pl.multiple_of((a * 2 + b) * rows + h * hr, 16), hr)

    def rows_one(a, b):
        here = part(a * 2 + b, rows)
        part_one[here] = (
            dot(dq[here], w3[0], NT) + dot(dk[here], w3[1], NT) + dot(dv[here], w3[2], NT)
        ).astype(BF16)

    y_dev = slot_dev(rhi, 1 - p.lo)
    r_y, r_z = [], []
    for j, a in enumerate(near):
        rows_one(a, 1 - p.lo)
        r_y.append(net.remote(part_one.at[top(a, 1 - p.lo, 0)], join_y.at[j], y_dev))
        r_z.append(net.remote(part_one.at[top(a, 1 - p.lo, 1)], join_z.at[j], slot_dev(a, p.lo)))
        start(r_y[j], r_z[j])()
    rows_one(rhi, 1 - p.lo)
    g_y = [net.remote(part_one.at[top(rhi, 1 - p.lo, h)], got.at[0, pl.ds(h * hr, hr)], y_dev)
           for h in range(2)]
    g_y[0].start()
    g_z = []
    for j, a in enumerate(near):
        rows_one(a, p.lo)
        g_z.append([net.remote(part_one.at[top(a, p.lo, h)], got.at[1 + j, pl.ds(h * hr, hr)],
                               slot_dev(a, p.lo)) for h in range(2)])
        g_z[j][1].start()
    rows_one(rhi, p.lo)
    r_keep = net.local(part_one.at[part(p.r, rows)], got.at[half])
    r_keep.start()

    def join():
        arrive(*r_z)()
        here = top(rhi, 1 - p.lo, 1)
        part_one[here] = add_refs(
            part_one[here], *[join_z[j] for j in range(half - 1)]
        ).astype(BF16)
        g_y[1].start()
        for j, a in enumerate(near):
            r_y[j].wait_recv()
            here = top(a, p.lo, 0)
            part_one[here] = add_refs(part_one[here], join_y[j]).astype(BF16)
            g_z[j][0].start()

    for m, t in enumerate((dq, dk, dv)):
        y = dot(n1[...], t[...], TN).astype(BF16)
        for g in range(z.NG):
            p3[g, m] = y[:, g * z.cw : (g + 1) * z.cw]
    w_c = [net.remote(p3.at[:, :, part(p.xi(i) * 2 + 1 - p.c, rq)], wc.at[i], p.core())
           for i in range(z.X)]
    start(*w_c)()
    wo_y()
    w_x = []
    for i in list(range(1, z.X)) + [0]:
        w_c[i].wait_recv()
        for g in range(z.NG):
            sw[i, g] = add_refs(p3[g, :, part(p.xi(i) * 2 + p.c, rq)], wc[i, g]).astype(BF16)
        if i:
            w_x.append(net.remote(sw.at[i], wx.at[i - 1], p.xdev(i)))
            w_x[-1].start()
    join()
    ffn_c(1)()
    wo_z()
    up_z_in()
    arrive(*w_x)()
    for g in range(z.NG):
        sw[0, g] = add_refs(sw[0, g], *[wx[i, g] for i in range(z.X - 1)]).astype(BF16)
    w_g = [net.remote(sw.at[0, p.gi(i)], wgr.at[i - 1], p.gdev(i)) for i in range(1, z.NG)]
    start(*w_g)()
    wo_a()
    ffn_c(2)()
    arrive(*w_g)()
    quarter = part(p.dp, rq)
    for m in range(3):
        ow[m, quarter] = add_refs(
            sw[0, p.g, m], *[wgr[i, m] for i in range(z.NG - 1)]
        ).astype(BF16)
    block = ow.at[:, quarter]
    w_a = [net.remote(block, block, p.xdev(i)) for i in range(1, z.X)]
    start(*w_a)()
    arrive(*w_a)()
    w_last = []
    for x in range(z.X):
        block = ow.at[:, part(x * 2 + p.c, rq)]
        w_last.append(net.remote(block, block, p.core()))
        w_last[-1].start()
    arrive(*c_c, *fc, *w_last, o_send, *g_y, *[cp for pair in g_z for cp in pair])()
    r_keep.wait()
    net.wait_sends()


def finish_kernel(
    z, got, tok, gain, sums_two, gm_h, part_h, far_h, grad_tok, output, norms,
    send, recv, lsem, gm, part_f, far_one, tok_out, out_low, t_sums, d_sums,
):
    p, net = Place(z), Net(send, recv, lsem)
    rows, d, chunk = z.rows, z.d, 128
    loads = [net.local(a, b) for a, b in ((gm_h, gm), (part_h, part_f), (far_h, far_one))]
    for cp in loads:
        cp.start()
    t_dev = [(p.dp, (p.t + i) % z.n_t) for i in range(1, z.n_t)]
    d_dev = [((p.dp + i) % z.n_dp, p.t) for i in range(1, z.n_dp)]
    meet(t_dev + d_dev)

    def rows_in(at):
        scaled, inverse = norm_stats(tok[at].astype(F32))
        return add_refs(*[got[i, at] for i in range(got.shape[0])]), scaled, inverse

    def sums(i, carry):
        e, scaled, _ = rows_in(part(i, chunk))
        return (
            carry[0] + jnp.sum(e * scaled, axis=0, keepdims=True),
            carry[1] + jnp.sum(e, axis=0, keepdims=True),
        )

    zero = jnp.zeros((1, d), F32)
    a, b = lax.fori_loop(0, rows // chunk, sums, (zero, zero))
    t_sums[p.t, 0:1] = a
    t_sums[p.t, 1:2] = b
    t_sums[p.t, 2:4] = sums_two[...]
    own = t_sums.at[p.t]
    first = [net.remote(own, own, dev) for dev in t_dev]
    for cp in first:
        cp.start()
    stores = []

    def store(src, dst):
        stores.append(net.local(src, dst))
        stores[-1].start()

    loads[0].wait()

    def back(i, _):
        at = part(i, chunk)
        e, scaled, inverse = rows_in(at)
        tok_out[at] = (gm[at] + norm_backward(e, scaled, inverse, gain[...])).astype(BF16)
        return 0

    lax.fori_loop(0, rows // chunk, back, 0)
    store(tok_out, grad_tok)
    for cp in first:
        cp.wait_recv()
    d_sums[p.dp] = add_refs(*[t_sums[i] for i in range(z.n_t)])
    own = d_sums.at[p.dp]
    second = [net.remote(own, own, dev) for dev in d_dev]
    for cp in second:
        cp.start()
    for cp in loads[1:]:
        cp.wait()
    out_low[...] = (part_f[...] + far_one[...].astype(F32)).astype(BF16)
    store(out_low, output)
    for cp in second:
        cp.wait_recv()
    norms[...] = add_refs(*[d_sums[i] for i in range(z.n_dp)])
    for cp in stores:
        cp.wait()
    net.wait_sends()


def norm_stats(v):
    centre = v - jnp.mean(v, axis=-1, keepdims=True)
    inverse = lax.rsqrt(jnp.mean(centre * centre, axis=-1, keepdims=True) + EPSILON)
    return centre * inverse, inverse


def norm_backward(grad_in, scaled, inverse, gain):
    weighted = grad_in * gain
    first_mean = jnp.mean(weighted, axis=-1, keepdims=True)
    second_mean = jnp.mean(weighted * scaled, axis=-1, keepdims=True)
    return inverse * (weighted - first_mean - scaled * second_mean)


def per_device(
    n_dp, n_t, tokens, lengths, ln1_gain, ln1_bias, w_query, w_key, w_value, w_out,
    ln2_gain, ln2_bias, w_gate, w_up, w_down, cotangent,
):
    rows, d = tokens.shape
    cw, cfull = w_query.shape[1], w_gate.shape[1]
    z = Sizes(n_dp, n_t, rows, d, cw, cfull)
    G, NG, H, X, hw, cf = z.G, z.NG, z.H, z.X, z.hw, z.cf
    rq, rx, dx = d // n_dp, d // X, cf // X
    slot = lax.axis_index("tensor") // G
    length = lax.dynamic_index_in_dim(lengths, slot, keepdims=False)
    lane = lax.broadcasted_iota(jnp.int32, (WIN, 128), 1) % HD
    place = lax.broadcasted_iota(jnp.int32, (WIN, 128), 0)
    bias = jnp.where((lane == 0) & (place >= length), -1e30, 0.0).astype(BF16)
    cos, sin = (jnp.asarray(t, F32) for t in rope_tables())

    w_three = [w_query, w_key, w_value]
    if cw % 128:
        wider = jnp.zeros((d, hw), BF16)
        w_three = [lax.dynamic_update_slice(wider, w, (0, slot * cw)) for w in w_three]
    n1, w3, q, k, v, o, qa, mixed_own, wo, wg, wu, wd, seed = comm_call(
        front_kernel, z, "front", 1,
        (
            shape((WIN, d)), shape((3, d, hw)), shape((WIN, hw)), shape((WIN, hw)),
            shape((WIN, hw)), shape((WIN, hw), F32), shape((hw // HD, WIN, 128)),
            shape((rows, d)), shape((d, d)), shape((d, H * cf)), shape((d, H * cf)),
            shape((H * cf, d)), shape((4, rows, d)),
        ),
        [VMEM] * 3 + [HBM] * 3 + [VMEM] * 3 + [HBM] * 5,
        [HBM] * 5 + [VMEM] * 4 + [HBM] * 4,
        [
            pltpu.VMEM((NG, 3) + w_three[0].shape, BF16), pltpu.VMEM((WIN, hw), BF16),
            pltpu.VMEM((WIN, d), BF16), pltpu.VMEM((3, d, hw), BF16),
            *[pltpu.VMEM((WIN, hw), BF16)] * 3, pltpu.VMEM((rows, d), BF16),
        ],
        n=160, vmem=60 * MIB,
    )(
        tokens, ln1_gain.reshape(1, d), ln1_bias.reshape(1, d), *w_three, cos, sin, bias,
        w_out, w_gate, w_up, w_down, cotangent,
    )
    every = 4 * rows
    width = H * cf
    mid_out = (
        shape((rows, d), F32), shape((rows, d)), shape((rows, d), F32), shape((rows, d)),
        shape((d, d)), shape((d, width)), shape((d, width)), shape((H, dx, d)), shape((2, d), F32),
    )
    out_part, out_pair, grad_middle, grad_mixed, p_wo, p_gate, p_up, p_down, sums_two = comm_call(
        middle_kernel, z, "middle", 4, mid_out,
        [HBM] * 11 + [VMEM] * 2, [HBM] * 8 + [VMEM],
        [
            pltpu.VMEM((rows, d), BF16), pltpu.VMEM((rows, d), BF16), pltpu.VMEM((d, d), BF16),
            pltpu.VMEM((d, width), BF16), pltpu.VMEM((d, width), BF16),
            pltpu.VMEM((width, d), BF16), pltpu.VMEM((every, d), BF16),
            pltpu.VMEM((every, d), BF16), pltpu.VMEM((rows, d), F32),
            pltpu.VMEM((every, width), BF16), pltpu.VMEM((every, width), BF16),
            pltpu.VMEM((every, width), BF16), pltpu.VMEM((every, d), BF16),
            pltpu.VMEM((every, d), BF16), pltpu.VMEM((2, 2, rows, d), BF16),
            pltpu.VMEM((rows, d), BF16), pltpu.VMEM((2, rows, d), BF16),
            pltpu.VMEM((rows, d), F32), pltpu.VMEM((X - 1, H, dx, d), BF16),
        ],
        vmem=62 * MIB,
    )(
        mixed_own, tokens, wo, wg, wu, wd, w_gate, w_up, w_down, seed.reshape(every, d), cotangent,
        ln2_gain.reshape(1, d), ln2_bias.reshape(1, d),
    )
    p_wo = p_wo.reshape(G, hw, d)
    V = pltpu.VMEM
    pieces = ((rx, cf), (rx, cf), (dx, d))
    got, out_got, g_gate, g_up, g_down, g_w3, g_wo = comm_call(
        back_kernel, z, "back", 8,
        (
            shape((G // 2 + 1, rows, d)), shape((rows, d)), shape((d, 2 * cf)), shape((d, 2 * cf)),
            shape((2 * cf, d)), shape((3, d, cw)), shape((cw, d)),
        ),
        [HBM] * 13 + [VMEM] * 3, [HBM] * 2 + [VMEM] * 5,
        [
            V((hw // HD, WIN, 128), BF16), V((WIN, hw), BF16), V((WIN, hw), BF16),
            V((WIN, hw), BF16), V((WIN, hw), F32), V((WIN, hw), BF16), V((WIN, hw), BF16),
            V((WIN, hw), BF16), V((WIN, hw), BF16), V((2, min(512, rows), 128), BF16),
            V((WIN, 128), F32), V((WIN, 128), F32), V((3, d, hw), BF16), V((WIN, d), BF16),
            V((WIN, d), BF16), V((NG, 3, d, cw), BF16),
            V((X - 1, rx, width), BF16), V((X - 1, H // 2, rx, cf), BF16),
            V((rx, width), BF16), V((H // 2, d, cf), BF16), V((H, dx, d), BF16),
            *[V((H // 2,) + dims, BF16) for dims in ((rx, cf), (d, cf), (dx, d))],
            *[V((H // 2 - 1,) + dims, BF16) for dims in pieces],
            V((X, G, hw, rq), BF16), V((X, G, hw, rq), BF16), V((X - 1, G, hw, rq), BF16),
            V((G // 2, hw, rq), BF16), V((H - 1, cw, rq), BF16),
            V((X, NG, 3, rq, cw), BF16), V((X, NG, 3, rq, cw), BF16),
            V((X - 1, NG, 3, rq, cw), BF16), V((NG - 1, 3, rq, cw), BF16),
            *[V((G // 2 - 1, rows // 2, d), BF16)] * 2,
        ],
        n=160, vmem=62 * MIB,
    )(
        grad_mixed, qa, q, k, v, o, w3, n1, p_gate, p_up, p_down, p_wo, out_pair, bias, cos, sin,
    )
    grad_tokens, output, norms = comm_call(
        finish_kernel, z, "finish", 9,
        (shape((rows, d)), shape((rows, d)), shape((4, d), F32)),
        [VMEM] * 4 + [HBM] * 3, [HBM] * 2 + [VMEM],
        [
            V((rows, d), F32), V((rows, d), F32), V((rows, d), BF16), V((rows, d), BF16),
            V((rows, d), BF16), V((n_t, 4, d), F32), V((n_dp, 4, d), F32),
        ],
        vmem=62 * MIB,
    )(got, tokens, ln1_gain.reshape(1, d), sums_two, grad_middle, out_part, out_got)
    return (
        output, grad_tokens, norms[0], norms[1],
        g_w3[0].astype(F32), g_w3[1].astype(F32), g_w3[2].astype(F32), g_wo.astype(F32),
        norms[2], norms[3], g_gate.astype(F32), g_up.astype(F32), g_down.astype(F32),
    )


def solution(mesh):
    rows, cols, each = P(("dp", "tensor"), None), P(None, "tensor"), P("tensor", None)
    return jax.shard_map(
        functools.partial(per_device, mesh.shape["dp"], mesh.shape["tensor"]),
        mesh=mesh,
        in_specs=(
            rows, P("dp"), P(), P(), cols, cols, cols, each, P(), P(), cols, cols, each, rows,
        ),
        out_specs=(
            rows, rows, P(), P(), cols, cols, cols, each, P(), P(), cols, cols, each,
        ),
        check_vma=False,
    )
```

```python
import functools

import jax
import jax.numpy as jnp
import numpy as np
from jax import lax
from jax.experimental import pallas as pl
from jax.experimental.pallas import tpu as pltpu
from jax.sharding import PartitionSpec as P

HD = 64
WIN = 2048
EPSILON = 1e-05
SCALE = HD ** (-0.5)
LOG2E = 1.4426950408889634
C2 = SCALE * LOG2E
NT = (((1,), (1,)), ((), ()))
NN = (((1,), (0,)), ((), ()))
TN = (((0,), (0,)), ((), ()))
MESH = pl.DeviceIdType.MESH
F32 = jnp.float32
BF16 = jnp.bfloat16
MIB = 1024 * 1024
HBM = pl.BlockSpec(memory_space=pl.ANY)
VMEM = pl.BlockSpec(memory_space=pltpu.VMEM)


def dot(a, b, dims=NN):
    return lax.dot_general(a, b, dims, preferred_element_type=F32)


def shape(dims, kind=BF16):
    return jax.ShapeDtypeStruct(dims, kind)


class Sizes:
    def __init__(self, n_dp, n_t, rows, d, cw, cfull):
        self.n_dp, self.n_t, self.rows, self.d = n_dp, n_t, rows, d
        self.X, self.H = n_dp // 2, n_t // 2
        self.G = WIN // rows
        self.NG = n_t // self.G
        self.cw, self.hw = cw, self.NG * cw
        self.cf = cfull // 2


class Place:
    def __init__(self, z):
        self.z = z
        dp, t = lax.axis_index("dp"), lax.axis_index("tensor")
        self.dp, self.t = dp, t
        self.x, self.c = dp // 2, dp % 2
        self.hi, self.lo = t // 2, t % 2
        self.g, self.r = t // z.G, t % z.G
        self.h2, self.hl = self.hi // 2, self.hi % 2

    def pair(self):
        return (self.dp, (self.h2 * 2 + 1 - self.hl) * 2 + self.lo)

    def h2dev(self, i):
        return (self.dp, (((self.h2 + i) % (self.z.H // 2)) * 2 + self.hl) * 2 + self.lo)

    def core(self):
        return (self.x * 2 + 1 - self.c, self.t)

    def y(self):
        return (self.dp, self.hi * 2 + 1 - self.lo)

    def xi(self, i):
        return (self.x + i) % self.z.X

    def xdev(self, i):
        return (self.xi(i) * 2 + self.c, self.t)

    def hii(self, i):
        return (self.hi + i) % self.z.H

    def hdev(self, i):
        return (self.dp, self.hii(i) * 2 + self.lo)

    def ri(self, i):
        return (self.r + i) % self.z.G

    def rdev(self, i):
        return (self.dp, self.g * self.z.G + self.ri(i))

    def gi(self, i):
        return (self.g + i) % self.z.NG

    def gdev(self, i):
        return (self.dp, self.gi(i) * self.z.G + self.r)


class Net:
    def __init__(self, send, recv, local=None):
        self.send, self.recv, self.local_sem = send, recv, local
        self.count, self.local_count = 0, 0
        self.all = []

    def remote(self, src, dst, device):
        k = self.count
        self.count += 1
        cp = pltpu.make_async_remote_copy(
            src_ref=src, dst_ref=dst, send_sem=self.send.at[k], recv_sem=self.recv.at[k],
            device_id=device, device_id_type=MESH,
        )
        self.all.append(cp)
        return cp

    def local(self, src, dst):
        k = self.local_count
        self.local_count += 1
        return pltpu.make_async_copy(src, dst, self.local_sem.at[k])

    def wait_sends(self):
        for cp in self.all:
            cp.wait_send()


def meet(devices):
    barrier = pltpu.get_barrier_semaphore()
    for device in devices:
        pl.semaphore_signal(barrier, inc=1, device_id=device, device_id_type=MESH)
    pl.semaphore_wait(barrier, len(devices))


def part(i, n):
    return pl.ds(pl.multiple_of(i * n, n), n)


def comm_call(body, z, name, cid, out_shape, in_specs, out_specs, scratch=(), n=64, vmem=None):
    return pl.pallas_call(
        functools.partial(body, z),
        out_shape=out_shape,
        in_specs=in_specs,
        out_specs=out_specs,
        scratch_shapes=[
            pltpu.SemaphoreType.DMA((n,)),
            pltpu.SemaphoreType.DMA((n,)),
            pltpu.SemaphoreType.DMA((64,)),
            *scratch,
        ],
        compiler_params=pltpu.CompilerParams(
            collective_id=cid, has_side_effects=True, vmem_limit_bytes=vmem
        ),
        name=name,
    )


def middle_kernel(
    z, own_h, tok_h, wo_h, wg_h, wu_h, wd_h, wg_o, wu_o, wd_o, seed_h, cot, gain, beta,
    out_part, out_pair, grad_mid, grad_mix, p_wo, p_gate, p_up, p_down, sums,
    send, recv, lsem,
    own, tok, wo, wg, wu, wd, seed, n2, middle, hidden, gg, gu, two, one, rc, ry, tot, out_f, rdx,
):
    p, net = Place(z), Net(send, recv, lsem)
    rows, d = z.rows, z.d
    cf, f_x = z.cf, []
    pairs = [(own_h, own), (wo_h, wo), (tok_h, tok)]
    for k in range(z.H):
        at = pl.ds(k * cf, cf)
        if k == 0:
            half = part(p.c, cf)
            pairs += [(wg_o.at[:, half], wg.at[:, at]), (wu_o.at[:, half], wu.at[:, at]),
                      (wd_o.at[half], wd.at[at])]
        elif k <= z.H // 2:
            pairs += [(wg_h.at[:, at], wg.at[:, at]), (wu_h.at[:, at], wu.at[:, at]),
                      (wd_h.at[at], wd.at[at])]
        else:
            up = part(p.x, d // z.X)
            down = pl.ds(pl.multiple_of(k * cf + p.x * (cf // z.X), 16), cf // z.X)
            some = [(wg_h.at[up, at], wg.at[up, at]), (wu_h.at[up, at], wu.at[up, at]),
                    (wd_h.at[down], wd.at[down])]
            pairs += some
            f_x += [net.remote(a, b, p.xdev(i)) for i in range(1, z.X) for a, b in some]
    for k, b in enumerate((p.hl * 2 + p.c, p.hl * 2 + 1 - p.c,
                           (1 - p.hl) * 2 + p.c, (1 - p.hl) * 2 + 1 - p.c)):
        at = part(b, rows)
        pairs.append((seed_h.at[at] if k else cot, seed.at[at]))
    loads = [net.local(a, b) for a, b in pairs]
    for cp in loads:
        cp.start()
    meet([p.pair(), p.core()] + [p.xdev(i) for i in range(1, z.X)])
    for cp in f_x:
        cp.start()
    chunk = 128
    blocks = [p.hl * 2 + p.c, p.hl * 2 + 1 - p.c,
              (1 - p.hl) * 2 + 1 - p.c, (1 - p.hl) * 2 + p.c]

    def block_rows(b):
        return pl.ds(pl.multiple_of(b * rows, rows), rows)

    for cp in loads[:3]:
        cp.wait()

    def norm(i, _):
        at = part(i, chunk)
        m = tok[at].astype(F32) + dot(own[at], wo[...])
        middle[at] = m
        scaled, _ = norm_stats(m)
        here = pl.ds(pl.multiple_of(blocks[0] * rows + i * chunk, chunk), chunk)
        n2[here] = (scaled * gain[...] + beta[...]).astype(BF16)
        return 0

    sub = rows // 2
    n_pair, n_core, n_hop = [], [], []
    for h in range(2):
        lax.fori_loop(h * (sub // chunk), (h + 1) * (sub // chunk), norm, 0)
        mine, far = [
            n2.at[pl.ds(pl.multiple_of(blocks[i] * rows + h * sub, sub), sub)] for i in (0, 3)
        ]
        n_pair.append(net.remote(mine, mine, p.pair()))
        n_core.append(net.remote(mine, mine, p.core()))
        n_hop.append(net.remote(far, far, p.core()))
        n_pair[h].start()
        n_core[h].start()
    for cp in loads[3:]:
        cp.wait()
    early, every = (z.H // 2 + 1) * cf, z.H * cf

    def sub_rows(b, i):
        return pl.ds(pl.multiple_of(b * rows + i * sub, sub), sub)

    def grads(b, low, high, first=0, last=2):
        cols = pl.ds(low, high - low)

        def body(i, _):
            at = sub_rows(b, i)
            a, e = n2[at], seed[at]
            gate, up = dot(a, wg[:, cols]), dot(a, wu[:, cols])
            sig = jax.nn.sigmoid(gate)
            silu = gate * sig
            hidden[at, cols] = (silu * up).astype(BF16)
            gh = dot(e, wd[cols], NT)
            gg[at, cols] = (gh * up * sig * (1.0 + gate * (1.0 - sig))).astype(BF16)
            gu[at, cols] = (gh * silu).astype(BF16)
            return 0

        lax.fori_loop(first, last, body, 0)

    def back_rows(b, i):
        at = sub_rows(b, i)
        two[at] = (dot(gg[at], wg[...], NT) + dot(gu[at], wu[...], NT)).astype(BF16)

    def out_rows(b, i):
        at = sub_rows(b, i)
        one[at] = dot(hidden[at], wd[...]).astype(BF16)

    def send_core(k, b, far):
        ref = (two, one)[k]
        cp = net.remote(ref.at[block_rows(b)], rc.at[k, far], p.core())
        cp.start()
        return cp

    grads(blocks[0], 0, early)
    for cp in n_core:
        cp.wait_recv()
    grads(blocks[1], 0, early)
    for cp in f_x:
        cp.wait_recv()
    for b in blocks[:2]:
        grads(b, early, every)
    to_pair = []
    for h in range(2):
        at = pl.ds(h * sub, sub)
        n_pair[h].wait_recv()
        n_hop[h].start()
        grads(blocks[3], 0, every, h, h + 1)
        n_hop[h].wait_recv()
        grads(blocks[2], 0, every, h, h + 1)
        back_rows(blocks[2], h)
        cp = net.remote(two.at[sub_rows(blocks[2], h)], rc.at[0, 1, at], p.core())
        cp.start()
        back_rows(blocks[3], h)
        cp.wait_recv()
        tot[0, at] = add_refs(two[sub_rows(blocks[3], h)], rc[0, 1, at]).astype(BF16)
        to_pair.append(net.remote(tot.at[0, at], ry.at[at], p.pair()))
        to_pair[h].start()

    def rows_of(f, b):
        def body(i, _):
            f(b, i)
            return 0

        lax.fori_loop(0, 2, body, 0)

    rows_of(back_rows, blocks[1])
    near = [send_core(0, blocks[1], 0)]
    rows_of(back_rows, blocks[0])
    rows_of(out_rows, blocks[2])
    away = send_core(1, blocks[2], 1)
    rows_of(out_rows, blocks[1])
    near.append(send_core(1, blocks[1], 0))
    rows_of(out_rows, blocks[3])
    rows_of(out_rows, blocks[0])
    away.wait_recv()
    tot[1] = add_refs(one[block_rows(blocks[3])], rc[1, 1]).astype(BF16)
    d_x, dx = [], cf // z.X
    stores = []
    for a, b, into, out in ((hidden, seed, wd, p_down), (n2, gg, wg, p_gate), (n2, gu, wu, p_up)):
        for i in range(into.shape[0] // 256):
            at = pl.ds(i * 256, 256)
            into[at] = dot(a[:, at], b[...], TN).astype(BF16)
        if into is wd:
            for i in range(1, z.X):
                for h in range(z.H):
                    far = pl.ds(pl.multiple_of(h * cf + p.xi(i) * dx, 16), dx)
                    d_x.append(net.remote(wd.at[far], rdx.at[i - 1, h], p.xdev(i)))
                    d_x[-1].start()
            continue
        stores.append(net.local(into, out))
        stores[-1].start()
    near[0].wait_recv()
    for cp in to_pair:
        cp.wait_recv()

    def back(i, carry):
        at = part(i, chunk)
        here = pl.ds(pl.multiple_of(blocks[0] * rows + i * chunk, chunk), chunk)
        scaled, inverse = norm_stats(middle[at])
        e = add_refs(two[here], rc[0, 0, at], ry[at])
        m = seed[here].astype(F32) + norm_backward(e, scaled, inverse, gain[...])
        out_f[at] = add_refs(middle[at], one[here], rc[1, 0, at])
        middle[at] = m
        tok[at] = m.astype(BF16)
        return (
            carry[0] + jnp.sum(e * scaled, axis=0, keepdims=True),
            carry[1] + jnp.sum(e, axis=0, keepdims=True),
        )

    near[1].wait_recv()
    zero = jnp.zeros((1, d), F32)
    a, b = lax.fori_loop(0, rows // chunk, back, (zero, zero))
    sums[0:1] = a
    sums[1:2] = b
    net.wait_sends()
    for i in range(d // 256):
        at = pl.ds(i * 256, 256)
        n2[at] = dot(own[:, at], tok[...], TN).astype(BF16)
    for h in range(z.H):
        mine = pl.ds(pl.multiple_of(h * cf + p.x * dx, 16), dx)
        for i in range(1, z.X):
            d_x[(i - 1) * z.H + h].wait_recv()
        wd[mine] = add_refs(wd[mine], *[rdx[i, h] for i in range(z.X - 1)]).astype(BF16)
        stores.append(net.local(wd.at[mine], p_down.at[h]))
        stores[-1].start()
    before = len(stores)
    stores.append(net.local(n2.at[pl.ds(0, d)], p_wo))
    stores.append(net.local(out_f, out_part))
    stores.append(net.local(tot.at[1], out_pair))
    stores.append(net.local(middle, grad_mid))
    for cp in stores[before:]:
        cp.start()
    mixed_at = pl.ds(0, rows)
    two[mixed_at] = dot(tok[...], wo[...], NT).astype(BF16)
    last = net.local(two.at[mixed_at], grad_mix)
    last.start()
    for cp in stores + [last]:
        cp.wait()


def add_refs(*values):
    total = values[0].astype(F32)
    for v in values[1:]:
        total = total + v.astype(F32)
    return total


def lane_of(rows):
    return lax.broadcasted_iota(jnp.int32, (rows, 128), 1)


def rope_tables():
    frequency = np.float32(10000.0) ** (-np.arange(HD // 2, dtype=np.float32) * 2.0 / HD)
    angles = np.arange(WIN, dtype=np.float32)[:, None] * frequency.astype(np.float32)[None, :]
    angles = np.concatenate([angles] * 4, axis=1)
    return np.cos(angles), np.sin(angles)


def turn(v, cosines, sines):
    swapped = jnp.where(
        lane_of(v.shape[0]) % HD < HD // 2, -pltpu.roll(v, 96, 1), pltpu.roll(v, 32, 1)
    )
    return v * cosines + swapped * sines


def spare_lanes(first, v, lane):
    high = v.astype(BF16)
    rest = v - high.astype(F32)
    middle = rest.astype(BF16)
    low = (rest - middle.astype(F32)).astype(BF16)
    s = lane % HD
    tail = jnp.where(s == 2, -middle.astype(F32), jnp.where(s == 3, -low.astype(F32), 0.0))
    return jnp.where(s == 0, first, jnp.where(s == 1, -high.astype(F32), tail))


def run_at(steps, i):
    for at, functions in sorted(steps.items()):

        @pl.when(i == at)
        def _(functions=functions):
            for f in functions:
                f()


def slot_order(p, z):
    half = z.G // 2
    rhi = p.r // 2
    order = [(rhi, p.lo), (rhi, 1 - p.lo)]
    for j in range(1, half):
        order += [((rhi + j) % half, p.lo), ((rhi + j) % half, 1 - p.lo)]
    return [a * 2 + b for a, b in order]


def front_kernel(
    z, tok, gain, beta, w_q, w_k, w_v, cos, sin, bias, wo, wg, wu, wd, cot,
    n1_o, w3_o, q_o, k_o, v_o, o_o, qa_o, own, wo_o, wgs, wus, wds, seed,
    send, recv, lsem, w3s, mixed, n1s, w3c, q, k, v, n1, o, qa, wos,
):
    p, net = Place(z), Net(send, recv, lsem)
    rq, qc = z.d // z.n_dp, z.d // z.n_dp
    rx, dx, cf = z.d // z.X, z.cf // z.X, z.cf
    half, wide = z.G // 2, z.cw % 128 == 0
    rhi = p.r // 2
    hr = z.rows // 2

    def slot_dev(a, b):
        return (p.dp, p.g * z.G + a * 2 + b)

    def slot_rows(a, b, top):
        return pl.ds(pl.multiple_of((a * 2 + b) * z.rows + top * hr, 16), hr)

    def norm(i, _):
        at = part(i, 128)
        scaled, _ = norm_stats(tok[at].astype(F32))
        n1[at] = (scaled * gain[...] + beta[...]).astype(BF16)
        return 0

    lax.fori_loop(0, z.rows // 128, norm, 0)
    near = [((rhi + j) % half) for j in range(1, half)]
    back = [((rhi + half - j) % half) for j in range(1, half)]
    meet(
        [slot_dev(rhi, 1 - p.lo)]
        + [slot_dev(a, 1 - p.lo) for a in near]
        + [p.hdev(i) for i in range(1, z.H)]
        + [p.xdev(i) for i in range(1, z.X)]
        + [p.core()]
    )
    quarter = part(p.dp, rq)
    w_out = [
        net.remote(ref.at[quarter], w3s.at[p.g, m, quarter], p.gdev(i))
        for i in range(1, z.NG) for m, ref in enumerate((w_q, w_k, w_v))
    ]
    y_out, a_out = [], []
    for top in (1, 0):
        y_out.append(
            net.remote(n1.at[pl.ds(top * hr, hr)], n1s.at[slot_rows(rhi, p.lo, top)],
                       slot_dev(rhi, 1 - p.lo))
        )
    for top in (0, 1):
        a_out.append(
            [
                net.remote(n1.at[pl.ds(top * hr, hr)], n1s.at[slot_rows(rhi, p.lo, top)],
                           slot_dev(a, p.lo))
                for a in near
            ]
        )
    def wo_rows(t):
        return part((t % z.G) * z.NG + t // z.G, z.cw)

    cols = part(p.dp, qc)
    own_o = wos.at[wo_rows(p.t), cols]
    o_out = [net.remote(wo.at[:, cols], own_o, p.hdev(i)) for i in range(1, z.H)]
    o_keep = net.local(wo.at[:, cols], own_o)
    o_hop = [net.remote(own_o, own_o, p.y())]
    for i in range(1, z.H):
        block = wos.at[wo_rows(((p.hi + z.H - i) % z.H) * 2 + p.lo), cols]
        o_hop.append(net.remote(block, block, p.y()))
    block = wos.at[:, cols]
    o_along = [net.remote(block, block, p.xdev(i)) for i in range(1, z.X)]
    o_across = []
    for x in range(z.X):
        block = wos.at[:, part(x * 2 + p.c, qc)]
        o_across.append(net.remote(block, block, p.core()))

    def pieces(h2, lo):
        k, x = lo * (z.H // 2) + h2, p.x
        return (
            wgs.at[part(x, rx), part(k, cf)],
            wus.at[part(x, rx), part(k, cf)],
            wds.at[pl.ds(pl.multiple_of(k * cf + x * dx, 16), dx)],
        )

    src = (
        wg.at[part(p.x, rx), part(p.c, cf)],
        wu.at[part(p.x, rx), part(p.c, cf)],
        wd.at[pl.ds(pl.multiple_of(p.c * cf + p.x * dx, 16), dx)],
    )
    h2n = z.H // 2

    def to(refs, into, device):
        return [net.remote(a, b, device) for a, b in zip(refs, into)]

    def all_x(refs):
        return [cp for m in range(1, z.X) for cp in to(refs, refs, p.xdev(m))]

    f_z = [to(src, pieces(h2n - i, 0), p.h2dev(i)) for i in range(1, h2n)]
    f_y = [to(src, pieces(0, 1), p.y())]
    f_y += [to(pieces(h2n - i, 0), pieces(h2n - i, 1), p.y()) for i in range(1, h2n)]
    f_x = [all_x(pieces(0, 1))]
    f_xz = [all_x(pieces(h2n - i, 0)) for i in range(1, h2n)]
    mine = seed.at[p.hl * 2 + p.c]
    other = seed.at[(1 - p.hl) * 2 + p.c]
    s_y, s_core = net.remote(cot, mine, p.pair()), net.remote(cot, mine, p.core())
    s_hop = net.remote(other, other, p.core())

    keep_w = [net.local(ref, w3s.at[p.g, m]) for m, ref in enumerate((w_q, w_k, w_v))]
    keep_n = net.local(n1, n1s.at[part(p.r, z.rows)])
    o_keep.start()
    for cp in w_out + o_out:
        cp.start()
    y_out[0].start()
    for cp in a_out[0]:
        cp.start()
    for cp in keep_w:
        cp.start()
    keep_n.start()
    y_out[1].start()
    for cp in a_out[1]:
        cp.start()
    for cp in w_out:
        cp.wait_recv()
    w_back = [(p.g + z.NG - i) % z.NG for i in range(1, z.NG)]
    along = []
    for g in w_back:
        block = w3s.at[g, :, quarter]
        along += [net.remote(block, block, p.xdev(i)) for i in range(1, z.X)]
    for cp in along:
        cp.start()
    o_keep.wait()
    o_hop[0].start()
    for i in range(1, z.H):
        o_out[i - 1].wait_recv()
        o_hop[i].start()
    for cp in along:
        cp.wait_recv()
    across = []
    for g in w_back:
        for x in range(z.X):
            block = w3s.at[g, :, part(x * 2 + p.c, rq)]
            across.append(net.remote(block, block, p.core()))
            across[-1].start()
    y_out[0].wait_recv()
    hop_a = []
    block = n1s.at[slot_rows(rhi, 1 - p.lo, 1)]
    hop_a = [net.remote(block, block, slot_dev(a, p.lo)) for a in near]
    for cp in hop_a:
        cp.start()
    hop_y = []
    for j, a in enumerate(back):
        a_out[0][j].wait_recv()
        block = n1s.at[slot_rows(a, p.lo, 0)]
        hop_y.append(net.remote(block, block, slot_dev(rhi, 1 - p.lo)))
        hop_y[-1].start()
    for cp in across:
        cp.wait_recv()
    for cp in o_hop:
        cp.wait_recv()
    for cp in o_along:
        cp.start()
    for cp in keep_w:
        cp.wait()
    keep_n.wait()
    for m in range(3):
        if wide:
            for g in range(z.NG):
                w3c[m, :, g * z.cw : (g + 1) * z.cw] = w3s[g, m]
        else:
            w3c[m] = add_refs(*[w3s[g, m] for g in range(z.NG)]).astype(BF16)

    def start(*copies):
        def f():
            for cp in copies:
                cp.start()
        return f

    def arrive(*copies):
        def f():
            for cp in copies:
                cp.wait_recv()
        return f

    width = q.shape[1]
    pairs, bq = width // 128, min(256, z.rows)
    per = z.rows // bq
    blocks = WIN // bq
    total = pairs * blocks
    steps = {}

    def at(i, *functions):
        steps.setdefault(min(i, total - 1), []).extend(functions)

    at(0, arrive(*o_along), start(*o_across))
    for m in range(3):
        at(3 + m, arrive(f_y[0][m]), start(*f_x[0][m::3]))
        for i in range(h2n - 1):
            at(7 + m, arrive(f_z[i][m]), start(f_y[i + 1][m], *f_xz[i][m::3]))
    at(0, start(s_core, s_y))
    at(total - 1, arrive(s_y), start(s_hop))

    order = slot_order(p, z)

    def project(r):
        rows = part(r, z.rows)
        a = n1s[rows]
        for m, ref in enumerate((q, k, v)):
            y = dot(a, w3c[m])
            for j in range(width // 128):
                t = y[:, j * 128 : j * 128 + 128]
                if m < 2:
                    t = turn(t, cos[rows], sin[rows])
                ref[rows, j * 128 : j * 128 + 128] = t.astype(BF16)

    project(order[0])
    y_out[1].wait_recv()
    for group in f_y[:1] + f_z:
        for cp in group:
            cp.start()
    project(order[1])
    for j in range(half - 1):
        a_out[1][j].wait_recv()
        hop_a[j].wait_recv()
        hop_y[j].wait_recv()
    for r in order[2:]:
        project(r)
    stores = [net.local(a, b) for a, b in (
        (n1s, n1_o), (w3c, w3_o), (q, q_o), (k, k_o), (v, v_o)
    )]
    for cp in stores:
        cp.start()
    wo_store = net.local(wos, wo_o)
    pair_stores = []
    for j in range(pairs):
        col, two = pl.ds(j * 128, 128), pl.ds(2 * j, 2)
        pair_stores += [net.local(o.at[:, col], o_o.at[:, col]),
                        net.local(qa.at[two], qa_o.at[two])]
        at((j + 1) * blocks - 1, start(*pair_stores[-2:]))
    at(total - 2, arrive(*o_across), wo_store.start)
    lane_k, lane_q = lane_of(WIN), lane_of(bq)

    m_out = {}
    for j in range(pairs):
        for i in range(1, z.G):
            col = pl.ds(pl.multiple_of(p.r * z.hw + j * 128, 128), 128)
            cp = net.remote(
                mixed.at[part(p.ri(i), z.rows), j * 128 : j * 128 + 128],
                own.at[:, col], p.rdev(i),
            )
            m_out[j, i] = cp
            at(j * blocks + i * per - 1, start(cp))

    def block(i, _):
        j, b = i // blocks, i % blocks
        row = ((p.r + 1 + b // per) % z.G) * z.rows + (b % per) * bq
        col, rows = part(j, 128), pl.ds(pl.multiple_of(row, bq), bq)
        k2, v2, kb, q2 = k[:, col], v[:, col], bias[...], q[rows, col]
        mixes = []
        for e in range(2):
            own_k = (lane_k < HD) if e == 0 else (lane_k >= HD)
            own_q = (lane_q < HD) if e == 0 else (lane_q >= HD)
            k_e = jnp.where(own_k, k2, kb)
            v_e = jnp.where(own_k, v2, jnp.ones_like(v2))
            q_e = jnp.where(own_q, q2, jnp.where(lane_q % HD == 0, 1.0, 0.0).astype(BF16))
            s = dot(q_e, k_e, NT)
            top = jnp.max(s, axis=1, keepdims=True)
            prob = jnp.exp2((s - top) * C2).astype(BF16)
            sums = dot(prob, v_e)
            mixes.append(sums / pltpu.roll(sums, HD, 1))
            norm = jnp.where(own_q, 0.0, top + jnp.log2(jnp.where(own_q, 1.0, sums)) * (1.0 / C2))
            full = jnp.where(own_q, q2.astype(F32), spare_lanes(1.0, norm, lane_q))
            qa[2 * j + e, rows] = full.astype(BF16)
        mix = jnp.where(lane_q < HD, mixes[0], mixes[1])
        o[rows, col] = mix
        mixed[rows, col] = mix.astype(BF16)
        run_at(steps, i)
        return 0

    lax.fori_loop(0, total, block, 0)
    m_keep = net.local(mixed.at[part(p.r, z.rows)], own.at[:, part(p.r, z.hw)])
    m_keep.start()
    for cp in list(m_out.values()) + [s_core]:
        cp.wait_recv()
    for group in f_x + f_xz + f_y[1:]:
        for cp in group:
            cp.wait_recv()
    s_hop.wait_recv()
    for cp in stores + pair_stores + [wo_store, m_keep]:
        cp.wait()
    net.wait_sends()


def back_kernel(
    z, gm, qa_h, q_h, k_h, v_h, o_h, w3_h, n1_h, dg, du, dd, do_w, out_pair, bias, cos, sin,
    got, out_got, og, ou, od, ow, oo,
    send, recv, lsem,
    qa, q, k, v, o, do, dq, dk, dv, do_e, dk_sum, dv_sum, w3, n1, part_one, p3,
    rgx, rux, sg, su, sd, rgy, ruy, rdy, rgz, ruz, rdz,
    oc, so, ox, oy, oz, wc, sw, wx, wgr, join_y, join_z,
):
    p, net = Place(z), Net(send, recv, lsem)
    d, rows = z.d, z.rows
    rq, rx, dx, cf, h2n = d // z.n_dp, d // z.X, z.cf // z.X, z.cf, z.H // 2
    width = q.shape[1]
    bq = min(512, rows)
    per, blocks, pairs = rows // bq, WIN // bq, width // 128
    total = pairs * blocks
    loads = [net.local(a, b) for a, b in (
        (qa_h, qa), (q_h, q), (k_h, k), (v_h, v), (o_h, o),
        (gm.at[:, part(p.r, z.hw)], do.at[part(p.r, rows)]),
    )]
    late = [net.local(a, b) for a, b in (
        (dd, sd), (dg.at[part(p.x, rx)], sg),
        *[(do_w.at[:, :, part(x * 2 + p.c, rq)], so.at[x]) for x in range(z.X)],
        (w3_h, w3), (n1_h, n1),
    )]
    for cp in loads + late:
        cp.start()
    meet(
        [p.rdev(i) for i in range(1, z.G)]
        + [p.hdev(i) for i in range(1, z.H)]
        + [p.xdev(i) for i in range(1, z.X)]
        + [p.core()]
    )

    def start(*copies):
        def f():
            for cp in copies:
                cp.start()
        return f

    def arrive(*copies):
        def f():
            for cp in copies:
                cp.wait_recv()
        return f

    steps = {}

    def at(i, *functions):
        steps.setdefault(min(i, total - 1), []).extend(functions)

    dest = do.at[part(p.r, rows)]
    a_out = [net.remote(gm.at[:, part(p.ri(i), z.hw)], dest, p.rdev(i)) for i in range(1, z.G)]
    for cp in a_out:
        cp.start()
    def spot(h2, lo):
        return ((lo + p.lo) % 2) * h2n + (h2 + h2n - p.h2) % h2n

    bufs = ((dd, None, sd, rdy, rdz, od), (dg, rgx, sg, rgy, rgz, og), (du, rux, su, ruy, ruz, ou))

    def piece(m, ref, s):
        return ref.at[s] if m == 0 else ref.at[:, part(s, cf)]

    fx = [[net.remote(bufs[m][0].at[part(p.xi(i), rx)], bufs[m][1].at[i - 1], p.xdev(i))
           for i in range(1, z.X) if m == 1] for m in range(2)]
    fy = [[net.remote(piece(m, bufs[m][2], spot(h2, 1 - p.lo)), bufs[m][3].at[h2], p.y())
           for h2 in range(h2n)] for m in range(2)]
    fz = [[net.remote(piece(m, bufs[m][2], spot((p.h2 + i) % h2n, p.lo)), bufs[m][4].at[i - 1],
                      p.h2dev(i)) for i in range(1, h2n)] for m in range(2)]
    up_y = [net.remote(du.at[:, part(spot(h2, 1 - p.lo), cf)], ruy.at[h2], p.y())
            for h2 in range(h2n)]
    up_own = [net.local(du.at[:, part(spot(h2, p.lo), cf)], su.at[h2]) for h2 in range(h2n)]
    up_x = [net.remote(su.at[:, part(p.xi(i), rx)], rux.at[i - 1], p.xdev(i))
            for i in range(1, z.X)]
    up_z = [net.remote(su.at[(p.h2 + i) % h2n, part(p.x, rx)], ruz.at[i - 1], p.h2dev(i))
            for i in range(1, h2n)]

    def up_y_in():
        for h2 in range(h2n):
            up_own[h2].wait()
            up_y[h2].wait_recv()
            su[h2] = add_refs(su[h2], ruy[h2]).astype(BF16)
        start(*up_x)()

    def up_x_in():
        arrive(*up_x)()
        for h2 in range(h2n):
            su[h2, part(p.x, rx)] = add_refs(
                su[h2, part(p.x, rx)], *[rux[i, h2] for i in range(z.X - 1)]
            ).astype(BF16)
        start(*up_z)()

    def up_z_in():
        arrive(*up_z)()
        ou[done_at[2]] = add_refs(
            su[p.h2, part(p.x, rx)], *[ruz[i] for i in range(h2n - 1)]
        ).astype(BF16)
        start(*fa[2])()
    done_at = [
        (pl.ds(pl.multiple_of(p.c * cf + p.x * dx, 16), dx),),
        (part(p.x, rx), part(p.c, cf)),
        (part(p.x, rx), part(p.c, cf)),
    ]
    fa, fc = [], []
    for m in range(3):
        block = bufs[m][5].at[done_at[m]]
        fa.append([net.remote(block, block, p.xdev(i)) for i in range(1, z.X)])
        block = od.at[part(p.c, cf)] if m == 0 else bufs[m][5].at[:, part(p.c, cf)]
        fc.append(net.remote(block, block, p.core()))

    def ffn_x(m):
        def f():
            arrive(*fx[m])()
            late[m].wait()
            got_x, own = bufs[m][1], bufs[m][2]
            for h in range(2 * h2n):
                c = pl.ds(h * cf, cf)
                own[:, c] = add_refs(
                    own[:, c], *[got_x[i, :, c] for i in range(z.X - 1)]
                ).astype(BF16)
            start(*fy[m])()
        return f

    def ffn_y(m):
        def f():
            arrive(*fy[m])()
            own, got_y = bufs[m][2], bufs[m][3]
            for h2 in range(h2n):
                if m == 0:
                    own[spot(h2, p.lo)] = add_refs(own[spot(h2, p.lo)], got_y[h2]).astype(BF16)
                else:
                    c = part(spot(h2, p.lo), cf)
                    own[:, c] = add_refs(own[:, c], got_y[h2]).astype(BF16)
            start(*fz[m])()
        return f

    def ffn_z(m):
        def f():
            arrive(*fz[m])()
            own, got_z, out = bufs[m][2], bufs[m][4], bufs[m][5]
            s = spot(p.h2, p.lo)
            mine = own[s] if m == 0 else own[:, part(s, cf)]
            out[done_at[m]] = add_refs(mine, *[got_z[i] for i in range(h2n - 1)]).astype(BF16)
            start(*fa[m])()
        return f

    def ffn_c(m):
        def f():
            arrive(*fa[m])()
            fc[m].start()
        return f

    half = z.G // 2
    c_out = [net.remote(do_w.at[:, :, part(p.xi(i) * 2 + 1 - p.c, rq)], oc.at[i], p.core())
             for i in range(z.X)]
    c_x = [net.remote(so.at[p.xi(i)], ox.at[i - 1], p.xdev(i)) for i in range(1, z.X)]
    c_y = [net.remote(so.at[p.x, i * 2 + 1 - p.lo], oy.at[i], p.y()) for i in range(half)]
    c_z = [net.remote(so.at[p.x, (p.hii(i) % half) * 2 + p.lo, part(p.hii(i) // half, z.cw)],
                      oz.at[i - 1], p.hdev(i)) for i in range(1, z.H)]
    cols = part(p.dp, rq)
    block = oo.at[:, cols]
    c_a = [net.remote(block, block, p.xdev(i)) for i in range(1, z.X)]
    c_c = []
    for x in range(z.X):
        block = oo.at[:, part(x * 2 + p.c, rq)]
        c_c.append(net.remote(block, block, p.core()))

    def wo_c():
        for cp in late[2 : 2 + z.X]:
            cp.wait()
        for i in list(range(1, z.X)) + [0]:
            c_out[i].wait_recv()
            for r in range(z.G):
                so[p.xi(i), r] = add_refs(so[p.xi(i), r], oc[i, r]).astype(BF16)
        start(*c_x)()

    def wo_x():
        arrive(*c_x)()
        for r in range(z.G):
            so[p.x, r] = add_refs(so[p.x, r], *[ox[i, r] for i in range(z.X - 1)]).astype(BF16)
        start(*c_y)()

    def wo_y():
        arrive(*c_y)()
        for i in range(half):
            r = i * 2 + p.lo
            so[p.x, r] = add_refs(so[p.x, r], oy[i]).astype(BF16)
        start(*c_z)()

    def wo_z():
        arrive(*c_z)()
        mine = so[p.x, (p.hi % half) * 2 + p.lo, part(p.hi // half, z.cw)]
        oo[:, cols] = add_refs(mine, *[oz[i] for i in range(z.H - 1)]).astype(BF16)
        start(*c_a)()

    def wo_a():
        arrive(*c_a)()
        start(*c_c)()

    o_send = net.remote(out_pair, out_got, p.pair())
    start(*fx[1], *c_out)()
    late[0].wait()
    start(*fy[0], *up_y, *up_own)()
    at(0, start(o_send))
    at(1, ffn_y(0))
    at(2, wo_c)
    at(3, ffn_x(1))
    at(4, ffn_z(0), up_y_in)
    at(5, ffn_y(1), wo_x)
    at(6, up_x_in, ffn_c(0))
    at(7, ffn_z(1))

    for cp in loads:
        cp.wait()
    lane_q, sub = lane_of(bq), 1024
    lane_k = lane_of(sub)
    s64 = lane_k % HD
    ones3 = jnp.where((s64 >= 1) & (s64 <= 3), 1.0, 0.0).astype(BF16)

    def block_step(i, _):
        j, b = i // blocks, i % blocks
        for n in range(1, z.G):

            @pl.when((j == 0) & (b == n * per))
            def _():
                a_out[z.G - 1 - n].wait_recv()

        row = ((p.r + b // per) % z.G) * rows + (b % per) * bq
        col, at_q = part(j, 128), pl.ds(pl.multiple_of(row, bq), bq)
        q2, do2 = q[at_q, col], do[at_q, col]
        prod = do2.astype(F32) * o[at_q, col]
        for e in range(2):
            own_q = (lane_q < HD) if e == 0 else (lane_q >= HD)
            delta = jnp.sum(jnp.where(own_q, prod, 0.0), axis=1, keepdims=True)
            spare = spare_lanes(0.0, jnp.broadcast_to(delta, prod.shape), lane_q)
            do_e[e] = jnp.where(own_q, do2.astype(F32), spare).astype(BF16)
        dqs = [jnp.zeros((bq, 128), F32)] * 2
        for s in range(WIN // sub):
            keys = pl.ds(s * sub, sub)
            k2, v2 = k[keys, col], v[keys, col]
            kb = bias[keys] + ones3
            dks, dvs = [], []
            for e in range(2):
                own_k = (lane_k < HD) if e == 0 else (lane_k >= HD)
                k_e = jnp.where(own_k, k2, kb)
                v_e = jnp.where(own_k, v2, ones3)
                prob = jnp.exp2(dot(k_e, qa[2 * j + e, at_q], NT) * C2)
                ds = (prob * dot(v_e, do_e[e], NT)).astype(BF16)
                dvs.append(dot(prob.astype(BF16), do2))
                dks.append(dot(ds, q2))
                dqs[e] = dqs[e] + dot(ds, k2, TN)
            dv_new = jnp.where(lane_k < HD, dvs[0], dvs[1])
            dk_new = jnp.where(lane_k < HD, dks[0], dks[1])

            @pl.when(b == 0)
            def _():
                dv_sum[keys] = dv_new
                dk_sum[keys] = dk_new

            @pl.when(b > 0)
            def _():
                dv_sum[keys] += dv_new
                dk_sum[keys] += dk_new

        dq_new = jnp.where(lane_q < HD, dqs[0], dqs[1]) * SCALE
        dq[at_q, col] = turn(dq_new, cos[at_q], -sin[at_q]).astype(BF16)

        @pl.when(b == blocks - 1)
        def _():
            dv[:, col] = dv_sum[...].astype(BF16)
            dk[:, col] = turn(dk_sum[...] * SCALE, cos[...], -sin[...]).astype(BF16)

        run_at(steps, i)
        return 0

    lax.fori_loop(0, total, block_step, 0)

    for cp in late[2 + z.X :]:
        cp.wait()
    half, hr, rhi = z.G // 2, rows // 2, p.r // 2
    near = [(rhi + j) % half for j in range(1, half)]

    def slot_dev(a, b):
        return (p.dp, p.g * z.G + a * 2 + b)

    def top(a, b, h):
        return pl.ds(pl.multiple_of((a * 2 + b) * rows + h * hr, 16), hr)

    def rows_one(a, b):
        here = part(a * 2 + b, rows)
        part_one[here] = (
            dot(dq[here], w3[0], NT) + dot(dk[here], w3[1], NT) + dot(dv[here], w3[2], NT)
        ).astype(BF16)

    y_dev = slot_dev(rhi, 1 - p.lo)
    r_y, r_z = [], []
    for j, a in enumerate(near):
        rows_one(a, 1 - p.lo)
        r_y.append(net.remote(part_one.at[top(a, 1 - p.lo, 0)], join_y.at[j], y_dev))
        r_z.append(net.remote(part_one.at[top(a, 1 - p.lo, 1)], join_z.at[j], slot_dev(a, p.lo)))
        start(r_y[j], r_z[j])()
    rows_one(rhi, 1 - p.lo)
    g_y = [net.remote(part_one.at[top(rhi, 1 - p.lo, h)], got.at[0, pl.ds(h * hr, hr)], y_dev)
           for h in range(2)]
    g_y[0].start()
    g_z = []
    for j, a in enumerate(near):
        rows_one(a, p.lo)
        g_z.append([net.remote(part_one.at[top(a, p.lo, h)], got.at[1 + j, pl.ds(h * hr, hr)],
                               slot_dev(a, p.lo)) for h in range(2)])
        g_z[j][1].start()
    rows_one(rhi, p.lo)
    r_keep = net.local(part_one.at[part(p.r, rows)], got.at[half])
    r_keep.start()

    def join():
        arrive(*r_z)()
        here = top(rhi, 1 - p.lo, 1)
        part_one[here] = add_refs(
            part_one[here], *[join_z[j] for j in range(half - 1)]
        ).astype(BF16)
        g_y[1].start()
        for j, a in enumerate(near):
            r_y[j].wait_recv()
            here = top(a, p.lo, 0)
            part_one[here] = add_refs(part_one[here], join_y[j]).astype(BF16)
            g_z[j][0].start()

    for m, t in enumerate((dq, dk, dv)):
        y = dot(n1[...], t[...], TN).astype(BF16)
        for g in range(z.NG):
            p3[g, m] = y[:, g * z.cw : (g + 1) * z.cw]
    w_c = [net.remote(p3.at[:, :, part(p.xi(i) * 2 + 1 - p.c, rq)], wc.at[i], p.core())
           for i in range(z.X)]
    start(*w_c)()
    wo_y()
    w_x = []
    for i in list(range(1, z.X)) + [0]:
        w_c[i].wait_recv()
        for g in range(z.NG):
            sw[i, g] = add_refs(p3[g, :, part(p.xi(i) * 2 + p.c, rq)], wc[i, g]).astype(BF16)
        if i:
            w_x.append(net.remote(sw.at[i], wx.at[i - 1], p.xdev(i)))
            w_x[-1].start()
    join()
    ffn_c(1)()
    wo_z()
    up_z_in()
    arrive(*w_x)()
    for g in range(z.NG):
        sw[0, g] = add_refs(sw[0, g], *[wx[i, g] for i in range(z.X - 1)]).astype(BF16)
    w_g = [net.remote(sw.at[0, p.gi(i)], wgr.at[i - 1], p.gdev(i)) for i in range(1, z.NG)]
    start(*w_g)()
    wo_a()
    ffn_c(2)()
    arrive(*w_g)()
    quarter = part(p.dp, rq)
    for m in range(3):
        ow[m, quarter] = add_refs(
            sw[0, p.g, m], *[wgr[i, m] for i in range(z.NG - 1)]
        ).astype(BF16)
    block = ow.at[:, quarter]
    w_a = [net.remote(block, block, p.xdev(i)) for i in range(1, z.X)]
    start(*w_a)()
    arrive(*w_a)()
    w_last = []
    for x in range(z.X):
        block = ow.at[:, part(x * 2 + p.c, rq)]
        w_last.append(net.remote(block, block, p.core()))
        w_last[-1].start()
    arrive(*c_c, *fc, *w_last, o_send, *g_y, *[cp for pair in g_z for cp in pair])()
    r_keep.wait()
    net.wait_sends()


def finish_kernel(
    z, got, tok, gain, sums_two, gm_h, part_h, far_h, grad_tok, output, norms,
    send, recv, lsem, gm, part_f, far_one, tok_out, out_low, t_sums, d_sums,
):
    p, net = Place(z), Net(send, recv, lsem)
    rows, d, chunk = z.rows, z.d, 128
    loads = [net.local(a, b) for a, b in ((gm_h, gm), (part_h, part_f), (far_h, far_one))]
    for cp in loads:
        cp.start()
    t_dev = [(p.dp, (p.t + i) % z.n_t) for i in range(1, z.n_t)]
    d_dev = [((p.dp + i) % z.n_dp, p.t) for i in range(1, z.n_dp)]
    meet(t_dev + d_dev)

    def rows_in(at):
        scaled, inverse = norm_stats(tok[at].astype(F32))
        return add_refs(*[got[i, at] for i in range(got.shape[0])]), scaled, inverse

    def sums(i, carry):
        e, scaled, _ = rows_in(part(i, chunk))
        return (
            carry[0] + jnp.sum(e * scaled, axis=0, keepdims=True),
            carry[1] + jnp.sum(e, axis=0, keepdims=True),
        )

    zero = jnp.zeros((1, d), F32)
    a, b = lax.fori_loop(0, rows // chunk, sums, (zero, zero))
    t_sums[p.t, 0:1] = a
    t_sums[p.t, 1:2] = b
    t_sums[p.t, 2:4] = sums_two[...]
    own = t_sums.at[p.t]
    first = [net.remote(own, own, dev) for dev in t_dev]
    for cp in first:
        cp.start()
    stores = []

    def store(src, dst):
        stores.append(net.local(src, dst))
        stores[-1].start()

    loads[0].wait()

    def back(i, _):
        at = part(i, chunk)
        e, scaled, inverse = rows_in(at)
        tok_out[at] = (gm[at] + norm_backward(e, scaled, inverse, gain[...])).astype(BF16)
        return 0

    lax.fori_loop(0, rows // chunk, back, 0)
    store(tok_out, grad_tok)
    for cp in first:
        cp.wait_recv()
    d_sums[p.dp] = add_refs(*[t_sums[i] for i in range(z.n_t)])
    own = d_sums.at[p.dp]
    second = [net.remote(own, own, dev) for dev in d_dev]
    for cp in second:
        cp.start()
    for cp in loads[1:]:
        cp.wait()
    out_low[...] = (part_f[...] + far_one[...].astype(F32)).astype(BF16)
    store(out_low, output)
    for cp in second:
        cp.wait_recv()
    norms[...] = add_refs(*[d_sums[i] for i in range(z.n_dp)])
    for cp in stores:
        cp.wait()
    net.wait_sends()


def widen_kernel(a, b, c, w, e, fa, fb, fc, fq, fk, fv, fe):
    for low, wide in ((a, fa), (b, fb), (c, fc), (e, fe)):
        wide[...] = low[...].astype(F32)
    for m, wide in enumerate((fq, fk, fv)):
        wide[...] = w[m].astype(F32)


def widen(g_gate, g_up, g_down, g_w3, g_wo):
    steps = 4
    d, wide = g_gate.shape
    cw = g_wo.shape[0]

    def rows(n, m):
        return pl.BlockSpec((n // steps, m), lambda i: (i, 0))

    flat = [rows(d, wide), rows(d, wide), rows(wide, d)]
    heads = pl.BlockSpec((3, d // steps, cw), lambda i: (0, i, 0))
    return pl.pallas_call(
        widen_kernel,
        grid=(steps,),
        out_shape=(
            shape((d, wide), F32), shape((d, wide), F32), shape((wide, d), F32),
            *[shape((d, cw), F32)] * 3, shape((cw, d), F32),
        ),
        in_specs=flat + [heads, rows(cw, d)],
        out_specs=flat + [rows(d, cw)] * 3 + [rows(cw, d)],
        compiler_params=pltpu.CompilerParams(vmem_limit_bytes=60 * MIB),
        name="widen",
    )(g_gate, g_up, g_down, g_w3, g_wo)


def norm_stats(v):
    centre = v - jnp.mean(v, axis=-1, keepdims=True)
    inverse = lax.rsqrt(jnp.mean(centre * centre, axis=-1, keepdims=True) + EPSILON)
    return centre * inverse, inverse


def norm_backward(grad_in, scaled, inverse, gain):
    weighted = grad_in * gain
    first_mean = jnp.mean(weighted, axis=-1, keepdims=True)
    second_mean = jnp.mean(weighted * scaled, axis=-1, keepdims=True)
    return inverse * (weighted - first_mean - scaled * second_mean)


def per_device(
    n_dp, n_t, tokens, lengths, ln1_gain, ln1_bias, w_query, w_key, w_value, w_out,
    ln2_gain, ln2_bias, w_gate, w_up, w_down, cotangent,
):
    rows, d = tokens.shape
    cw, cfull = w_query.shape[1], w_gate.shape[1]
    z = Sizes(n_dp, n_t, rows, d, cw, cfull)
    G, NG, H, X, hw, cf = z.G, z.NG, z.H, z.X, z.hw, z.cf
    rq, rx, dx = d // n_dp, d // X, cf // X
    slot = lax.axis_index("tensor") // G
    length = lengths[0]
    for i in range(1, NG):
        length = jnp.where(slot == i, lengths[i], length)
    lane = lax.broadcasted_iota(jnp.int32, (WIN, 128), 1) % HD
    place = lax.broadcasted_iota(jnp.int32, (WIN, 128), 0)
    bias = jnp.where((lane == 0) & (place >= length), -1e30, 0.0).astype(BF16)
    cos, sin = (jnp.asarray(t, F32) for t in rope_tables())

    w_three = [w_query, w_key, w_value]
    if cw % 128:
        wider = jnp.zeros((d, hw), BF16)
        w_three = [lax.dynamic_update_slice(wider, w, (0, slot * cw)) for w in w_three]
    n1, w3, q, k, v, o, qa, mixed_own, wo, wg, wu, wd, seed = comm_call(
        front_kernel, z, "front", 1,
        (
            shape((WIN, d)), shape((3, d, hw)), shape((WIN, hw)), shape((WIN, hw)),
            shape((WIN, hw)), shape((WIN, hw), F32), shape((hw // HD, WIN, 128)),
            shape((rows, d)), shape((d, d)), shape((d, H * cf)), shape((d, H * cf)),
            shape((H * cf, d)), shape((4, rows, d)),
        ),
        [VMEM] * 3 + [HBM] * 3 + [VMEM] * 3 + [HBM] * 5,
        [HBM] * 7 + [VMEM] + [HBM] * 5,
        [
            pltpu.VMEM((NG, 3) + w_three[0].shape, BF16), pltpu.VMEM((WIN, hw), BF16),
            pltpu.VMEM((WIN, d), BF16), pltpu.VMEM((3, d, hw), BF16),
            *[pltpu.VMEM((WIN, hw), BF16)] * 3, pltpu.VMEM((rows, d), BF16),
            pltpu.VMEM((WIN, hw), F32), pltpu.VMEM((hw // HD, WIN, 128), BF16),
            pltpu.VMEM((d, d), BF16),
        ],
        n=160, vmem=60 * MIB,
    )(
        tokens, ln1_gain.reshape(1, d), ln1_bias.reshape(1, d), *w_three, cos, sin, bias,
        w_out, w_gate, w_up, w_down, cotangent,
    )
    every = 4 * rows
    width = H * cf
    mid_out = (
        shape((rows, d), F32), shape((rows, d)), shape((rows, d), F32), shape((rows, d)),
        shape((d, d)), shape((d, width)), shape((d, width)), shape((H, dx, d)), shape((2, d), F32),
    )
    out_part, out_pair, grad_middle, grad_mixed, p_wo, p_gate, p_up, p_down, sums_two = comm_call(
        middle_kernel, z, "middle", 4, mid_out,
        [HBM] * 11 + [VMEM] * 2, [HBM] * 8 + [VMEM],
        [
            pltpu.VMEM((rows, d), BF16), pltpu.VMEM((rows, d), BF16), pltpu.VMEM((d, d), BF16),
            pltpu.VMEM((d, width), BF16), pltpu.VMEM((d, width), BF16),
            pltpu.VMEM((width, d), BF16), pltpu.VMEM((every, d), BF16),
            pltpu.VMEM((every, d), BF16), pltpu.VMEM((rows, d), F32),
            pltpu.VMEM((every, width), BF16), pltpu.VMEM((every, width), BF16),
            pltpu.VMEM((every, width), BF16), pltpu.VMEM((every, d), BF16),
            pltpu.VMEM((every, d), BF16), pltpu.VMEM((2, 2, rows, d), BF16),
            pltpu.VMEM((rows, d), BF16), pltpu.VMEM((2, rows, d), BF16),
            pltpu.VMEM((rows, d), F32), pltpu.VMEM((X - 1, H, dx, d), BF16),
        ],
        vmem=62 * MIB,
    )(
        mixed_own, tokens, wo, wg, wu, wd, w_gate, w_up, w_down, seed.reshape(every, d), cotangent,
        ln2_gain.reshape(1, d), ln2_bias.reshape(1, d),
    )
    p_wo = p_wo.reshape(G, hw, d)
    V = pltpu.VMEM
    pieces = ((rx, cf), (rx, cf), (dx, d))
    got, out_got, g_gate, g_up, g_down, g_w3, g_wo = comm_call(
        back_kernel, z, "back", 8,
        (
            shape((G // 2 + 1, rows, d)), shape((rows, d)), shape((d, 2 * cf)), shape((d, 2 * cf)),
            shape((2 * cf, d)), shape((3, d, cw)), shape((cw, d)),
        ),
        [HBM] * 13 + [VMEM] * 3, [HBM] * 2 + [VMEM] * 5,
        [
            V((hw // HD, WIN, 128), BF16), V((WIN, hw), BF16), V((WIN, hw), BF16),
            V((WIN, hw), BF16), V((WIN, hw), F32), V((WIN, hw), BF16), V((WIN, hw), BF16),
            V((WIN, hw), BF16), V((WIN, hw), BF16), V((2, min(512, rows), 128), BF16),
            V((WIN, 128), F32), V((WIN, 128), F32), V((3, d, hw), BF16), V((WIN, d), BF16),
            V((WIN, d), BF16), V((NG, 3, d, cw), BF16),
            V((X - 1, rx, width), BF16), V((X - 1, H // 2, rx, cf), BF16),
            V((rx, width), BF16), V((H // 2, d, cf), BF16), V((H, dx, d), BF16),
            *[V((H // 2,) + dims, BF16) for dims in ((rx, cf), (d, cf), (dx, d))],
            *[V((H // 2 - 1,) + dims, BF16) for dims in pieces],
            V((X, G, hw, rq), BF16), V((X, G, hw, rq), BF16), V((X - 1, G, hw, rq), BF16),
            V((G // 2, hw, rq), BF16), V((H - 1, cw, rq), BF16),
            V((X, NG, 3, rq, cw), BF16), V((X, NG, 3, rq, cw), BF16),
            V((X - 1, NG, 3, rq, cw), BF16), V((NG - 1, 3, rq, cw), BF16),
            *[V((G // 2 - 1, rows // 2, d), BF16)] * 2,
        ],
        n=160, vmem=62 * MIB,
    )(
        grad_mixed, qa, q, k, v, o, w3, n1, p_gate, p_up, p_down, p_wo, out_pair, bias, cos, sin,
    )
    grad_tokens, output, norms = comm_call(
        finish_kernel, z, "finish", 9,
        (shape((rows, d)), shape((rows, d)), shape((4, d), F32)),
        [VMEM] * 4 + [HBM] * 3, [HBM] * 2 + [VMEM],
        [
            V((rows, d), F32), V((rows, d), F32), V((rows, d), BF16), V((rows, d), BF16),
            V((rows, d), BF16), V((n_t, 4, d), F32), V((n_dp, 4, d), F32),
        ],
        vmem=62 * MIB,
    )(got, tokens, ln1_gain.reshape(1, d), sums_two, grad_middle, out_part, out_got)
    f_gate, f_up, f_down, f_q, f_k, f_v, f_wo = widen(g_gate, g_up, g_down, g_w3, g_wo)
    return (
        output, grad_tokens, norms[0], norms[1], f_q, f_k, f_v, f_wo,
        norms[2], norms[3], f_gate, f_up, f_down,
    )


def solution(mesh):
    rows, cols, each = P(("dp", "tensor"), None), P(None, "tensor"), P("tensor", None)
    return jax.shard_map(
        functools.partial(per_device, mesh.shape["dp"], mesh.shape["tensor"]),
        mesh=mesh,
        in_specs=(
            rows, P("dp"), P(), P(), cols, cols, cols, each, P(), P(), cols, cols, each, rows,
        ),
        out_specs=(
            rows, rows, P(), P(), cols, cols, cols, each, P(), P(), cols, cols, each,
        ),
        check_vma=False,
    )
```
